128 devices in a mesh: seq: 4 (over x_hi, core), fsdp: 32 (over z, x_lo, y).
Axes of the slice: x: 4 (x_hi: 2, x_lo: 2; x = x_hi * 2 + x_lo), y: 4, z: 4, core: 2. Of those that a mesh axis runs over, the one named last changes fastest.
Arguments:
- tokens: bfloat16 [32, 1024, 768], P('fsdp', 'seq'), may hold values from -6 to 6
- image_ids: int32 [32, 1024], P('fsdp'), may hold values from 0 to 1, as said below
- cotangent: bfloat16 [32, 1024, 768], P('fsdp', 'seq'), may hold values from -6 to 6
- attn_norm_gain: bfloat16 [2, 768], P(None, 'fsdp'), may hold values from 0.25 to 1.75
- attn_norm_bias: bfloat16 [2, 768], P(None, 'fsdp'), may hold values from -1 to 1
- qkv_weight: bfloat16 [2, 768, 2304], P(None, 'fsdp'), may hold values from -0.21875 to 0.21875
- query_bias: bfloat16 [2, 768], P(None, 'fsdp'), may hold values from -1.5 to 1.5
- value_bias: bfloat16 [2, 768], P(None, 'fsdp'), may hold values from -0.25 to 0.25
- proj_weight: bfloat16 [2, 768, 768], P(None, 'fsdp'), may hold values from -1.75 to 1.75
- proj_bias: bfloat16 [2, 768], P(None, 'fsdp'), may hold values from -1 to 1
- mlp_norm_gain: bfloat16 [2, 768], P(None, 'fsdp'), may hold values from 0.25 to 1.75
- mlp_norm_bias: bfloat16 [2, 768], P(None, 'fsdp'), may hold values from -1 to 1
- fc_in_weight: bfloat16 [2, 768, 3072], P(None, 'fsdp'), may hold values from -0.21875 to 0.21875
- fc_in_bias: bfloat16 [2, 3072], P(None, 'fsdp'), may hold values from -2.5 to 2.5
- fc_out_weight: bfloat16 [2, 3072, 768], P(None, 'fsdp'), may hold values from -0.109375 to 0.109375
- fc_out_bias: bfloat16 [2, 768], P(None, 'fsdp'), may hold values from -1 to 1
Outputs:
- block_output: bfloat16 [32, 1024, 768], P('fsdp', 'seq')
- tokens_grad: float32 [32, 1024, 768], P('fsdp', 'seq')
- attn_norm_gain_grad: float32 [2, 768], P(None, 'fsdp')
- attn_norm_bias_grad: float32 [2, 768], P(None, 'fsdp')
- qkv_weight_grad: float32 [2, 768, 2304], P(None, 'fsdp')
- query_bias_grad: float32 [2, 768], P(None, 'fsdp')
- value_bias_grad: float32 [2, 768], P(None, 'fsdp')
- proj_weight_grad: float32 [2, 768, 768], P(None, 'fsdp')
- proj_bias_grad: float32 [2, 768], P(None, 'fsdp')
- mlp_norm_gain_grad: float32 [2, 768], P(None, 'fsdp')
- mlp_norm_bias_grad: float32 [2, 768], P(None, 'fsdp')
- fc_in_weight_grad: float32 [2, 768, 3072], P(None, 'fsdp')
- fc_in_bias_grad: float32 [2, 3072], P(None, 'fsdp')
- fc_out_weight_grad: float32 [2, 3072, 768], P(None, 'fsdp')
- fc_out_bias_grad: float32 [2, 768], P(None, 'fsdp')
The draws below stay inside these ranges and needn't reach their ends.
Inputs may be any that keep to these rules, and one draw needn't show every extreme that they name: `image_ids`: each sequence holds one image: a run of 785 tokens with id 0 that starts at one of its first 240 positions; every other token of the sequence is padding with id 1. A token attends to the tokens of its own sequence that carry its id.
All inputs are finite; a program needn't handle non-finite values.
Results may differ from the reference program's by a relative error of at most 0.023.
Values may be sent and summed in bfloat16 or wider, within the bound.
No kernel may reach another device: no remote copies, remote signals or barrier semaphores. Data moves between devices by JAX's collectives and lax.ppermute only.
A program may use at most 256 MiB of HBM per device.

```python
import jax
import jax.numpy as jnp
from jax import lax

D = 768
HEADS = 12
HD = 64
FF = 3072
LAYERS = 2
L = 1024
IMG_TOK = 785
SEQS = 32


def draw_image_ids(key, part):
    key = jax.random.fold_in(key, 11)
    offsets = jax.random.randint(key, (SEQS, 1), 0, L - IMG_TOK + 1)
    positions = jnp.arange(L, dtype=jnp.int32)[None, :]
    inside = (positions >= offsets) & (positions < offsets + IMG_TOK)
    return jnp.where(inside, 0, 1).astype(jnp.int32)


def spiked(array, stream_key, source, target, blocks, factor):
    def block_of(position):
        return (jnp.arange(array.shape[position]) // (array.shape[position] // blocks)).reshape((-1,) + (1,) * (array.ndim - 1 - position))

    one_side = jax.random.permutation(stream_key, blocks)[block_of(target)]
    far = (block_of(target) + blocks // 2) % blocks
    return jnp.where((block_of(source) == one_side) | (block_of(source) == far), factor * array, array)


def block_scale(rng, extent, split, least, top_value):
    def one(position, parts):
        heights = jax.random.uniform(jax.random.fold_in(jax.random.fold_in(rng, 6), position), (parts,), jnp.float32, least / len(split), top_value / len(split))
        return jnp.repeat(jnp.exp(heights), extent[position] // parts).reshape((-1,) + (1,) * (len(extent) - position - 1))

    loudness = one(*split[0])
    for cut in split[1:]:
        loudness = loudness * one(*cut)
    return loudness


def scatter_about(key, extent, scale, limit, pieces=(), kind=jnp.bfloat16):
    entries = jax.random.normal(key, extent, jnp.float32) * scale
    if len(pieces) > 0:
        entries = block_scale(key, extent, pieces, -0.22, 0.18) * entries
    return jnp.clip(entries, min=-limit, max=limit).astype(kind)


def bell_draw_with(stream_key, extent, width, reach, pieces, heavy, held_as=jnp.bfloat16):
    values = width * jax.random.normal(stream_key, extent, jnp.float32)
    if pieces:
        values = values * block_scale(stream_key, extent, pieces, -0.22, 0.18)
    return jnp.clip(spiked(values, jax.random.fold_in(stream_key, 3), *heavy), -reach, reach).astype(held_as)


def setup_inputs(seed: int = 0) -> dict:
    seeds = jax.random.split(jax.random.key(seed), 17)
    return {
        "tokens": bell_draw_with(seeds[0], (SEQS, L, D), 1.0, 6.0, ((0, 32), (1, 4)), (0, 2, 32, 2.75)),
        "image_ids": draw_image_ids(jax.random.fold_in(seeds[16], 71), 0),
        "cotangent": scatter_about(seeds[2], (SEQS, L, D), 1.0, 6.0, ((0, 32), (1, 4))),
        "attn_norm_gain": jnp.clip(1.0 + 0.15 * jax.random.normal(seeds[3], (LAYERS, D), jnp.float32), 0.25, 1.75).astype(jnp.bfloat16),
        "attn_norm_bias": scatter_about(seeds[4], (LAYERS, D), 0.2, 1.0, ((1, 32),)),
        "qkv_weight": scatter_about(seeds[5], (LAYERS, D, 3 * D), D ** -0.5, 0.21875, ((1, 32),)),
        "query_bias": scatter_about(seeds[6], (LAYERS, D), 0.3, 1.5, ((1, 32),)),
        "value_bias": scatter_about(seeds[7], (LAYERS, D), 0.05, 0.25, ((1, 32),)),
        "proj_weight": scatter_about(seeds[8], (LAYERS, D, D), (max(D // 64, 1)) ** -0.5, 1.75, ((1, 32),)),
        "proj_bias": scatter_about(seeds[9], (LAYERS, D), 0.2, 1.0, ((1, 32),)),
        "mlp_norm_gain": jnp.clip(1.0 + 0.15 * jax.random.normal(seeds[10], (LAYERS, D), jnp.float32), 0.25, 1.75).astype(jnp.bfloat16),
        "mlp_norm_bias": scatter_about(seeds[11], (LAYERS, D), 0.2, 1.0, ((1, 32),)),
        "fc_in_weight": scatter_about(seeds[12], (LAYERS, D, FF), D ** -0.5, 0.21875, ((1, 32),)),
        "fc_in_bias": scatter_about(seeds[13], (LAYERS, FF), 0.5, 2.5, ((1, 32),)),
        "fc_out_weight": scatter_about(seeds[14], (LAYERS, FF, D), FF ** -0.5, 0.109375, ((1, 32),)),
        "fc_out_bias": scatter_about(seeds[15], (LAYERS, D), 0.2, 1.0, ((1, 32),)),
    }


@jax.custom_vjp
def low(v):
    return lax.optimization_barrier(v.astype(jnp.bfloat16)).astype(jnp.float32)

@jax.custom_vjp
def low_back(v):
    return v

def low_keep(v):
    return (low(v), None)

def low_pass(kept, grad):
    return (grad,)

def back_keep(v):
    return (v, None)

def back_low(kept, grad):
    return (low(grad),)
low.defvjp(low_keep, low_pass)
low_back.defvjp(back_keep, back_low)

def layer_norm(values, gain_row, bias_row):
    centre = lax.optimization_barrier(jnp.mean(values, -1, keepdims=True))
    centred = values - centre
    spread = lax.optimization_barrier(jnp.mean(centred * centred, -1, keepdims=True))
    return centred * lax.rsqrt(spread + 1e-06) * gain_row + bias_row

def matmul(left, right):
    return jnp.dot(left, right, precision=lax.Precision.HIGHEST, preferred_element_type=jnp.float32)

def attend_one(packed):
    queries, key_rows, value_rows, labels = packed
    q_heads = queries.reshape(L, HEADS, HD)
    k_heads = key_rows.reshape(L, HEADS, HD)
    v_heads = value_rows.reshape(L, HEADS, HD)
    scores = jnp.einsum('qhe,khe->hqk', q_heads, k_heads, precision=lax.Precision.HIGHEST) * HD ** (-0.5)
    scores = low_back(scores)
    allowed = labels[:, None] == labels[None, :]
    scores = jnp.where(allowed[None], scores, -1e+30)
    row_peak = lax.optimization_barrier(jnp.max(scores, -1, keepdims=True))
    expons = jnp.exp(scores - row_peak)
    probabilities = low(expons / lax.optimization_barrier(jnp.sum(expons, -1, keepdims=True)))
    attended = jnp.einsum('hqk,khe->qhe', probabilities, v_heads, precision=lax.Precision.HIGHEST)
    return attended.reshape(L, D)

def encoder_block(rows, labels, layer_set):
    norm_gain, norm_bias, qkv_full, q_bias, v_bias, proj_full, proj_shift, mlp_gain, mlp_bias, in_full, in_shift, out_full, out_shift = layer_set
    attn_in = low(layer_norm(rows, norm_gain, norm_bias))
    projected = matmul(attn_in, qkv_full)
    queries = low(low_back(projected[:, :D] + q_bias))
    key_rows = low(low_back(projected[:, D:2 * D]))
    value_rows = low(low_back(projected[:, 2 * D:] + v_bias))
    attended = lax.map(jax.checkpoint(attend_one), (queries.reshape(SEQS, L, D), key_rows.reshape(SEQS, L, D), value_rows.reshape(SEQS, L, D), labels))
    tok_out = low(low_back(attended.reshape(-1, D)))
    middle = rows + low_back(matmul(tok_out, proj_full) + proj_shift)
    mlp_in = low(layer_norm(middle, mlp_gain, mlp_bias))
    hidden_pre = low_back(matmul(mlp_in, in_full) + in_shift)
    hidden = low(jax.nn.gelu(hidden_pre, approximate=False))
    return middle + low_back(matmul(hidden, out_full) + out_shift)

def reference(tokens, image_ids, cotangent, attn_norm_gain, attn_norm_bias, qkv_weight, query_bias, value_bias, proj_weight, proj_bias, mlp_norm_gain, mlp_norm_bias, fc_in_weight, fc_in_bias, fc_out_weight, fc_out_bias):
    weight_list = tuple((member.astype(jnp.float32) for member in (attn_norm_gain, attn_norm_bias, qkv_weight, query_bias, value_bias, proj_weight, proj_bias, mlp_norm_gain, mlp_norm_bias, fc_in_weight, fc_in_bias, fc_out_weight, fc_out_bias)))

    def forward(start_rows, *members):
        rows = start_rows
        for layer_index in range(LAYERS):
            rows = encoder_block(rows, image_ids, tuple((member[layer_index] for member in members)))
        return rows
    final_rows, pull_back = jax.vjp(forward, tokens.astype(jnp.float32).reshape(-1, D), *weight_list)
    grads = pull_back(cotangent.astype(jnp.float32).reshape(-1, D))
    return (final_rows.astype(jnp.bfloat16).reshape(SEQS, L, D), grads[0].reshape(SEQS, L, D), grads[1], grads[2], grads[3], grads[4], grads[5], grads[6], grads[7], grads[8], grads[9], grads[10], grads[11], grads[12], grads[13])
```

```python
import functools

import jax
import jax.numpy as jnp
from jax import lax
from jax.experimental import pallas as pl
from jax.experimental.pallas import tpu as pltpu
from jax.sharding import Mesh
from jax.sharding import PartitionSpec as P

HD = 64
AXES = ("xh", "core", "z", "xl", "y")
SIZES = (2, 2, 4, 2, 4)
FSDP = ("z", "xl", "y")
SEQ = ("xh", "core")
UNIT = 384
ROWS = 24
BF = jnp.bfloat16
F32 = jnp.float32
ANY = pl.BlockSpec(memory_space=pl.ANY)
SMEM = pl.BlockSpec(memory_space=pltpu.SMEM)
VMEM = pl.BlockSpec(memory_space=pltpu.VMEM)
ROOMY = pltpu.CompilerParams(vmem_limit_bytes=48 * 2**20)


def ravel(coords):
    index = 0
    for size, coord in zip(SIZES, coords):
        index = index * size + coord % size
    return index


def all_coords():
    xh_n, core_n, z_n, xl_n, y_n = SIZES
    return [
        (xh, core, z, xl, y)
        for xh in range(xh_n)
        for core in range(core_n)
        for z in range(z_n)
        for xl in range(xl_n)
        for y in range(y_n)
    ]


def shift(array, move):
    pairs = [(ravel(c), ravel(move(*c))) for c in all_coords()]
    return lax.ppermute(array, AXES, pairs)


def to_core(array):
    return shift(array, lambda xh, core, z, xl, y: (xh, core + 1, z, xl, y))


def to_xh(array):
    return shift(array, lambda xh, core, z, xl, y: (xh + 1, core, z, xl, y))


def to_xl(array):
    return shift(array, lambda xh, core, z, xl, y: (xh, core, z, xl + 1, y))


def to_inner(array, d):
    return shift(
        array,
        lambda xh, core, z, xl, y: (xh, core, z, xl, y + d) if core == 0 else (xh, core, z + d, xl, y),
    )


def to_outer(array, d):
    return shift(
        array,
        lambda xh, core, z, xl, y: (xh, core, z + d, xl, y) if core == 0 else (xh, core, z, xl, y + d),
    )


def slot_table(sign):
    core, z, xl, y = (lax.axis_index(n) for n in ("core", "z", "xl", "y"))
    inner = jnp.where(core == 0, y, z)
    outer = jnp.where(core == 0, z, y)
    dq = jnp.arange(4, dtype=jnp.int32)[:, None, None]
    dp = jnp.arange(4, dtype=jnp.int32)[None, :, None]
    dx = jnp.arange(2, dtype=jnp.int32)[None, None, :]
    q = (outer + sign * dq + 4) % 4
    if sign < 0:
        p = (inner - dp + 4) % 4
        x = (xl + dx) % 2
    else:
        p = dp
        x = dx
    owner = jnp.where(core == 0, q * 8 + x * 4 + p, p * 8 + x * 4 + q)
    return owner.astype(jnp.int32).reshape(32)


def assemble_kernel(wide, table, s0, s1, s2, s3, *rest):
    outs, sem = rest[:-1], rest[-1]
    copies = []
    for dq, src in enumerate((s0, s1, s2, s3)):
        for dp in range(4):
            for dx in range(2):
                n = dq * 8 + dp * 2 + dx
                f = table[n]
                copies.append(
                    pltpu.make_async_copy(
                        src.at[dp, dx, pl.ds(0, wide)], outs[0].at[:, f], sem.at[n, 0]
                    )
                )
                if len(outs) > 1:
                    copies.append(
                        pltpu.make_async_copy(
                            src.at[dp, dx, pl.ds(wide, 4)], outs[1].at[f], sem.at[n, 1]
                        )
                    )
    for copy in copies:
        copy.start()
    for copy in copies:
        copy.wait()


def gather_units(units, wide, table):
    count = units.shape[0]
    pair = jnp.stack([units, to_xl(units)])
    inner = jnp.stack([pair] + [to_inner(pair, d) for d in (1, 2, 3)])
    outer = [inner] + [to_outer(inner, d) for d in (1, 2, 3)]
    shapes = [jax.ShapeDtypeStruct((wide, 32, ROWS, UNIT), BF)]
    if count > wide:
        shapes.append(jax.ShapeDtypeStruct((32, 4, ROWS, UNIT), BF))
    return pl.pallas_call(
        functools.partial(assemble_kernel, wide),
        out_shape=shapes,
        in_specs=[SMEM] + [ANY] * 4,
        out_specs=[VMEM] * len(shapes),
        scratch_shapes=[pltpu.SemaphoreType.DMA((32, 2))],
        compiler_params=ROOMY,
    )(table, *outer)


def split_kernel(table, *rest):
    sem = rest[-1]
    outs = rest[-5:-1]
    srcs = rest[:-5]
    copies = []
    for dq, dst in enumerate(outs):
        for p in range(4):
            for x in range(2):
                n = dq * 8 + p * 2 + x
                f = table[n]
                wide = srcs[0].shape[0]
                copies.append(
                    pltpu.make_async_copy(
                        srcs[0].at[:, f], dst.at[p, x, pl.ds(0, wide)], sem.at[n, 0]
                    )
                )
                if len(srcs) > 1:
                    copies.append(
                        pltpu.make_async_copy(
                            srcs[1].at[f], dst.at[p, x, pl.ds(wide, 4)], sem.at[n, 1]
                        )
                    )
    for copy in copies:
        copy.start()
    for copy in copies:
        copy.wait()


def add_all(*parts):
    total = parts[0].astype(F32)
    for part in parts[1:]:
        total = total + part.astype(F32)
    return total.astype(BF)


def scatter_units(grads, table):
    count = grads[0].shape[0] + (4 if len(grads) > 1 else 0)
    blocks = pl.pallas_call(
        split_kernel,
        out_shape=[jax.ShapeDtypeStruct((4, 2, count, ROWS, UNIT), BF)] * 4,
        in_specs=[SMEM] + [ANY] * len(grads),
        out_specs=[VMEM] * 4,
        scratch_shapes=[pltpu.SemaphoreType.DMA((32, 2))],
        compiler_params=ROOMY,
    )(table, *grads)
    total = add_all(blocks[0], *[to_outer(blocks[d], d) for d in (1, 2, 3)])
    core, z, xl, y = (lax.axis_index(n) for n in ("core", "z", "xl", "y"))
    inner = jnp.where(core == 0, y, z)
    parts = [lax.dynamic_index_in_dim(total, (inner + d) % 4, 0, keepdims=False) for d in range(4)]
    total = add_all(parts[0], *[to_inner(parts[d], d) for d in (1, 2, 3)])
    mine = lax.dynamic_index_in_dim(total, xl, 0, keepdims=False)
    other = lax.dynamic_index_in_dim(total, 1 - xl, 0, keepdims=False)
    total = add_all(mine, to_xl(other))
    return add_all(total, to_xh(total))


def norm_parts(values):
    centred = values - jnp.mean(values, -1, keepdims=True)
    scale = lax.rsqrt(jnp.mean(centred * centred, -1, keepdims=True) + 1e-06)
    return centred * scale, scale


def layer_norm(values, gain, bias):
    return norm_parts(values)[0] * gain + bias


def norm_back(values, gain, grad):
    n, scale = norm_parts(values)
    dg = grad * gain
    out = scale * (
        dg - jnp.mean(dg, -1, keepdims=True) - n * jnp.mean(dg * n, -1, keepdims=True)
    )
    return out, jnp.sum(grad * n, 0), jnp.sum(grad, 0)


def dot(a, b):
    return jnp.dot(a, b, preferred_element_type=F32)


def dot_nt(a, b):
    return lax.dot_general(a, b, (((1,), (1,)), ((), ())), preferred_element_type=F32)


def dot_tn(a, b):
    return lax.dot_general(a, b, (((0,), (0,)), ((), ())), preferred_element_type=F32)


def pick(flag, first, second, axis):
    return jnp.concatenate(
        [jnp.where(flag, first, second), jnp.where(flag, second, first)], axis
    )


def heads_of(rows):
    return rows.reshape(rows.shape[0], -1, HD)


def attend(q, k, v, ids_q, ids_k):
    s = jnp.einsum("qhe,khe->hqk", heads_of(q), heads_of(k), preferred_element_type=F32)
    s = jnp.where((ids_q[:, None] == ids_k[None, :])[None], s * HD**-0.5, -1e30)
    peak = jnp.max(s, -1, keepdims=True)
    e = jnp.exp(s - peak)
    total = jnp.sum(e, -1, keepdims=True)
    prob = (e / total).astype(BF)
    o = jnp.einsum("hqk,khe->qhe", prob, heads_of(v), preferred_element_type=F32)
    return o.astype(BF).reshape(q.shape), (peak + jnp.log(total))[..., 0]


def attend_back(q, k, v, ids_q, ids_k, lse, go):
    qh, kh, vh, gh = heads_of(q), heads_of(k), heads_of(v), heads_of(go)
    s = jnp.einsum("qhe,khe->hqk", qh, kh, preferred_element_type=F32)
    s = jnp.where((ids_q[:, None] == ids_k[None, :])[None], s * HD**-0.5, -1e30)
    prob = jnp.exp(s - lse[..., None])
    gv = jnp.einsum("hqk,qhe->khe", prob.astype(BF), gh, preferred_element_type=F32)
    dp = jnp.einsum("qhe,khe->hqk", gh, vh, preferred_element_type=F32)
    gs = (prob * (dp - jnp.sum(dp * prob, -1, keepdims=True))).astype(BF)
    gq = jnp.einsum("hqk,khe->qhe", gs, kh, preferred_element_type=F32) * HD**-0.5
    gk = jnp.einsum("hqk,qhe->khe", gs, qh, preferred_element_type=F32) * HD**-0.5
    return (
        gq.astype(BF).reshape(q.shape),
        gk.astype(BF).reshape(k.shape),
        gv.astype(BF).reshape(v.shape),
    )


def gelu(u):
    return jax.nn.gelu(u, approximate=False)


def body(
    tokens,
    image_ids,
    cotangent,
    attn_norm_gain,
    attn_norm_bias,
    qkv_weight,
    query_bias,
    value_bias,
    proj_weight,
    proj_bias,
    mlp_norm_gain,
    mlp_norm_bias,
    fc_in_weight,
    fc_in_bias,
    fc_out_weight,
    fc_out_bias,
):
    core, xh, xl = (lax.axis_index(n) for n in ("core", "xh", "xl"))
    first = core == 0
    width = tokens.shape[2]
    half = width // 2
    tok = tokens.shape[1]

    def column(vec):
        return vec[:, None]

    vec_list = []
    for l in range(2):
        for vec in (
            attn_norm_gain,
            attn_norm_bias,
            query_bias,
            value_bias,
            proj_bias,
            mlp_norm_gain,
            mlp_norm_bias,
            fc_out_bias,
        ):
            vec_list.append(column(vec[l]))
        vec_list.append(fc_in_bias[l].reshape(4, ROWS).T)
    vec_unit = jnp.concatenate(vec_list, 1)
    vec_unit = jnp.pad(vec_unit, ((0, 0), (0, UNIT - vec_unit.shape[1])))

    def mine(part, start):
        return lax.dynamic_slice_in_dim(part, start + core * UNIT, UNIT, 1)

    def attn_units(l):
        return [mine(qkv_weight[l], j * width) for j in range(3)] + [mine(proj_weight[l], 0)]

    def mlp_units(l):
        inner = lax.dynamic_slice_in_dim(fc_in_weight[l], core * 4 * UNIT, 4 * UNIT, 1)
        outs = mine(fc_out_weight[l], 0).reshape(4, ROWS, UNIT)
        return [inner[:, j * UNIT : (j + 1) * UNIT] for j in range(4)] + [outs[j] for j in range(4)]

    table_in = slot_table(-1)
    table_out = slot_table(1)

    g1 = gather_units(jnp.stack(attn_units(0) + [vec_unit]), 5, table_in)[0]
    g2 = gather_units(jnp.stack(mlp_units(0)), 4, table_in)
    g3 = gather_units(jnp.stack(attn_units(1)), 4, table_in)[0]
    g4 = gather_units(jnp.stack(mlp_units(1)), 4, table_in)

    vec_rows = g1[4].reshape(width, UNIT)[:, :32].T.astype(F32)

    def weights(attn, mlp, l):
        wq, wk, wv, proj_h = (attn[j].reshape(width, UNIT) for j in range(4))
        proj = pick(first, proj_h, to_core(proj_h), 1)
        inner = mlp[0].reshape(4, width, UNIT)
        other = to_core(inner)
        inner = pick(first, inner, other, 0)
        fc_in = jnp.concatenate([inner[j] for j in range(8)], 1)
        out_h = mlp[1].reshape(4 * width, UNIT)
        fc_out = pick(first, out_h, to_core(out_h), 1)
        vec = vec_rows[l * 12 : l * 12 + 8]
        fin = vec_rows[l * 12 + 8 : l * 12 + 12].reshape(4, 32, ROWS).transpose(1, 0, 2).reshape(-1)
        return dict(wq=wq, wk=wk, wv=wv, proj=proj, fc_in=fc_in, fc_out=fc_out, vec=vec, fin=fin)

    sets = [weights(g1, g2, 0), weights(g3, g4, 1)]

    def segment(dx, dc):
        return lax.dynamic_slice_in_dim(
            image_ids[0], (((xh + dx) % 2) * 2 + (core + dc) % 2) * tok, tok, 0
        )

    ids = jnp.concatenate([segment(0, 0), segment(0, 1), segment(1, 0), segment(1, 1)])
    ids_q = ids[: 2 * tok]

    def half_vec(vec):
        return lax.dynamic_slice_in_dim(vec, core * half, half, 0)

    def forward(x, w):
        vec = w["vec"]
        a = layer_norm(x, vec[0], vec[1]).astype(BF)
        far = to_xh(a)
        a_all = jnp.concatenate([a, to_core(a), far, to_core(far)], 0)
        q = (dot(a_all[: 2 * tok], w["wq"]) + half_vec(vec[2])).astype(BF)
        k = dot(a_all, w["wk"]).astype(BF)
        v = (dot(a_all, w["wv"]) + half_vec(vec[3])).astype(BF)
        o, lse = attend(q, k, v, ids_q, ids)
        o_full = pick(first, o[:tok], to_core(o[tok:]), 1)
        m = x + (dot(o_full, w["proj"]) + vec[4])
        c = layer_norm(m, vec[5], vec[6]).astype(BF)
        u = dot(c, w["fc_in"]) + w["fin"]
        z = gelu(u).astype(BF)
        out = m + (dot(z, w["fc_out"]) + vec[7])
        return out, (x, a_all, q, k, v, lse, o_full, m, c, u, z)

    def backward(gx, w, saved):
        x, a_all, q, k, v, lse, o_full, m, c, u, z = saved
        vec = w["vec"]
        gm = gx.astype(BF)
        dz = dot_nt(gm, w["fc_out"])
        gu = jax.vjp(gelu, u)[1](dz)[0].astype(BF)
        dc = dot_nt(gu, w["fc_in"])
        dm, mlp_gain_g, mlp_bias_g = norm_back(m, vec[5], dc)
        gmid = gx + dm
        ga = gmid.astype(BF)
        go = dot_nt(ga, w["proj"]).astype(BF)
        go_mine = lax.dynamic_slice_in_dim(go, core * half, half, 1)
        go_other = lax.dynamic_slice_in_dim(go, (1 - core) * half, half, 1)
        go_heads = jnp.concatenate([go_mine, to_core(go_other)], 0)
        d_out = dot_tn(z, gm).astype(BF)
        d_in = dot_tn(c, gu).astype(BF)
        d_proj = dot_tn(o_full, ga).astype(BF)
        gq, gk, gv = attend_back(q, k, v, ids_q, ids, lse, go_heads)
        da = dot_nt(gk, w["wk"]) + dot_nt(gv, w["wv"])
        da_near = da[: 2 * tok] + dot_nt(gq, w["wq"])
        da_far = da[2 * tok :]
        recv = to_core(da_far[tok:].astype(BF))
        far = to_xh((da_far[:tok] + recv.astype(F32)).astype(BF))
        near = to_core(da_near[tok:].astype(BF))
        da_own = da_near[:tok] + near.astype(F32) + far.astype(F32)
        dx, gain_g, bias_g = norm_back(x, vec[0], da_own)
        d_q = dot_tn(a_all[: 2 * tok], gq).astype(BF)
        d_k = dot_tn(a_all, gk).astype(BF)
        d_v = dot_tn(a_all, gv).astype(BF)

        def spread(vec_half):
            zero = jnp.zeros((half,), F32)
            return pick(first, vec_half, zero, 0)

        def total(g):
            return jnp.sum(g.astype(F32), 0)

        rows = [
            gain_g,
            bias_g,
            spread(total(gq)),
            spread(total(gv)),
            total(ga),
            mlp_gain_g,
            mlp_bias_g,
            total(gm),
        ]
        fin = total(gu).reshape(32, 4, ROWS).transpose(1, 0, 2).reshape(4, width)
        table = jnp.concatenate([jnp.stack(rows), fin], 0).astype(BF)
        table = jnp.pad(table, ((0, UNIT - 12), (0, 0)))
        table = table.T
        table = add_all(table, to_core(table))

        def halves(grad):
            keep = lax.dynamic_slice_in_dim(grad, core * (grad.shape[1] // 2), grad.shape[1] // 2, 1)
            send = lax.dynamic_slice_in_dim(
                grad, (1 - core) * (grad.shape[1] // 2), grad.shape[1] // 2, 1
            )
            return add_all(keep, to_core(send))

        d_in = halves(d_in)
        wide = [d_in[:, j * UNIT : (j + 1) * UNIT] for j in range(4)] + [halves(d_proj)]
        part1 = scatter_units(
            [
                jnp.stack(wide).reshape(5, 32, ROWS, UNIT),
                halves(d_out).reshape(32, 4, ROWS, UNIT),
            ],
            table_out,
        )
        part2 = scatter_units(
            [jnp.stack([d_q, d_k, d_v, table]).reshape(4, 32, ROWS, UNIT)], table_out
        )
        return gmid + dx, (part1, part2)

    x = tokens[0].astype(F32)
    saved = []
    for l in range(2):
        x, keep = forward(x, sets[l])
        saved.append(keep)
    gx = cotangent[0].astype(F32)
    parts = [None, None]
    for l in (1, 0):
        gx, parts[l] = backward(gx, sets[l], saved[l])

    def finish(l):
        part1, part2 = parts[l]
        own = jnp.concatenate([part1, part2], 0)
        other = to_core(own)
        lo = jnp.where(first, own, other).astype(F32)
        hi = jnp.where(first, other, own).astype(F32)
        fc_in = jnp.concatenate([lo[j] for j in range(4)] + [hi[j] for j in range(4)], 1)
        proj = jnp.concatenate([lo[4], hi[4]], 1)
        fc_out = jnp.concatenate(
            [lo[5:9].reshape(4 * ROWS, UNIT), hi[5:9].reshape(4 * ROWS, UNIT)], 1
        )
        qkv = jnp.concatenate([lo[9], hi[9], lo[10], hi[10], lo[11], hi[11]], 1)
        vecs = lo[12]
        cols = [vecs[:, j] for j in range(8)]
        fin = vecs[:, 8:12].T.reshape(-1)
        return (
            cols[0],
            cols[1],
            qkv,
            cols[2],
            cols[3],
            proj,
            cols[4],
            cols[5],
            cols[6],
            fc_in,
            fin,
            fc_out,
            cols[7],
        )

    done = [finish(0), finish(1)]
    stacked = tuple(jnp.stack([done[0][j], done[1][j]]) for j in range(13))
    return (x.astype(BF)[None], gx[None]) + stacked


def solution(mesh):
    fine = Mesh(mesh.devices.reshape(SIZES), AXES)
    row = P(None, FSDP)
    mat = P(None, FSDP, None)
    tok = P(FSDP, SEQ, None)
    return jax.shard_map(
        body,
        mesh=fine,
        in_specs=(
            tok,
            P(FSDP, None),
            tok,
            row,
            row,
            mat,
            row,
            row,
            mat,
            row,
            row,
            row,
            mat,
            row,
            mat,
            row,
        ),
        out_specs=(tok, tok, row, row, mat, row, row, mat, row, row, row, mat, row, mat, row),
        check_vma=False,
    )
```

```python
import functools

import jax
import jax.numpy as jnp
from jax import lax
from jax.experimental import pallas as pl
from jax.experimental.pallas import tpu as pltpu
from jax.sharding import Mesh
from jax.sharding import PartitionSpec as P

HD = 64
AXES = ("xh", "core", "z", "xl", "y")
SIZES = (2, 2, 4, 2, 4)
FSDP = ("z", "xl", "y")
SEQ = ("xh", "core")
UNIT = 384
ROWS = 24
BF = jnp.bfloat16
F32 = jnp.float32
ANY = pl.BlockSpec(memory_space=pl.ANY)
SMEM = pl.BlockSpec(memory_space=pltpu.SMEM)
VMEM = pl.BlockSpec(memory_space=pltpu.VMEM)
LIGHT = pl.CostEstimate(flops=10**6, bytes_accessed=10**5, transcendentals=0)
ROOMY = pltpu.CompilerParams(vmem_limit_bytes=48 * 2**20)


def ravel(coords):
    index = 0
    for size, coord in zip(SIZES, coords):
        index = index * size + coord % size
    return index


def all_coords():
    xh_n, core_n, z_n, xl_n, y_n = SIZES
    return [
        (xh, core, z, xl, y)
        for xh in range(xh_n)
        for core in range(core_n)
        for z in range(z_n)
        for xl in range(xl_n)
        for y in range(y_n)
    ]


def shift(array, move):
    pairs = [(ravel(c), ravel(move(*c))) for c in all_coords()]
    return lax.ppermute(array, AXES, pairs)


def to_core(array):
    return shift(array, lambda xh, core, z, xl, y: (xh, core + 1, z, xl, y))


def to_xh(array):
    return shift(array, lambda xh, core, z, xl, y: (xh + 1, core, z, xl, y))


def to_xl(array):
    return shift(array, lambda xh, core, z, xl, y: (xh, core, z, xl + 1, y))


def to_next_x(array, d):
    def move(xh, core, z, xl, y):
        x = (2 * xh + xl + d) % 4
        return (x // 2, core, z, x % 2, y)

    return shift(array, move)


def to_inner(array, d):
    return shift(
        array,
        lambda xh, core, z, xl, y: (xh, core, z, xl, y + d) if core == 0 else (xh, core, z + d, xl, y),
    )


def to_outer(array, d):
    return shift(
        array,
        lambda xh, core, z, xl, y: (xh, core, z + d, xl, y) if core == 0 else (xh, core, z, xl, y + d),
    )


def nothing(*refs):
    del refs


def after(array, *deps):
    return pl.pallas_call(
        nothing,
        out_shape=jax.ShapeDtypeStruct(array.shape, array.dtype),
        in_specs=[ANY] * (1 + len(deps)),
        out_specs=ANY,
        input_output_aliases={0: 0},
    )(array, *deps)


def groups(outer):
    sets = []
    for xh in range(2):
        for core in range(2):
            for xl in range(2):
                for other in range(4):
                    along_z = (core == 0) == outer
                    sets.append(
                        [
                            ravel((xh, core, i, xl, other) if along_z else (xh, core, other, xl, i))
                            for i in range(4)
                        ]
                    )
    return sets


OUTER = groups(True)
INNER = groups(False)
PLANE = [
    [ravel((xh, core, z, xl, y)) for z in range(4) for y in range(4)]
    for xh in range(2)
    for core in range(2)
    for xl in range(2)
]


def pin(*arrays):
    return [pltpu.with_memory_space_constraint(array, pltpu.HBM) for array in arrays]


def slot_table(sign, core, absolute=False):
    z, xl, y = (lax.axis_index(n) for n in ("z", "xl", "y"))
    inner = jnp.where(core == 0, y, z)
    outer = jnp.where(core == 0, z, y)
    dq = jnp.arange(4, dtype=jnp.int32)[:, None, None]
    dp = jnp.arange(4, dtype=jnp.int32)[None, :, None]
    dx = jnp.arange(2, dtype=jnp.int32)[None, None, :]
    q = dq + 0 * outer if absolute and sign > 0 else (outer + sign * dq + 4) % 4
    if sign < 0:
        p = dp + 0 * inner if absolute else (inner - dp + 4) % 4
        x = (xl + dx) % 2
    else:
        p = dp
        x = dx
    owner = jnp.where(core == 0, q * 8 + x * 4 + p, p * 8 + x * 4 + q)
    return owner.astype(jnp.int32).reshape(32)


SLOTS = [(dq, dp, dx) for dq in range(4) for dp in range(4) for dx in range(2)]


def run_all(copies):
    for copy in copies:
        copy.start()
    for copy in copies:
        copy.wait()


def pieces_of(srcs):
    if len(srcs) == 1:
        return [srcs[0].at[dq] for dq in range(4)]
    return srcs


def assemble_kernel(n_dep, table, *refs):
    srcs, (out, sem) = refs[:4], refs[4 + n_dep :]
    copies = []
    for n, (dq, dp, dx) in enumerate(SLOTS):
        src = srcs[dq].at[dp, dx, pl.ds(0, 3)]
        copies.append(pltpu.make_async_copy(src, out.at[:, table[n]], sem.at[n]))
    run_all(copies)


def assemble(table, pieces, deps):
    return pl.pallas_call(
        functools.partial(assemble_kernel, len(deps)),
        out_shape=pltpu.HBM((3, 32, ROWS, UNIT), BF),
        in_specs=[SMEM] + [ANY] * (4 + len(deps)),
        out_specs=VMEM,
        scratch_shapes=[pltpu.SemaphoreType.DMA((32,))],
        compiler_params=ROOMY,
        cost_estimate=LIGHT,
    )(table, *pieces, *deps)


def window(f):
    return (f * 96 // 128) * 128, f * 96 % 128


def assemble_first_kernel(n_dep, table, *refs):
    srcs, (out, rows_ref, fins_ref, vun, fbuf, sem) = refs[:4], refs[4 + n_dep :]
    copies = []
    for n, (dq, dp, dx) in enumerate(SLOTS):
        src = srcs[dq].at[dp, dx]
        f = table[n]
        copies.append(pltpu.make_async_copy(src.at[3], vun.at[f], sem.at[n, 0]))
        copies.append(pltpu.make_async_copy(src.at[pl.ds(0, 3)], out.at[:, f], sem.at[n, 1]))
    run_all(copies)
    vectors = vun[...].astype(F32)
    rows_ref[...] = vectors[:, :, :128].reshape(32 * ROWS, 128).T[:32]
    fbuf[...] = jnp.zeros(fbuf.shape, F32)
    for f in range(32):
        base, off = window(f)
        piece = jnp.concatenate([vectors[f, :8, 128:256], jnp.zeros((8, 128), F32)], 1)
        if off:
            piece = pltpu.roll(piece, off, 1)
        fbuf[:, base : base + 256] += piece
    fins_ref[...] = fbuf[:, : fins_ref.shape[1]]


def assemble_first(table, pieces, deps):
    return pl.pallas_call(
        functools.partial(assemble_first_kernel, len(deps)),
        out_shape=[
            pltpu.HBM((3, 32, ROWS, UNIT), BF),
            pltpu.HBM((32, 32 * ROWS), F32),
            pltpu.HBM((8, 128 * ROWS), F32),
        ],
        in_specs=[SMEM] + [ANY] * (4 + len(deps)),
        out_specs=[VMEM] * 3,
        scratch_shapes=[
            pltpu.VMEM((32, ROWS, UNIT), BF),
            pltpu.VMEM((8, 128 * ROWS + 128), F32),
            pltpu.SemaphoreType.DMA((32, 2)),
        ],
        compiler_params=ROOMY,
        cost_estimate=LIGHT,
    )(table, *pieces, *deps)


def assemble_both_kernel(begin, core, table, table_o, *refs):
    srcs, (wide, outs, sem) = refs[:8], refs[-3:]
    copies = []
    for side, at, tab in ((0, core[0], table), (1, 1 - core[0], table_o)):
        for n, (dq, dp, dx) in enumerate(SLOTS):
            src = srcs[4 * side + dq].at[dp, dx]
            f = tab[n]
            copies.append(
                pltpu.make_async_copy(src.at[pl.ds(begin, 5)], wide.at[at, :, f], sem.at[n, side, 0])
            )
            copies.append(
                pltpu.make_async_copy(
                    src.at[pl.ds(begin + 5, 4)], outs.at[at, f], sem.at[n, side, 1]
                )
            )
    run_all(copies)


def assemble_both(begin, core, tables, pieces, others, deps):
    wide, outs = pl.pallas_call(
        functools.partial(assemble_both_kernel, begin),
        out_shape=[
            pltpu.HBM((2, 5, 32, ROWS, UNIT), BF),
            pltpu.HBM((2, 32, 4, ROWS, UNIT), BF),
        ],
        in_specs=[SMEM] * (1 + len(tables)) + [ANY] * (2 * len(pieces) + len(deps)),
        out_specs=[VMEM] * 2,
        scratch_shapes=[pltpu.SemaphoreType.DMA((32, 2, 5))],
        compiler_params=ROOMY,
        cost_estimate=LIGHT,
    )(core, *tables, *pieces, *others, *deps)
    return wide.reshape(2, 5, 32 * ROWS, UNIT), outs.reshape(2, 128 * ROWS, UNIT)


def prep_kernel(core, *refs):
    vecs, (fin, qkv, proj, fc_in, fc_out, u12, u3, vbuf, ubuf) = refs[:8], refs[8:]
    at = pl.multiple_of(core[0] * UNIT, 128)
    wide = pl.multiple_of(core[0] * 4 * UNIT, 128)
    for l in range(2):
        units = [qkv[l, :, pl.ds(at + 2 * j * UNIT, UNIT)] for j in range(3)]
        units.append(proj[l, :, pl.ds(at, UNIT)])
        units += [fc_in[l, :, pl.ds(wide + j * UNIT, UNIT)] for j in range(4)]
        rows = fc_out[l, :, pl.ds(at, UNIT)].astype(F32)
        units += [rows[j * ROWS : (j + 1) * ROWS].astype(BF) for j in range(4)]
        for j, unit in enumerate(units):
            if l == 0:
                u12[j if j < 3 else j + 1] = unit
            else:
                u3[j] = unit
    vbuf[...] = jnp.zeros(vbuf.shape, F32)
    for j, vec in enumerate(vecs):
        value = vec[...].astype(F32)
        for l in range(2):
            vbuf[l * 12 + j : l * 12 + j + 1, :ROWS] = value[l : l + 1]
    ubuf[...] = jnp.zeros(ubuf.shape, F32)
    ubuf[:, :128] = vbuf[...].T[:ROWS]
    ubuf[0:2, 128:224] = fin[...].astype(F32)
    u12[3] = ubuf[...].astype(BF)


def prep(core, arrays):
    return pl.pallas_call(
        prep_kernel,
        out_shape=[pltpu.HBM((count, ROWS, UNIT), BF) for count in (13, 12)],
        in_specs=[SMEM] + [VMEM] * 13,
        out_specs=[VMEM] * 2,
        scratch_shapes=[pltpu.VMEM((128, 128), F32), pltpu.VMEM((ROWS, UNIT), F32)],
        compiler_params=ROOMY,
        cost_estimate=LIGHT,
    )(core, *arrays)


def inner_of(pair, got, units=slice(None)):
    return jnp.stack([part[:, units] for part in [pair] + got])


def three_inner(pair):
    return [to_inner(pair, d) for d in (1, 2, 3)]


def three_outer(block):
    return [to_outer(block, d) for d in (1, 2, 3)]


def send_outer(blocks):
    return [blocks[0]] + [to_outer(blocks[d], d) for d in (1, 2, 3)]


def take_sets(sizes, refs):
    sets = []
    for size in sizes:
        sets.append(refs[:size])
        refs = refs[size:]
    return sets


def sum_outer_kernel(n_set, n_dep, place_at, *refs):
    sets, outs = take_sets(n_set, refs), refs[sum(n_set) + n_dep :]
    for d, out in enumerate(outs):
        at = lax.rem(place_at[0] + d, 4)
        begin = 0
        for parts in sets:
            count = parts[0].shape[2]
            for x in range(2):
                total = parts[0][at, x].astype(F32)
                for part in parts[1:]:
                    total = total + part[at, x].astype(F32)
                out[x, begin : begin + count] = total.astype(BF)
            begin += count


def sum_outer(place_at, sets, deps=()):
    flat = [part for parts in sets for part in parts]
    count = sum(parts[0].shape[2] for parts in sets)
    return pl.pallas_call(
        functools.partial(sum_outer_kernel, [len(s) for s in sets], len(deps)),
        out_shape=[pltpu.HBM((2, count, ROWS, UNIT), BF)] * 4,
        in_specs=[SMEM] + [VMEM] * len(flat) + [ANY] * len(deps),
        out_specs=[VMEM] * 4,
        compiler_params=ROOMY,
        cost_estimate=LIGHT,
    )(place_at, *flat, *deps)


def sum_inner_kernel(n_set, n_dep, xl, *refs):
    sets, outs = take_sets(n_set, refs), refs[sum(n_set) + n_dep :]
    for j, out in enumerate(outs):
        at = xl[0] if j == 0 else 1 - xl[0]
        begin = 0
        for parts in sets:
            count = parts[0].shape[1]
            total = parts[0][at].astype(F32)
            for part in parts[1:]:
                total = total + part[at].astype(F32)
            out[begin : begin + count] = total.astype(BF)
            begin += count


def sum_inner(xl, sets, deps=()):
    flat = [part for parts in sets for part in parts]
    count = sum(parts[0].shape[1] for parts in sets)
    return pl.pallas_call(
        functools.partial(sum_inner_kernel, [len(s) for s in sets], len(deps)),
        out_shape=[pltpu.HBM((count, ROWS, UNIT), BF)] * 2,
        in_specs=[SMEM] + [VMEM] * len(flat) + [ANY] * len(deps),
        out_specs=[VMEM] * 2,
        compiler_params=ROOMY,
        cost_estimate=LIGHT,
    )(xl, *flat, *deps)


def add_all(*parts):
    total = parts[0].astype(F32)
    for part in parts[1:]:
        total = total + part.astype(F32)
    return total.astype(BF)


def norm_parts(values):
    centred = values - jnp.mean(values, -1, keepdims=True)
    scale = lax.rsqrt(jnp.mean(centred * centred, -1, keepdims=True) + 1e-06)
    return centred * scale, scale


def layer_norm(values, gain, bias):
    return norm_parts(values)[0] * gain + bias


def norm_back(values, gain, grad):
    n, scale = norm_parts(values)
    dg = grad * gain
    out = scale * (
        dg - jnp.mean(dg, -1, keepdims=True) - n * jnp.mean(dg * n, -1, keepdims=True)
    )
    return out, jnp.sum(grad * n, 0, keepdims=True), jnp.sum(grad, 0, keepdims=True)


def fdot(a, b, ca=1, cb=0):
    return lax.dot_general(a, b, (((ca,), (cb,)), ((), ())), preferred_element_type=F32)


def lanes(rows):
    return lax.broadcasted_iota(jnp.int32, (rows, 128), 1)


def place(lane, base, columns):
    out = jnp.zeros(lane.shape, F32)
    for j, column in enumerate(columns):
        out = jnp.where(lane == base + j, column, out)
    return out


def load_qkv(units, wbuf, sem):
    return [
        pltpu.make_async_copy(units.at[j], wbuf.at[:, pl.ds(j * UNIT, UNIT)], sem.at[j])
        for j in range(3)
    ]


def three(column):
    hi = column.astype(BF).astype(F32)
    mid = (column - hi).astype(BF).astype(F32)
    return [hi, mid, column - hi - mid]


def attn_fwd_kernel(raw, row, n_dep, core, x0, x1, x2, x3, units, vec, idc, *rest):
    rest = rest[n_dep:]
    a_ref, q_ref, k_ref, v_ref, lse_ref, o32_ref, own_ref, oth_ref, wbuf, sem = rest
    copies = load_qkv(units, wbuf, sem)
    for copy in copies:
        copy.start()
    tok = x0.shape[0]
    for j, x in enumerate((x0, x1, x2, x3)):
        if raw:
            a = layer_norm(x[...].astype(F32), vec[row : row + 1, :], vec[row + 1 : row + 2, :])
            a_ref[j * tok : (j + 1) * tok, :] = a.astype(BF)
        else:
            a_ref[j * tok : (j + 1) * tok, :] = x[...]
    start = pl.multiple_of(core[0] * UNIT, 128)
    qb = vec[row + 2 : row + 3, pl.ds(start, UNIT)]
    vb = vec[row + 3 : row + 4, pl.ds(start, UNIT)]
    for copy in copies:
        copy.wait()
    k_ref[...] = fdot(a_ref[...], wbuf[:, UNIT : 2 * UNIT]).astype(BF)
    v_ref[...] = (fdot(a_ref[...], wbuf[:, 2 * UNIT :]) + vb).astype(BF)
    q_ref[...] = (fdot(a_ref[: 2 * tok, :], wbuf[:, :UNIT]) + qb).astype(BF)
    ids = idc[...]
    lane_k = lanes(4 * tok)
    lane_q = lanes(tok)
    lse_all = [jnp.zeros((tok, 128), F32) for _ in range(2)]
    for t in range(3):
        cols = slice(t * 128, (t + 1) * 128)
        tiles = [[], []]
        for hh in range(2):
            base = 64 * (1 - hh)
            sel_k = (lane_k < 64) == (hh == 0)
            sel_q = (lane_q < 64) == (hh == 0)
            kk = jnp.where(
                sel_k, k_ref[:, cols].astype(F32), place(lane_k, base, [-1e30 * (1 - ids), -1e30 * ids])
            ).astype(BF)
            vv = jnp.where(sel_k, v_ref[:, cols].astype(F32), 1.0).astype(BF)
            for b in range(2):
                rows = slice(b * tok, (b + 1) * tok)
                idq = ids[rows, :]
                qq = jnp.where(
                    sel_q,
                    q_ref[rows, cols].astype(F32) * HD**-0.5,
                    place(lane_q, base, [idq, 1 - idq]),
                ).astype(BF)
                s = fdot(qq, kk, 1, 1)
                peak = jnp.max(s, -1, keepdims=True)
                e = jnp.exp(s - peak).astype(BF)
                o = fdot(e, vv)
                total = o[:, base : base + 1]
                lse = peak + jnp.log(total)
                lse_all[b] = jnp.where(lane_q == 2 * t + hh, lse, lse_all[b])
                tiles[b].append(o / total)
        for b, out in enumerate((own_ref, oth_ref)):
            o = jnp.where(lane_q < 64, tiles[b][0], tiles[b][1])
            o32_ref[b * tok : (b + 1) * tok, cols] = o
            out[:, cols] = o.astype(BF)
    for b in range(2):
        lse_ref[b * tok : (b + 1) * tok, :] = lse_all[b]


def attn_fwd(raw, row, core, parts, units, vec, idc, deps=()):
    tok = parts[0].shape[0]
    width = parts[0].shape[1]
    sds = pltpu.HBM
    shapes = [
        sds((4 * tok, width), BF),
        sds((2 * tok, UNIT), BF),
        sds((4 * tok, UNIT), BF),
        sds((4 * tok, UNIT), BF),
        sds((2 * tok, 128), F32),
        sds((2 * tok, UNIT), F32),
        sds((tok, UNIT), BF),
        sds((tok, UNIT), BF),
    ]
    scratch = [pltpu.VMEM((width, 3 * UNIT), BF), pltpu.SemaphoreType.DMA((3,))]
    return pl.pallas_call(
        functools.partial(attn_fwd_kernel, raw, row, len(deps)),
        out_shape=shapes,
        in_specs=[SMEM] + [VMEM] * 4 + [ANY] + [VMEM] * 2 + [ANY] * len(deps),
        out_specs=[VMEM] * len(shapes),
        scratch_shapes=scratch,
        compiler_params=ROOMY,
        cost_estimate=LIGHT,
    )(core, *pin(parts[0]), *parts[1:], *pin(units, vec), idc, *deps)


def load_mlp(wide, outs, pbuf, ibuf, obuf, sem):
    proj, inner, last = [], [], []
    for side in range(2):
        cols = pl.ds(side * UNIT, UNIT)
        proj.append(pltpu.make_async_copy(wide.at[side, 0], pbuf.at[:, cols], sem.at[side, 0]))
        for j in range(4):
            at = pl.ds((side * 4 + j) * UNIT, UNIT)
            inner.append(
                pltpu.make_async_copy(wide.at[side, 1 + j], ibuf.at[:, at], sem.at[side, 1 + j])
            )
        last.append(pltpu.make_async_copy(outs.at[side], obuf.at[:, cols], sem.at[side, 5]))
    return proj, inner, last


def wait_all(copies):
    for copy in copies:
        copy.wait()


def mlp_fwd_kernel(row, last, core, x, o_own, o_oth, vec, fin, *rest):
    wide, outs_w, outs = rest[0], rest[1], rest[2:-5]
    pbuf, ibuf, obuf, full, sem = rest[-5:]
    m_ref, pack, d_ref, y_ref = outs[:4]
    proj, inner, outer = load_mlp(wide, outs_w, pbuf, ibuf, obuf, sem)
    for copy in proj + inner + outer:
        copy.start()
    width = x.shape[1]
    here = pl.multiple_of(core[0] * UNIT, 128)
    there = pl.multiple_of((1 - core[0]) * UNIT, 128)
    full[:, pl.ds(here, UNIT)] = o_own[...]
    full[:, pl.ds(there, UNIT)] = o_oth[...]
    pack[:, 5 * width :] = full[...]
    wait_all(proj)
    m = x[...].astype(F32) + (fdot(full[...], pbuf[...]) + vec[row + 4 : row + 5, :])
    m_ref[...] = m
    c = layer_norm(m, vec[row + 5 : row + 6, :], vec[row + 6 : row + 7, :]).astype(BF)
    pack[:, :width] = c
    wait_all(inner)
    total = None
    for j in range(4):
        cols = slice(j * width, (j + 1) * width)
        u = fdot(c, ibuf[:, cols]) + fin[row // 12 : row // 12 + 1, cols]
        cdf = 0.5 + 0.5 * lax.erf(u * 0.5**0.5)
        z = (u * cdf).astype(BF)
        pack[:, (j + 1) * width : (j + 2) * width] = z
        d_ref[:, cols] = (cdf + u * (jnp.exp(-0.5 * u * u) * (0.5 / jnp.pi) ** 0.5)).astype(d_ref.dtype)
        if j == 0:
            wait_all(outer)
        part = fdot(z, obuf[cols, :])
        total = part if total is None else total + part
    y = m + (total + vec[row + 7 : row + 8, :])
    y_ref[...] = y.astype(y_ref.dtype)
    if not last:
        a = layer_norm(y, vec[row + 12 : row + 13, :], vec[row + 13 : row + 14, :])
        outs[4][...] = a.astype(BF)


def mlp_scratch(width):
    return [
        pltpu.VMEM((width, width), BF),
        pltpu.VMEM((width, 4 * width), BF),
        pltpu.VMEM((4 * width, width), BF),
        pltpu.VMEM((8, 128), F32),
        pltpu.SemaphoreType.DMA((2, 6)),
    ]


def mlp_fwd(row, last, core, x, o_own, o_oth, vec, fin, weights):
    tok, width = x.shape
    sds = pltpu.HBM
    shapes = [
        sds((tok, width), F32),
        sds((tok, 6 * width), BF),
        sds((tok, 4 * width), F32),
        sds((tok, width), BF if last else F32),
    ]
    if not last:
        shapes.append(sds((tok, width), BF))
    scratch = mlp_scratch(width)
    scratch[3] = pltpu.VMEM((tok, width), BF)
    return pl.pallas_call(
        functools.partial(mlp_fwd_kernel, row, last),
        out_shape=shapes,
        in_specs=[SMEM] + [VMEM] * 5 + [ANY] * 2,
        out_specs=[VMEM] * len(shapes),
        scratch_shapes=scratch,
        compiler_params=ROOMY,
        cost_estimate=LIGHT,
    )(core, *pin(x, o_own), o_oth, *pin(vec, fin, *weights))


def norm_back_kernel(row, vec, x, gmid, da, near, far):
    grad = da[...] + near[: da.shape[0], :].astype(F32) + far[...].astype(F32)
    dx, gain_g, bias_g = norm_back(x[...].astype(F32), vec[row : row + 1, :], grad)
    return gmid[...] + dx, gain_g, bias_g


def mlp_bwd_kernel(row, first, n_dep, core, vec, m_ref, d_ref, *rest):
    n_in = 1 if first else 5
    ins, (wide, outs_w), rest = rest[:n_in], rest[n_in : n_in + 2], rest[n_in + 2 + n_dep :]
    pbuf, ibuf, obuf, full, sem = rest[-5:]
    gmid_ref, own, oth, rows_ref, fin_ref = rest[:-5]
    proj, inner, outer = load_mlp(wide, outs_w, pbuf, ibuf, obuf, sem)
    for copy in outer + inner + proj:
        copy.start()
    width = m_ref.shape[1]
    half = width // 2

    def split(value, at):
        full[:, :width] = value
        here = pl.multiple_of(core[0] * half, 128)
        there = pl.multiple_of((1 - core[0]) * half, 128)
        own[:, at : at + half] = full[:, pl.ds(here, half)]
        oth[:, at : at + half] = full[:, pl.ds(there, half)]

    rows_ref[...] = jnp.zeros(rows_ref.shape, F32)
    if first:
        gx = ins[0][...].astype(F32)
    else:
        gx, gain_g, bias_g = norm_back_kernel(row + 12, vec, *ins)
        rows_ref[8:9, :] = gain_g
        rows_ref[9:10, :] = bias_g
    gm = gx.astype(BF)
    rows_ref[7:8, :] = jnp.sum(gm.astype(F32), 0, keepdims=True)
    split(gm, 2 * width)
    wait_all(outer)
    total = None
    for j in range(4):
        cols = slice(j * width, (j + 1) * width)
        dz = fdot(gm, obuf[cols, :], 1, 1)
        gu = (d_ref[:, cols].astype(F32) * dz).astype(BF)
        full[:, cols] = gu
        fin_ref[:, cols] = jnp.sum(gu.astype(F32), 0, keepdims=True)
        if j == 0:
            wait_all(inner)
        part = fdot(gu, ibuf[:, cols], 1, 1)
        total = part if total is None else total + part
    own[:, : 2 * width] = full[:, pl.ds(pl.multiple_of(core[0] * 2 * width, 128), 2 * width)]
    oth[:, : 2 * width] = full[:, pl.ds(pl.multiple_of((1 - core[0]) * 2 * width, 128), 2 * width)]
    dm, gain_g, bias_g = norm_back(m_ref[...], vec[row + 5 : row + 6, :], total)
    rows_ref[5:6, :] = gain_g
    rows_ref[6:7, :] = bias_g
    gmid = gx + dm
    gmid_ref[...] = gmid
    ga = gmid.astype(BF)
    rows_ref[4:5, :] = jnp.sum(ga.astype(F32), 0, keepdims=True)
    split(ga, 2 * width + half)
    wait_all(proj)
    split(fdot(ga, pbuf[...], 1, 1).astype(BF), 3 * width)


def mlp_bwd(row, first, core, vec, m, d, ins, weights, deps):
    tok, width = m.shape
    sds = pltpu.HBM
    shapes = (
        [sds((tok, width), F32)]
        + [sds((tok, 7 * width // 2), BF)] * 2
        + [sds((16, width), F32), sds((1, 4 * width), F32)]
    )
    scratch = mlp_scratch(width)
    scratch[3] = pltpu.VMEM((tok, 4 * width), BF)
    return pl.pallas_call(
        functools.partial(mlp_bwd_kernel, row, first, len(deps)),
        out_shape=shapes,
        in_specs=[SMEM] + [VMEM] * (3 + len(ins)) + [ANY] * (2 + len(deps)),
        out_specs=[VMEM] * len(shapes),
        scratch_shapes=scratch,
        compiler_params=ROOMY,
        cost_estimate=LIGHT,
    )(core, *pin(vec, m, d, *ins[:3]), *ins[3:], *pin(*weights), *deps)


def last_norm_kernel(row, vec, x, gmid, da, near, far, gx_ref):
    gx_ref[...] = norm_back_kernel(row, vec, x, gmid, da, near, far)[0]


def last_norm(row, vec, ins):
    return pl.pallas_call(
        functools.partial(last_norm_kernel, row),
        out_shape=pltpu.HBM(ins[1].shape, F32),
        in_specs=[VMEM] * 6,
        out_specs=VMEM,
        compiler_params=ROOMY,
        cost_estimate=LIGHT,
    )(*pin(vec, *ins[:3]), *ins[3:])


def attn_bwd_kernel(row, n_raw, n_dep, q_ref, k_ref, v_ref, lse_ref, o32_ref, idc, *rest):
    raw, rest = rest[:n_raw], rest[n_raw:]
    (go_own, go_oth, units), rest = rest[:3], rest[3 + n_dep :]
    (
        gq_ref,
        gk_ref,
        gv_ref,
        da_own,
        da_keep,
        da_send,
        sums,
        rows_ref,
        go_ref,
        wbuf,
        sem,
    ) = rest
    tok = go_own.shape[0]
    width = units.shape[1]
    at = pl.ds(3 * width, UNIT)
    first = [
        pltpu.make_async_copy(go_own.at[:, at], go_ref.at[pl.ds(0, tok)], sem.at[3]),
        pltpu.make_async_copy(go_oth.at[:, at], go_ref.at[pl.ds(tok, tok)], sem.at[4]),
    ]
    copies = load_qkv(units, wbuf, sem)
    for copy in first + copies:
        copy.start()
    wait_all(first)
    ids = idc[...]
    near = 2 * tok
    lane_q = lanes(near)
    lane_k = lanes(near)
    for t in range(3):
        cols = slice(t * 128, (t + 1) * 128)
        gq_tile = []
        gk_tile = [[], []]
        gv_tile = [[], []]
        for hh in range(2):
            base = 64 * (1 - hh)
            h = 2 * t + hh
            sel = (lane_q < 64) == (hh == 0)
            go32 = go_ref[:, cols].astype(F32)
            inner = jnp.sum(jnp.where(sel, go32 * o32_ref[:, cols], 0.0), -1, keepdims=True)
            lse = lse_ref[:, h : h + 1]
            idq = ids[:near, :]
            qq = jnp.where(
                sel,
                q_ref[:, cols].astype(F32) * HD**-0.5,
                place(lane_q, base, [idq, 1 - idq] + three(-lse)),
            ).astype(BF)
            gg = jnp.where(sel, go32, place(lane_q, base, three(-inner))).astype(BF)
            gq = None
            for b in range(2):
                rows = slice(b * near, (b + 1) * near)
                idk = ids[rows, :]
                kk = jnp.where(
                    sel,
                    k_ref[rows, cols].astype(F32),
                    place(lane_k, base, [-1e30 * (1 - idk), -1e30 * idk, 1.0, 1.0, 1.0]),
                ).astype(BF)
                vv = jnp.where(
                    sel, v_ref[rows, cols].astype(F32), place(lane_k, base, [1.0, 1.0, 1.0])
                ).astype(BF)
                prob = jnp.exp(fdot(kk, qq, 1, 1))
                gs = (prob * fdot(vv, gg, 1, 1)).astype(BF)
                gv_tile[b].append(fdot(prob.astype(BF), go_ref[:, cols]))
                gk_tile[b].append(fdot(gs, q_ref[:, cols]))
                part = fdot(gs, k_ref[rows, cols], 0, 0)
                gq = part if gq is None else gq + part
            gq_tile.append(gq)
        left = lane_q < 64
        gq_ref[:, cols] = (jnp.where(left, gq_tile[0], gq_tile[1]) * HD**-0.5).astype(BF)
        for b in range(2):
            rows = slice(b * near, (b + 1) * near)
            gk_ref[rows, cols] = (jnp.where(left, *gk_tile[b]) * HD**-0.5).astype(BF)
            gv_ref[rows, cols] = jnp.where(left, *gv_tile[b]).astype(BF)
    for copy in copies:
        copy.wait()
    far = fdot(gk_ref[near:, :], wbuf[:, UNIT : 2 * UNIT], 1, 1) + fdot(
        gv_ref[near:, :], wbuf[:, 2 * UNIT :], 1, 1
    )
    da_keep[...] = far[:tok]
    da_send[tok:, :] = far[tok:].astype(BF)
    own = (
        fdot(gk_ref[:near, :], wbuf[:, UNIT : 2 * UNIT], 1, 1)
        + fdot(gv_ref[:near, :], wbuf[:, 2 * UNIT :], 1, 1)
        + fdot(gq_ref[...], wbuf[:, :UNIT], 1, 1)
    )
    da_own[...] = own[:tok]
    da_send[:tok, :] = own[tok:].astype(BF)
    rows_ref[...] = jnp.zeros(rows_ref.shape, F32)
    if raw:
        gain_g, bias_g = 0.0, 0.0
        for x, grad in zip(raw, (own[:tok], own[tok:], far[:tok], far[tok:])):
            n = norm_parts(x[...].astype(F32))[0]
            gain_g = gain_g + jnp.sum(grad * n, 0, keepdims=True)
            bias_g = bias_g + jnp.sum(grad, 0, keepdims=True)
        rows_ref[0:1, :] = gain_g
        rows_ref[1:2, :] = bias_g
    sums[...] = jnp.zeros(sums.shape, F32)
    sums[0:1, :] = jnp.sum(gq_ref[...].astype(F32), 0, keepdims=True)
    sums[1:2, :] = jnp.sum(gv_ref[...].astype(F32), 0, keepdims=True)


def attn_bwd(row, saved, raw, go_own, go_oth, idc, units, deps):
    tok = go_own.shape[0]
    width = units.shape[1]
    sds = pltpu.HBM
    shapes = [
        sds((2 * tok, UNIT), BF),
        sds((4 * tok, UNIT), BF),
        sds((4 * tok, UNIT), BF),
        sds((tok, width), F32),
        sds((tok, width), F32),
        sds((2 * tok, width), BF),
        sds((8, UNIT), F32),
        sds((8, width), F32),
    ]
    return pl.pallas_call(
        functools.partial(attn_bwd_kernel, row, len(raw), len(deps)),
        out_shape=shapes,
        in_specs=[VMEM] * (6 + len(raw)) + [ANY] * (3 + len(deps)),
        out_specs=[VMEM] * len(shapes),
        scratch_shapes=[
            pltpu.VMEM((2 * tok, UNIT), BF),
            pltpu.VMEM((width, 3 * UNIT), BF),
            pltpu.SemaphoreType.DMA((5,)),
        ],
        compiler_params=ROOMY,
        cost_estimate=LIGHT,
    )(*pin(*saved, idc, *raw, go_own), go_oth, *pin(units), *deps)


def deal(table, outs, buf, value, j, at):
    buf[at] = value.reshape(32, ROWS, UNIT)
    for dq, out in enumerate(outs):
        for p in range(4):
            for x in range(2):
                out[p, x, j] = buf[at, table[dq * 8 + p * 2 + x]].astype(BF)


def blocks_shape(count):
    return [pltpu.HBM((4, 2, count, ROWS, UNIT), BF)] * 4


def qkv_grad_kernel(with_vec, n_dep, table, core, a_ref, gq, gk, gv, *rest):
    n_vec = 7 if with_vec else 0
    vecs, rest = rest[:n_vec], rest[n_vec + n_dep :]
    outs, buf = rest[:4], rest[4]
    near = gq.shape[0]
    deal(table, outs, buf, fdot(a_ref[:near, :], gq[...], 0, 0), 0, 0)
    deal(table, outs, buf, fdot(a_ref[...], gk[...], 0, 0), 1, 1)
    deal(table, outs, buf, fdot(a_ref[...], gv[...], 0, 0), 2, 0)
    if with_vec:
        vbuf, tbuf, fbuf, wbuf = rest[5:9]
        rows0, rows1, sums0, sums1, fin0, fin1, norm0 = vecs
        vbuf[...] = jnp.zeros(vbuf.shape, F32)
        fbuf[...] = jnp.zeros(fbuf.shape, F32)
        cols = pl.ds(pl.multiple_of(core[0] * UNIT, 128), UNIT)
        vbuf[0:2, :] = norm0[0:2, :]
        vbuf[12:14, :] = rows0[8:10, :]
        for l, (rows, sums, fin) in enumerate(((rows0, sums0, fin0), (rows1, sums1, fin1))):
            vbuf[l * 12 + 2 : l * 12 + 3, cols] = sums[0:1, :]
            vbuf[l * 12 + 3 : l * 12 + 4, cols] = sums[1:2, :]
            vbuf[l * 12 + 4 : l * 12 + 8, :] = rows[4:8, :]
            fbuf[l : l + 1, : fin.shape[1]] = fin[...]
        tbuf[...] = vbuf[...].T.reshape(32, ROWS, 128)
        wbuf[...] = jnp.zeros(wbuf.shape, F32)
        for f in range(32):
            base, off = window(f)
            piece = fbuf[:, base : base + 256]
            if off:
                piece = pltpu.roll(piece, 256 - off, 1)
            wbuf[f, :8, :] = piece[:, :128]
        none = jnp.zeros((ROWS, 128), F32)
        for n, (dq, p, x) in enumerate(SLOTS):
            unit = jnp.concatenate([tbuf[table[n]], wbuf[table[n]], none], 1)
            outs[dq][p, x, 3] = unit.astype(BF)


def qkv_grad(table, core, a_all, gq, gk, gv, vecs, deps):
    count = 4 if vecs else 3
    scratch = [pltpu.VMEM((2, 32, ROWS, UNIT), F32)]
    if vecs:
        scratch += [
            pltpu.VMEM((128, a_all.shape[1]), F32),
            pltpu.VMEM((32, ROWS, 128), F32),
            pltpu.VMEM((8, 4 * a_all.shape[1] + 128), F32),
            pltpu.VMEM((32, ROWS, 128), F32),
        ]
    return pl.pallas_call(
        functools.partial(qkv_grad_kernel, bool(vecs), len(deps)),
        out_shape=blocks_shape(count),
        in_specs=[SMEM] * 2 + [VMEM] * (4 + len(vecs)) + [ANY] * len(deps),
        out_specs=[VMEM] * 4,
        scratch_shapes=scratch,
        compiler_params=ROOMY,
        cost_estimate=LIGHT,
    )(table, core, *pin(a_all, gq, gk, gv, *vecs), *deps)


def mlp_grad_kernel(joint, table, f0, f1, b0, b1, *rest):
    if joint:
        dests, (out, sem, buf, obuf) = rest[4:8], rest[8:]
    else:
        out, buf, obuf = rest
    outs = [out.at[q] for q in range(4)]
    width = f0.shape[1] // 6

    def both(lc, rc):
        return fdot(f0[:, lc], b0[:, rc], 0, 0) + fdot(f1[:, lc], b1[:, rc], 0, 0)

    def cols(begin, size):
        return slice(begin, begin + size)

    for j in range(4):
        deal(table, outs, buf, both(cols(0, width), cols(j * UNIT, UNIT)), j, j % 2)
    ga = cols(2 * width + UNIT, UNIT)
    deal(table, outs, buf, both(cols(5 * width, width), ga), 4, 0)
    for j in range(4):
        part = both(cols((j + 1) * width, width), cols(2 * width, UNIT))
        obuf[j * 8 : (j + 1) * 8] = part.reshape(8, 4, ROWS, UNIT)
    for n, (dq, p, x) in enumerate(SLOTS):
        outs[dq][p, x, pl.ds(5, 4)] = obuf[table[n]].astype(BF)
    if joint:
        spread_units(out, dests, sem, 0)


def mlp_grad(table, packs, joint=()):
    more = len(joint)
    blocks = (4, 4, 2, 9, ROWS, UNIT)
    scratch = [
        pltpu.VMEM((2, 32, ROWS, UNIT), F32),
        pltpu.VMEM((32, 4, ROWS, UNIT), F32),
    ]
    if more:
        scratch = [pltpu.VMEM(blocks, BF), pltpu.SemaphoreType.DMA((4,))] + scratch
    return pl.pallas_call(
        functools.partial(mlp_grad_kernel, more),
        out_shape=blocks_shape(12) if more else pltpu.HBM(blocks, BF),
        in_specs=[SMEM] + [VMEM] * 4 + [ANY] * more,
        out_specs=[ANY] * 4 if more else VMEM,
        input_output_aliases={5 + i: i for i in range(more)},
        scratch_shapes=scratch,
        compiler_params=ROOMY,
        cost_estimate=LIGHT,
    )(table, *pin(packs[0]), packs[1], *pin(packs[2]), packs[3], *joint)


def spread_units(out, dests, sem, begin):
    count = out.shape[3]
    run_all(
        [
            pltpu.make_async_copy(out.at[q], dest.at[:, :, pl.ds(begin, count)], sem.at[q])
            for q, dest in enumerate(dests)
        ]
    )


def qkv_grad_rest_kernel(n_dep, table, a_ref, gq, gk, gv, *rest):
    rest = rest[n_dep:]
    dests, (out, buf, sem) = rest[:4], rest[4:]
    outs = [out.at[q] for q in range(4)]
    near = gq.shape[0]
    deal(table, outs, buf, fdot(a_ref[:near, :], gq[...], 0, 0), 0, 0)
    deal(table, outs, buf, fdot(a_ref[...], gk[...], 0, 0), 1, 1)
    deal(table, outs, buf, fdot(a_ref[...], gv[...], 0, 0), 2, 0)
    spread_units(out, dests, sem, 9)


def qkv_grad_rest(table, a_all, gq, gk, gv, deps):
    return pl.pallas_call(
        functools.partial(qkv_grad_rest_kernel, len(deps)),
        out_shape=blocks_shape(12),
        in_specs=[SMEM] + [VMEM] * 4 + [ANY] * len(deps),
        out_specs=[ANY] * 4,
        scratch_shapes=[
            pltpu.VMEM((4, 4, 2, 3, ROWS, UNIT), BF),
            pltpu.VMEM((2, 32, ROWS, UNIT), F32),
            pltpu.SemaphoreType.DMA((4,)),
        ],
        compiler_params=ROOMY,
        cost_estimate=LIGHT,
    )(table, *pin(a_all, gq, gk, gv), *deps)


def reduce_along(blocks, sets):
    flat = blocks.reshape(-1, ROWS, UNIT)
    got = lax.psum_scatter(flat, AXES, scatter_dimension=0, axis_index_groups=sets, tiled=True)
    return got.reshape(blocks.shape[1:])


def gather_along(block, sets):
    flat = block.reshape(-1, ROWS, UNIT)
    got = lax.all_gather(flat, AXES, axis=0, axis_index_groups=sets, tiled=True)
    return got.reshape(4, *block.shape)


def finish_kernel(core, own0, oth0, own1, oth1, *rest):
    qkv, proj, fc_in, fc_out, fin = rest[:5]
    vecs, vbuf = rest[5:13], rest[13]
    first = core[0] == 0
    for l, (own, oth) in enumerate(((own0, oth0), (own1, oth1))):

        def put(out, rows, at, unit, own=own, oth=oth):
            lo = jnp.where(first, own[unit], oth[unit]).astype(F32)
            hi = jnp.where(first, oth[unit], own[unit]).astype(F32)
            out[l, rows, at[0] : at[0] + UNIT] = lo
            out[l, rows, at[1] : at[1] + UNIT] = hi

        every = slice(0, ROWS)
        for j in range(4):
            put(fc_in, every, (j * UNIT, (j + 4) * UNIT), j)
            put(fc_out, slice(j * ROWS, (j + 1) * ROWS), (0, UNIT), 5 + j)
        put(proj, every, (0, UNIT), 4)
        for j in range(3):
            at = 12 + j if l == 0 else 9 + j
            put(qkv, every, (2 * j * UNIT, (2 * j + 1) * UNIT), at, own0, oth0)
    both = own0[15].astype(F32) + oth0[15].astype(F32)
    fin[...] = both[0:2, 128:224]
    vbuf[...] = jnp.zeros(vbuf.shape, F32)
    vbuf[:ROWS, :] = both[:, :128]
    turned = vbuf[...].T
    for j, vec in enumerate(vecs):
        for l in range(2):
            vec[l : l + 1, :] = turned[l * 12 + j : l * 12 + j + 1, :ROWS]


def finish(core, parts):
    sds = jax.ShapeDtypeStruct
    width = 2 * UNIT
    return pl.pallas_call(
        finish_kernel,
        out_shape=[
            sds((2, ROWS, 3 * width), F32),
            sds((2, ROWS, width), F32),
            sds((2, ROWS, 4 * width), F32),
            sds((2, 4 * ROWS, width), F32),
            sds((2, 4 * ROWS), F32),
        ]
        + [sds((2, ROWS), F32)] * 8,
        in_specs=[SMEM] + [VMEM] * 4,
        out_specs=[VMEM] * 13,
        scratch_shapes=[pltpu.VMEM((128, 128), F32)],
        compiler_params=ROOMY,
        cost_estimate=LIGHT,
    )(core, *parts)


def body(
    tokens,
    image_ids,
    cotangent,
    attn_norm_gain,
    attn_norm_bias,
    qkv_weight,
    query_bias,
    value_bias,
    proj_weight,
    proj_bias,
    mlp_norm_gain,
    mlp_norm_bias,
    fc_in_weight,
    fc_in_bias,
    fc_out_weight,
    fc_out_bias,
):
    core, xh, xl = (lax.axis_index(n) for n in ("core", "xh", "xl"))
    width = tokens.shape[2]
    tok = tokens.shape[1]

    one = core.astype(jnp.int32).reshape(1)
    xl_one = xl.astype(jnp.int32).reshape(1)
    z, y = lax.axis_index("z"), lax.axis_index("y")
    inner_at = jnp.where(core == 0, y, z).astype(jnp.int32).reshape(1)
    table = slot_table(-1, core)
    table_o = slot_table(-1, 1 - core)
    table_out = slot_table(1, core)
    table_abs = slot_table(-1, core, True)
    table_abs_o = slot_table(-1, 1 - core, True)
    table_sum = slot_table(1, core, True)

    def segment(dx, dc):
        return lax.dynamic_slice_in_dim(
            image_ids[0], (((xh + dx) % 2) * 2 + (core + dc) % 2) * tok, tok, 0
        )

    ids = jnp.concatenate([segment(0, 0), segment(0, 1), segment(1, 0), segment(1, 1)])
    idc = ids.astype(F32)[:, None]

    u12, u3 = prep(
        one,
        pin(
            attn_norm_gain,
            attn_norm_bias,
            query_bias,
            value_bias,
            proj_bias,
            mlp_norm_gain,
            mlp_norm_bias,
            fc_out_bias,
            fc_in_bias,
            qkv_weight,
            proj_weight,
            fc_in_weight,
            fc_out_weight,
        ),
    )
    tokens_own = tokens[0]
    u12_far = to_xl(u12)
    p1 = jnp.stack([u12[:4], u12_far[:4]])
    p2 = jnp.stack([u12[4:], u12_far[4:]])
    tokens_far = to_xh(tokens_own)
    share = [tokens_own, to_core(tokens_own), tokens_far, to_core(tokens_far)]
    s1 = three_inner(p1)
    inner1 = after(inner_of(p1, s1), tokens_far)
    pieces1 = [inner1] + three_outer(inner1)
    p2 = after(p2, *pieces1[1:])
    u3 = after(u3, inner1)
    p3 = jnp.stack([u3, to_xl(u3)])
    p3 = after(p3, *pieces1[1:])
    inner3 = gather_along(p3, INNER)
    s2 = three_inner(p2)
    qkv0, vec_rows, fins = assemble_first(table, pieces1, [p2, p3])
    qkv0 = qkv0.reshape(3, width, UNIT)
    fwd0 = attn_fwd(True, 0, one, share, qkv0, vec_rows, idc)
    o_own, o_oth = fwd0[6:]
    o_got = to_core(o_oth)
    inner2 = inner_of(p2, [after(part, o_own) for part in s2])
    pieces2 = [inner2] + three_outer(inner2)
    others2 = [to_core(piece) for piece in pieces2]
    inner3 = after(after(inner3, o_own), *pieces2[1:])
    pieces3 = [inner3] + three_outer(inner3)
    full0 = assemble_both(0, one, [table, table_o], pieces2, others2, [o_got, inner3])
    m0, pack0, d0, x1, a1 = mlp_fwd(0, False, one, tokens_own, o_own, o_got, vec_rows, fins, full0)
    pack0_o = to_core(pack0)
    a1_far = to_xh(a1)
    share1 = [a1, to_core(a1), a1_far, to_core(a1_far)]
    pieces3 = [inner3] + [after(piece, x1) for piece in pieces3[1:]]
    qkv1 = assemble(table_abs, pieces3, []).reshape(3, width, UNIT)
    fwd1 = attn_fwd(False, 12, one, share1, qkv1, vec_rows, idc, [pack0_o])
    o_own, o_oth = fwd1[6:]
    o_got = to_core(o_oth)
    others3 = [to_core(part) for part in pieces3]
    full1 = assemble_both(3, one, [table_abs, table_abs_o], pieces3, others3, [o_got])
    m1, pack1, d1, block_output = mlp_fwd(12, True, one, x1, o_own, o_got, vec_rows, fins, full1)
    pack1_o = to_core(pack1)

    gmid1, own1, oth1, rows1, fing1 = mlp_bwd(
        12, True, one, vec_rows, m1, d1, [cotangent[0]], full1, [block_output]
    )
    got1 = to_core(oth1)
    block_a = mlp_grad(table_sum, [pack1, pack1_o, own1, got1])
    sum_a = reduce_along(block_a, OUTER)
    gq, gk, gv, da, da_keep, da_send, sums1, _ = attn_bwd(
        12, fwd1[1:6], [], own1, got1, idc, qkv1, [block_a]
    )
    da_got = to_core(da_send)
    far_in = (da_keep + da_got[tok:].astype(F32)).astype(BF)
    far = to_xh(far_in)
    block_e = qkv_grad_rest(table_out, fwd1[0], gq, gk, gv, [far_in])

    gmid0, own0, oth0, rows0, fing0 = mlp_bwd(
        0, False, one, vec_rows, m0, d0, [x1, gmid1, da, da_got, far], full0, block_e
    )
    got0 = to_core(oth0)
    sum_a = after(sum_a, gmid0)
    mid_a = sum_a
    sum_a = reduce_along(sum_a, INNER)
    block_b = mlp_grad(table_out, [pack0, pack0_o, own0, got0], block_e)
    sent_b = send_outer(block_b)
    gq, gk, gv, da, da_keep, da_send, sums0, norm0 = attn_bwd(
        0, fwd0[1:6], share, own0, got0, idc, qkv0, [block_b[0], mid_a]
    )
    da_got = to_core(da_send)
    far = to_xh((da_keep + da_got[tok:].astype(F32)).astype(BF))

    vecs = [rows0, rows1, sums0, sums1, fing0, fing1, norm0]
    block_c = qkv_grad(table_out, one, fwd0[0], gq, gk, gv, vecs, [])
    sent_c = send_outer(block_c)
    gx = last_norm(0, vec_rows, [tokens_own, gmid0, da, da_got, far])
    mine_a, other_a = sum_inner(xl_one, [[sum_a]], [block_c[0]])
    part_a = add_all(mine_a, to_xl(other_a))
    part_a = add_all(part_a, to_xh(part_a))
    part_a_o = to_core(part_a)
    sum_bc = sum_outer(inner_at, [sent_b, sent_c], [far, other_a])
    sent_bc = [sum_bc[0]] + [to_inner(sum_bc[d], d) for d in (1, 2, 3)]
    mine_bc, other_bc = sum_inner(xl_one, [sent_bc], [gx])
    part_bc = add_all(mine_bc, to_xl(other_bc))
    part_bc = add_all(part_bc, to_xh(part_bc))
    done = finish(one, [part_bc, to_core(part_bc), part_a, part_a_o])
    qkv_g, proj_g, fc_in_g, fc_out_g, fin_g = done[:5]
    vec_g = done[5:]
    return (
        block_output[None],
        gx[None],
        vec_g[0],
        vec_g[1],
        qkv_g,
        vec_g[2],
        vec_g[3],
        proj_g,
        vec_g[4],
        vec_g[5],
        vec_g[6],
        fc_in_g,
        fin_g,
        fc_out_g,
        vec_g[7],
    )


def solution(mesh):
    fine = Mesh(mesh.devices.reshape(SIZES), AXES)
    row = P(None, FSDP)
    mat = P(None, FSDP, None)
    tok = P(FSDP, SEQ, None)
    return jax.shard_map(
        body,
        mesh=fine,
        in_specs=(
            tok,
            P(FSDP, None),
            tok,
            row,
            row,
            mat,
            row,
            row,
            mat,
            row,
            row,
            row,
            mat,
            row,
            mat,
            row,
        ),
        out_specs=(tok, tok, row, row, mat, row, row, mat, row, row, row, mat, row, mat, row),
        check_vma=False,
    )
```

```python
import functools

import jax
import jax.numpy as jnp
from jax import lax
from jax.experimental import pallas as pl
from jax.experimental.pallas import tpu as pltpu
from jax.sharding import Mesh
from jax.sharding import PartitionSpec as P

HD = 64
AXES = ("xh", "core", "z", "xl", "y")
SIZES = (2, 2, 4, 2, 4)
FSDP = ("z", "xl", "y")
SEQ = ("xh", "core")
UNIT = 384
ROWS = 24
BF = jnp.bfloat16
F32 = jnp.float32
ANY = pl.BlockSpec(memory_space=pl.ANY)
SMEM = pl.BlockSpec(memory_space=pltpu.SMEM)
VMEM = pl.BlockSpec(memory_space=pltpu.VMEM)
LIGHT = pl.CostEstimate(flops=10**6, bytes_accessed=10**5, transcendentals=0)
ROOMY = pltpu.CompilerParams(vmem_limit_bytes=48 * 2**20)


def ravel(coords):
    index = 0
    for size, coord in zip(SIZES, coords):
        index = index * size + coord % size
    return index


def all_coords():
    xh_n, core_n, z_n, xl_n, y_n = SIZES
    return [
        (xh, core, z, xl, y)
        for xh in range(xh_n)
        for core in range(core_n)
        for z in range(z_n)
        for xl in range(xl_n)
        for y in range(y_n)
    ]


def shift(array, move):
    pairs = [(ravel(c), ravel(move(*c))) for c in all_coords()]
    return lax.ppermute(array, AXES, pairs)


def to_core(array):
    return shift(array, lambda xh, core, z, xl, y: (xh, core + 1, z, xl, y))


def to_xh(array):
    return shift(array, lambda xh, core, z, xl, y: (xh + 1, core, z, xl, y))


def to_xl(array):
    return shift(array, lambda xh, core, z, xl, y: (xh, core, z, xl + 1, y))


def to_next_x(array, d):
    def move(xh, core, z, xl, y):
        x = (2 * xh + xl + d) % 4
        return (x // 2, core, z, x % 2, y)

    return shift(array, move)


def to_inner(array, d):
    return shift(
        array,
        lambda xh, core, z, xl, y: (xh, core, z, xl, y + d) if core == 0 else (xh, core, z + d, xl, y),
    )


def to_outer(array, d):
    return shift(
        array,
        lambda xh, core, z, xl, y: (xh, core, z + d, xl, y) if core == 0 else (xh, core, z, xl, y + d),
    )


def nothing(*refs):
    del refs


def after(array, *deps):
    return pl.pallas_call(
        nothing,
        out_shape=jax.ShapeDtypeStruct(array.shape, array.dtype),
        in_specs=[ANY] * (1 + len(deps)),
        out_specs=ANY,
        input_output_aliases={0: 0},
    )(array, *deps)


def groups(outer):
    sets = []
    for xh in range(2):
        for core in range(2):
            for xl in range(2):
                for other in range(4):
                    along_z = (core == 0) == outer
                    sets.append(
                        [
                            ravel((xh, core, i, xl, other) if along_z else (xh, core, other, xl, i))
                            for i in range(4)
                        ]
                    )
    return sets


OUTER = groups(True)
INNER = groups(False)
PLANE = [
    [ravel((xh, core, z, xl, y)) for z in range(4) for y in range(4)]
    for xh in range(2)
    for core in range(2)
    for xl in range(2)
]


def pin(*arrays):
    return [pltpu.with_memory_space_constraint(array, pltpu.HBM) for array in arrays]


def slot_table(sign, core, absolute=False):
    z, xl, y = (lax.axis_index(n) for n in ("z", "xl", "y"))
    inner = jnp.where(core == 0, y, z)
    outer = jnp.where(core == 0, z, y)
    dq = jnp.arange(4, dtype=jnp.int32)[:, None, None]
    dp = jnp.arange(4, dtype=jnp.int32)[None, :, None]
    dx = jnp.arange(2, dtype=jnp.int32)[None, None, :]
    q = dq + 0 * outer if absolute and sign > 0 else (outer + sign * dq + 4) % 4
    if sign < 0:
        p = dp + 0 * inner if absolute else (inner - dp + 4) % 4
        x = (xl + dx) % 2
    else:
        p = dp
        x = dx
    owner = jnp.where(core == 0, q * 8 + x * 4 + p, p * 8 + x * 4 + q)
    return owner.astype(jnp.int32).reshape(32)


SLOTS = [(dq, dp, dx) for dq in range(4) for dp in range(4) for dx in range(2)]


def run_all(copies):
    for copy in copies:
        copy.start()
    for copy in copies:
        copy.wait()


def pieces_of(srcs):
    if len(srcs) == 1:
        return [srcs[0].at[dq] for dq in range(4)]
    return srcs


def assemble_kernel(specs, n_dep, table, *refs):
    srcs, outs, sem = refs[:4], refs[4 + n_dep : -1], refs[-1]
    copies = []
    for n, (dq, dp, dx) in enumerate(SLOTS):
        f = table[n]
        for m, (begin, count, rows_first) in enumerate(specs):
            src = srcs[dq].at[dp, dx, pl.ds(begin, count)]
            dst = outs[m].at[f] if rows_first else outs[m].at[:, f]
            copies.append(pltpu.make_async_copy(src, dst, sem.at[n, m]))
    run_all(copies)


def assemble(specs, table, pieces, deps):
    shapes = [
        pltpu.HBM((32, count, ROWS, UNIT) if rows_first else (count, 32, ROWS, UNIT), BF)
        for _, count, rows_first in specs
    ]
    outs = pl.pallas_call(
        functools.partial(assemble_kernel, specs, len(deps)),
        out_shape=shapes,
        in_specs=[SMEM] + [ANY] * (4 + len(deps)),
        out_specs=[VMEM] * len(shapes),
        scratch_shapes=[pltpu.SemaphoreType.DMA((32, len(shapes)))],
        compiler_params=ROOMY,
        cost_estimate=LIGHT,
    )(table, *pieces, *deps)
    return [
        out.reshape(32 * count * ROWS, UNIT) if rows_first else out.reshape(count, 32 * ROWS, UNIT)
        for out, (_, count, rows_first) in zip(outs, specs)
    ]


def window(f):
    return (f * 96 // 128) * 128, f * 96 % 128


def assemble_first_kernel(n_dep, table, *refs):
    srcs, (out, rows_ref, fins_ref, vun, fbuf, sem) = refs[:4], refs[4 + n_dep :]
    copies = []
    for n, (dq, dp, dx) in enumerate(SLOTS):
        src = srcs[dq].at[dp, dx]
        f = table[n]
        copies.append(pltpu.make_async_copy(src.at[3], vun.at[f], sem.at[n, 0]))
        copies.append(pltpu.make_async_copy(src.at[pl.ds(0, 3)], out.at[:, f], sem.at[n, 1]))
    run_all(copies)
    vectors = vun[...].astype(F32)
    rows_ref[...] = vectors[:, :, :128].reshape(32 * ROWS, 128).T[:32]
    fbuf[...] = jnp.zeros(fbuf.shape, F32)
    for f in range(32):
        base, off = window(f)
        piece = jnp.concatenate([vectors[f, :8, 128:256], jnp.zeros((8, 128), F32)], 1)
        if off:
            piece = pltpu.roll(piece, off, 1)
        fbuf[:, base : base + 256] += piece
    fins_ref[...] = fbuf[:, : fins_ref.shape[1]]


def assemble_first(table, pieces, deps):
    return pl.pallas_call(
        functools.partial(assemble_first_kernel, len(deps)),
        out_shape=[
            pltpu.HBM((3, 32, ROWS, UNIT), BF),
            pltpu.HBM((32, 32 * ROWS), F32),
            pltpu.HBM((8, 128 * ROWS), F32),
        ],
        in_specs=[SMEM] + [ANY] * (4 + len(deps)),
        out_specs=[VMEM] * 3,
        scratch_shapes=[
            pltpu.VMEM((32, ROWS, UNIT), BF),
            pltpu.VMEM((8, 128 * ROWS + 128), F32),
            pltpu.SemaphoreType.DMA((32, 2)),
        ],
        compiler_params=ROOMY,
        cost_estimate=LIGHT,
    )(table, *pieces, *deps)


def assemble_both_kernel(begin, core, table, table_o, *refs):
    srcs, (wide, outs, sem) = refs[:8], refs[-3:]
    copies = []
    for side, at, tab in ((0, core[0], table), (1, 1 - core[0], table_o)):
        for n, (dq, dp, dx) in enumerate(SLOTS):
            src = srcs[4 * side + dq].at[dp, dx]
            f = tab[n]
            copies.append(
                pltpu.make_async_copy(src.at[pl.ds(begin, 5)], wide.at[at, :, f], sem.at[n, side, 0])
            )
            copies.append(
                pltpu.make_async_copy(
                    src.at[pl.ds(begin + 5, 4)], outs.at[at, f], sem.at[n, side, 1]
                )
            )
    run_all(copies)


def assemble_both(begin, core, tables, pieces, others, deps):
    wide, outs = pl.pallas_call(
        functools.partial(assemble_both_kernel, begin),
        out_shape=[
            pltpu.HBM((2, 5, 32, ROWS, UNIT), BF),
            pltpu.HBM((2, 32, 4, ROWS, UNIT), BF),
        ],
        in_specs=[SMEM] * (1 + len(tables)) + [ANY] * (2 * len(pieces) + len(deps)),
        out_specs=[VMEM] * 2,
        scratch_shapes=[pltpu.SemaphoreType.DMA((32, 2, 5))],
        compiler_params=ROOMY,
        cost_estimate=LIGHT,
    )(core, *tables, *pieces, *others, *deps)
    return wide.reshape(2, 5, 32 * ROWS, UNIT), outs.reshape(2, 128 * ROWS, UNIT)


def prep_kernel(core, *refs):
    vecs, (fin, qkv, proj, fc_in, fc_out, u1, u2, u3, vbuf, ubuf) = refs[:8], refs[8:]
    at = pl.multiple_of(core[0] * UNIT, 128)
    wide = pl.multiple_of(core[0] * 4 * UNIT, 128)
    for l in range(2):
        units = [qkv[l, :, pl.ds(at + 2 * j * UNIT, UNIT)] for j in range(3)]
        units.append(proj[l, :, pl.ds(at, UNIT)])
        units += [fc_in[l, :, pl.ds(wide + j * UNIT, UNIT)] for j in range(4)]
        rows = fc_out[l, :, pl.ds(at, UNIT)].astype(F32)
        units += [rows[j * ROWS : (j + 1) * ROWS].astype(BF) for j in range(4)]
        for j, unit in enumerate(units):
            if l == 0:
                if j < 3:
                    u1[j] = unit
                else:
                    u2[j - 3] = unit
            else:
                u3[j] = unit
    vbuf[...] = jnp.zeros(vbuf.shape, F32)
    for j, vec in enumerate(vecs):
        value = vec[...].astype(F32)
        for l in range(2):
            vbuf[l * 12 + j : l * 12 + j + 1, :ROWS] = value[l : l + 1]
    ubuf[...] = jnp.zeros(ubuf.shape, F32)
    ubuf[:, :128] = vbuf[...].T[:ROWS]
    ubuf[0:2, 128:224] = fin[...].astype(F32)
    u1[3] = ubuf[...].astype(BF)


def prep(core, arrays):
    return pl.pallas_call(
        prep_kernel,
        out_shape=[pltpu.HBM((count, ROWS, UNIT), BF) for count in (4, 9, 12)],
        in_specs=[SMEM] + [VMEM] * 13,
        out_specs=[VMEM] * 3,
        scratch_shapes=[pltpu.VMEM((128, 128), F32), pltpu.VMEM((ROWS, UNIT), F32)],
        compiler_params=ROOMY,
        cost_estimate=LIGHT,
    )(core, *arrays)


def inner_of(pair, got, units=slice(None)):
    return jnp.stack([part[:, units] for part in [pair] + got])


def three_inner(pair):
    return [to_inner(pair, d) for d in (1, 2, 3)]


def three_outer(block):
    return [to_outer(block, d) for d in (1, 2, 3)]


def send_outer(blocks):
    return [blocks[0]] + [to_outer(blocks[d], d) for d in (1, 2, 3)]


def take_sets(sizes, refs):
    sets = []
    for size in sizes:
        sets.append(refs[:size])
        refs = refs[size:]
    return sets


def sum_outer_kernel(n_set, n_dep, place_at, *refs):
    sets, outs = take_sets(n_set, refs), refs[sum(n_set) + n_dep :]
    for d, out in enumerate(outs):
        at = lax.rem(place_at[0] + d, 4)
        begin = 0
        for parts in sets:
            count = parts[0].shape[2]
            for x in range(2):
                total = parts[0][at, x].astype(F32)
                for part in parts[1:]:
                    total = total + part[at, x].astype(F32)
                out[x, begin : begin + count] = total.astype(BF)
            begin += count


def sum_outer(place_at, sets, deps=()):
    flat = [part for parts in sets for part in pin(parts[0]) + list(parts[1:])]
    count = sum(parts[0].shape[2] for parts in sets)
    return pl.pallas_call(
        functools.partial(sum_outer_kernel, [len(s) for s in sets], len(deps)),
        out_shape=[pltpu.HBM((2, count, ROWS, UNIT), BF)] * 4,
        in_specs=[SMEM] + [VMEM] * len(flat) + [ANY] * len(deps),
        out_specs=[VMEM] * 4,
        compiler_params=ROOMY,
        cost_estimate=LIGHT,
    )(place_at, *flat, *deps)


def sum_inner_kernel(n_set, n_dep, xl, *refs):
    sets, outs = take_sets(n_set, refs), refs[sum(n_set) + n_dep :]
    for j, out in enumerate(outs):
        at = xl[0] if j == 0 else 1 - xl[0]
        begin = 0
        for parts in sets:
            count = parts[0].shape[1]
            total = parts[0][at].astype(F32)
            for part in parts[1:]:
                total = total + part[at].astype(F32)
            out[begin : begin + count] = total.astype(BF)
            begin += count


def sum_inner(xl, sets, deps=()):
    flat = [part for parts in sets for part in pin(parts[0]) + list(parts[1:])]
    count = sum(parts[0].shape[1] for parts in sets)
    return pl.pallas_call(
        functools.partial(sum_inner_kernel, [len(s) for s in sets], len(deps)),
        out_shape=[pltpu.HBM((count, ROWS, UNIT), BF)] * 2,
        in_specs=[SMEM] + [VMEM] * len(flat) + [ANY] * len(deps),
        out_specs=[VMEM] * 2,
        compiler_params=ROOMY,
        cost_estimate=LIGHT,
    )(xl, *flat, *deps)


def add_all(*parts):
    total = parts[0].astype(F32)
    for part in parts[1:]:
        total = total + part.astype(F32)
    return total.astype(BF)


def norm_parts(values):
    centred = values - jnp.mean(values, -1, keepdims=True)
    scale = lax.rsqrt(jnp.mean(centred * centred, -1, keepdims=True) + 1e-06)
    return centred * scale, scale


def layer_norm(values, gain, bias):
    return norm_parts(values)[0] * gain + bias


def norm_back(values, gain, grad):
    n, scale = norm_parts(values)
    dg = grad * gain
    out = scale * (
        dg - jnp.mean(dg, -1, keepdims=True) - n * jnp.mean(dg * n, -1, keepdims=True)
    )
    return out, jnp.sum(grad * n, 0, keepdims=True), jnp.sum(grad, 0, keepdims=True)


def fdot(a, b, ca=1, cb=0):
    return lax.dot_general(a, b, (((ca,), (cb,)), ((), ())), preferred_element_type=F32)


def lanes(rows):
    return lax.broadcasted_iota(jnp.int32, (rows, 128), 1)


def place(lane, base, columns):
    out = jnp.zeros(lane.shape, F32)
    for j, column in enumerate(columns):
        out = jnp.where(lane == base + j, column, out)
    return out


def load_qkv(units, wbuf, sem):
    return [
        pltpu.make_async_copy(units.at[j], wbuf.at[:, pl.ds(j * UNIT, UNIT)], sem.at[j])
        for j in range(3)
    ]


def three(column):
    hi = column.astype(BF).astype(F32)
    mid = (column - hi).astype(BF).astype(F32)
    return [hi, mid, column - hi - mid]


def attn_fwd_kernel(raw, row, n_dep, core, x0, x1, x2, x3, units, vec, idc, *rest):
    rest = rest[n_dep:]
    a_ref, q_ref, k_ref, v_ref, lse_ref, o32_ref, own_ref, oth_ref, wbuf, sem = rest
    copies = load_qkv(units, wbuf, sem)
    for copy in copies:
        copy.start()
    tok = x0.shape[0]
    for j, x in enumerate((x0, x1, x2, x3)):
        if raw:
            a = layer_norm(x[...].astype(F32), vec[row : row + 1, :], vec[row + 1 : row + 2, :])
            a_ref[j * tok : (j + 1) * tok, :] = a.astype(BF)
        else:
            a_ref[j * tok : (j + 1) * tok, :] = x[...]
    start = pl.multiple_of(core[0] * UNIT, 128)
    qb = vec[row + 2 : row + 3, pl.ds(start, UNIT)]
    vb = vec[row + 3 : row + 4, pl.ds(start, UNIT)]
    for copy in copies:
        copy.wait()
    k_ref[...] = fdot(a_ref[...], wbuf[:, UNIT : 2 * UNIT]).astype(BF)
    v_ref[...] = (fdot(a_ref[...], wbuf[:, 2 * UNIT :]) + vb).astype(BF)
    q_ref[...] = (fdot(a_ref[: 2 * tok, :], wbuf[:, :UNIT]) + qb).astype(BF)
    ids = idc[...]
    lane_k = lanes(4 * tok)
    lane_q = lanes(tok)
    lse_all = [jnp.zeros((tok, 128), F32) for _ in range(2)]
    for t in range(3):
        cols = slice(t * 128, (t + 1) * 128)
        tiles = [[], []]
        for hh in range(2):
            base = 64 * (1 - hh)
            sel_k = (lane_k < 64) == (hh == 0)
            sel_q = (lane_q < 64) == (hh == 0)
            kk = jnp.where(
                sel_k, k_ref[:, cols].astype(F32), place(lane_k, base, [-1e30 * (1 - ids), -1e30 * ids])
            ).astype(BF)
            vv = jnp.where(sel_k, v_ref[:, cols].astype(F32), 1.0).astype(BF)
            for b in range(2):
                rows = slice(b * tok, (b + 1) * tok)
                idq = ids[rows, :]
                qq = jnp.where(
                    sel_q,
                    q_ref[rows, cols].astype(F32) * HD**-0.5,
                    place(lane_q, base, [idq, 1 - idq]),
                ).astype(BF)
                s = fdot(qq, kk, 1, 1)
                peak = jnp.max(s, -1, keepdims=True)
                e = jnp.exp(s - peak).astype(BF)
                o = fdot(e, vv)
                total = o[:, base : base + 1]
                lse = peak + jnp.log(total)
                lse_all[b] = jnp.where(lane_q == 2 * t + hh, lse, lse_all[b])
                tiles[b].append(o / total)
        for b, out in enumerate((own_ref, oth_ref)):
            o = jnp.where(lane_q < 64, tiles[b][0], tiles[b][1])
            o32_ref[b * tok : (b + 1) * tok, cols] = o
            out[:, cols] = o.astype(BF)
    for b in range(2):
        lse_ref[b * tok : (b + 1) * tok, :] = lse_all[b]


def attn_fwd(raw, row, core, parts, units, vec, idc, deps=()):
    tok = parts[0].shape[0]
    width = parts[0].shape[1]
    sds = pltpu.HBM
    shapes = [
        sds((4 * tok, width), BF),
        sds((2 * tok, UNIT), BF),
        sds((4 * tok, UNIT), BF),
        sds((4 * tok, UNIT), BF),
        sds((2 * tok, 128), F32),
        sds((2 * tok, UNIT), F32),
        sds((tok, UNIT), BF),
        sds((tok, UNIT), BF),
    ]
    scratch = [pltpu.VMEM((width, 3 * UNIT), BF), pltpu.SemaphoreType.DMA((3,))]
    return pl.pallas_call(
        functools.partial(attn_fwd_kernel, raw, row, len(deps)),
        out_shape=shapes,
        in_specs=[SMEM] + [VMEM] * 4 + [ANY] + [VMEM] * 2 + [ANY] * len(deps),
        out_specs=[VMEM] * len(shapes),
        scratch_shapes=scratch,
        compiler_params=ROOMY,
        cost_estimate=LIGHT,
    )(core, *pin(parts[0]), *parts[1:], *pin(units, vec), idc, *deps)


def load_mlp(core, parts, pbuf, ibuf, obuf, sem):
    proj, inner, last = [], [], []
    for side in range(2):
        if len(parts) == 2:
            wide, outs, place_at = parts[0].at[side], parts[1].at[side], side
        else:
            wide, outs = parts[2 * side : 2 * side + 2]
            place_at = core[0] if side == 0 else 1 - core[0]

        def cols(at):
            return pl.ds(at if isinstance(at, int) else pl.multiple_of(at, 128), UNIT)

        proj.append(
            pltpu.make_async_copy(wide.at[0], pbuf.at[:, cols(place_at * UNIT)], sem.at[side, 0])
        )
        for j in range(4):
            at = cols((place_at * 4 + j) * UNIT)
            inner.append(
                pltpu.make_async_copy(wide.at[1 + j], ibuf.at[:, at], sem.at[side, 1 + j])
            )
        last.append(pltpu.make_async_copy(outs, obuf.at[:, cols(place_at * UNIT)], sem.at[side, 5]))
    return proj, inner, last


def wait_all(copies):
    for copy in copies:
        copy.wait()


def mlp_fwd_kernel(row, last, n_part, core, x, o_own, o_oth, vec, fin, *rest):
    parts, outs = rest[:n_part], rest[n_part:-5]
    pbuf, ibuf, obuf, full, sem = rest[-5:]
    m_ref, pack, d_ref, y_ref = outs[:4]
    proj, inner, outer = load_mlp(core, parts, pbuf, ibuf, obuf, sem)
    for copy in proj + inner + outer:
        copy.start()
    width = x.shape[1]
    here = pl.multiple_of(core[0] * UNIT, 128)
    there = pl.multiple_of((1 - core[0]) * UNIT, 128)
    full[:, pl.ds(here, UNIT)] = o_own[...]
    full[:, pl.ds(there, UNIT)] = o_oth[...]
    pack[:, 5 * width :] = full[...]
    wait_all(proj)
    m = x[...].astype(F32) + (fdot(full[...], pbuf[...]) + vec[row + 4 : row + 5, :])
    m_ref[...] = m
    c = layer_norm(m, vec[row + 5 : row + 6, :], vec[row + 6 : row + 7, :]).astype(BF)
    pack[:, :width] = c
    wait_all(inner)
    total = None
    for j in range(4):
        cols = slice(j * width, (j + 1) * width)
        u = fdot(c, ibuf[:, cols]) + fin[row // 12 : row // 12 + 1, cols]
        cdf = 0.5 + 0.5 * lax.erf(u * 0.5**0.5)
        z = (u * cdf).astype(BF)
        pack[:, (j + 1) * width : (j + 2) * width] = z
        d_ref[:, cols] = (cdf + u * (jnp.exp(-0.5 * u * u) * (0.5 / jnp.pi) ** 0.5)).astype(d_ref.dtype)
        if j == 0:
            wait_all(outer)
        part = fdot(z, obuf[cols, :])
        total = part if total is None else total + part
    y = m + (total + vec[row + 7 : row + 8, :])
    y_ref[...] = y.astype(y_ref.dtype)
    if not last:
        a = layer_norm(y, vec[row + 12 : row + 13, :], vec[row + 13 : row + 14, :])
        outs[4][...] = a.astype(BF)


def mlp_scratch(width):
    return [
        pltpu.VMEM((width, width), BF),
        pltpu.VMEM((width, 4 * width), BF),
        pltpu.VMEM((4 * width, width), BF),
        pltpu.VMEM((8, 128), F32),
        pltpu.SemaphoreType.DMA((2, 6)),
    ]


def mlp_fwd(row, last, core, x, o_own, o_oth, vec, fin, weights):
    tok, width = x.shape
    sds = pltpu.HBM
    shapes = [
        sds((tok, width), F32),
        sds((tok, 6 * width), BF),
        sds((tok, 4 * width), F32),
        sds((tok, width), BF if last else F32),
    ]
    if not last:
        shapes.append(sds((tok, width), BF))
    scratch = mlp_scratch(width)
    scratch[3] = pltpu.VMEM((tok, width), BF)
    return pl.pallas_call(
        functools.partial(mlp_fwd_kernel, row, last, len(weights)),
        out_shape=shapes,
        in_specs=[SMEM] + [VMEM] * 5 + [ANY] * len(weights),
        out_specs=[VMEM] * len(shapes),
        scratch_shapes=scratch,
        compiler_params=ROOMY,
        cost_estimate=LIGHT,
    )(core, *pin(x, o_own), o_oth, *pin(vec, fin, *weights[:2]), *weights[2:])


def norm_back_kernel(row, vec, x, gmid, da, near, far):
    grad = da[...] + near[: da.shape[0], :].astype(F32) + far[...].astype(F32)
    dx, gain_g, bias_g = norm_back(x[...].astype(F32), vec[row : row + 1, :], grad)
    return gmid[...] + dx, gain_g, bias_g


def mlp_bwd_kernel(row, first, n_part, n_dep, core, vec, m_ref, d_ref, *rest):
    n_in = 1 if first else 5
    ins, parts, rest = rest[:n_in], rest[n_in : n_in + n_part], rest[n_in + n_part + n_dep :]
    pbuf, ibuf, obuf, full, sem = rest[-5:]
    gmid_ref, own, oth, rows_ref, fin_ref = rest[:-5]
    proj, inner, outer = load_mlp(core, parts, pbuf, ibuf, obuf, sem)
    for copy in outer + inner + proj:
        copy.start()
    width = m_ref.shape[1]
    half = width // 2

    def split(value, at):
        full[:, :width] = value
        here = pl.multiple_of(core[0] * half, 128)
        there = pl.multiple_of((1 - core[0]) * half, 128)
        own[:, at : at + half] = full[:, pl.ds(here, half)]
        oth[:, at : at + half] = full[:, pl.ds(there, half)]

    rows_ref[...] = jnp.zeros(rows_ref.shape, F32)
    if first:
        gx = ins[0][...].astype(F32)
    else:
        gx, gain_g, bias_g = norm_back_kernel(row + 12, vec, *ins)
        rows_ref[8:9, :] = gain_g
        rows_ref[9:10, :] = bias_g
    gm = gx.astype(BF)
    rows_ref[7:8, :] = jnp.sum(gm.astype(F32), 0, keepdims=True)
    split(gm, 2 * width)
    wait_all(outer)
    total = None
    for j in range(4):
        cols = slice(j * width, (j + 1) * width)
        dz = fdot(gm, obuf[cols, :], 1, 1)
        gu = (d_ref[:, cols].astype(F32) * dz).astype(BF)
        full[:, cols] = gu
        fin_ref[:, cols] = jnp.sum(gu.astype(F32), 0, keepdims=True)
        if j == 0:
            wait_all(inner)
        part = fdot(gu, ibuf[:, cols], 1, 1)
        total = part if total is None else total + part
    own[:, : 2 * width] = full[:, pl.ds(pl.multiple_of(core[0] * 2 * width, 128), 2 * width)]
    oth[:, : 2 * width] = full[:, pl.ds(pl.multiple_of((1 - core[0]) * 2 * width, 128), 2 * width)]
    dm, gain_g, bias_g = norm_back(m_ref[...], vec[row + 5 : row + 6, :], total)
    rows_ref[5:6, :] = gain_g
    rows_ref[6:7, :] = bias_g
    gmid = gx + dm
    gmid_ref[...] = gmid
    ga = gmid.astype(BF)
    rows_ref[4:5, :] = jnp.sum(ga.astype(F32), 0, keepdims=True)
    split(ga, 2 * width + half)
    wait_all(proj)
    split(fdot(ga, pbuf[...], 1, 1).astype(BF), 3 * width)


def mlp_bwd(row, first, core, vec, m, d, ins, weights, deps):
    tok, width = m.shape
    sds = pltpu.HBM
    shapes = (
        [sds((tok, width), F32)]
        + [sds((tok, 7 * width // 2), BF)] * 2
        + [sds((16, width), F32), sds((1, 4 * width), F32)]
    )
    scratch = mlp_scratch(width)
    scratch[3] = pltpu.VMEM((tok, 4 * width), BF)
    return pl.pallas_call(
        functools.partial(mlp_bwd_kernel, row, first, len(weights), len(deps)),
        out_shape=shapes,
        in_specs=[SMEM] + [VMEM] * (3 + len(ins)) + [ANY] * (len(weights) + len(deps)),
        out_specs=[VMEM] * len(shapes),
        scratch_shapes=scratch,
        compiler_params=ROOMY,
        cost_estimate=LIGHT,
    )(core, *pin(vec, m, d, *ins[:3]), *ins[3:], *pin(*weights[:2]), *weights[2:], *deps)


def last_norm_kernel(row, vec, x, gmid, da, near, far, gx_ref):
    gx_ref[...] = norm_back_kernel(row, vec, x, gmid, da, near, far)[0]


def last_norm(row, vec, ins):
    return pl.pallas_call(
        functools.partial(last_norm_kernel, row),
        out_shape=pltpu.HBM(ins[1].shape, F32),
        in_specs=[VMEM] * 6,
        out_specs=VMEM,
        compiler_params=ROOMY,
        cost_estimate=LIGHT,
    )(*pin(vec, *ins[:3]), *ins[3:])


def attn_bwd_kernel(row, n_raw, n_dep, q_ref, k_ref, v_ref, lse_ref, o32_ref, idc, *rest):
    raw, rest = rest[:n_raw], rest[n_raw:]
    (go_own, go_oth, units), rest = rest[:3], rest[3 + n_dep :]
    (
        gq_ref,
        gk_ref,
        gv_ref,
        da_own,
        da_keep,
        da_send,
        sums,
        rows_ref,
        go_ref,
        wbuf,
        sem,
    ) = rest
    tok = go_own.shape[0]
    width = units.shape[1]
    at = pl.ds(3 * width, UNIT)
    first = [
        pltpu.make_async_copy(go_own.at[:, at], go_ref.at[pl.ds(0, tok)], sem.at[3]),
        pltpu.make_async_copy(go_oth.at[:, at], go_ref.at[pl.ds(tok, tok)], sem.at[4]),
    ]
    copies = load_qkv(units, wbuf, sem)
    for copy in first + copies:
        copy.start()
    wait_all(first)
    ids = idc[...]
    near = 2 * tok
    lane_q = lanes(near)
    lane_k = lanes(near)
    for t in range(3):
        cols = slice(t * 128, (t + 1) * 128)
        gq_tile = []
        gk_tile = [[], []]
        gv_tile = [[], []]
        for hh in range(2):
            base = 64 * (1 - hh)
            h = 2 * t + hh
            sel = (lane_q < 64) == (hh == 0)
            go32 = go_ref[:, cols].astype(F32)
            inner = jnp.sum(jnp.where(sel, go32 * o32_ref[:, cols], 0.0), -1, keepdims=True)
            lse = lse_ref[:, h : h + 1]
            idq = ids[:near, :]
            qq = jnp.where(
                sel,
                q_ref[:, cols].astype(F32) * HD**-0.5,
                place(lane_q, base, [idq, 1 - idq] + three(-lse)),
            ).astype(BF)
            gg = jnp.where(sel, go32, place(lane_q, base, three(-inner))).astype(BF)
            gq = None
            for b in range(2):
                rows = slice(b * near, (b + 1) * near)
                idk = ids[rows, :]
                kk = jnp.where(
                    sel,
                    k_ref[rows, cols].astype(F32),
                    place(lane_k, base, [-1e30 * (1 - idk), -1e30 * idk, 1.0, 1.0, 1.0]),
                ).astype(BF)
                vv = jnp.where(
                    sel, v_ref[rows, cols].astype(F32), place(lane_k, base, [1.0, 1.0, 1.0])
                ).astype(BF)
                prob = jnp.exp(fdot(kk, qq, 1, 1))
                gs = (prob * fdot(vv, gg, 1, 1)).astype(BF)
                gv_tile[b].append(fdot(prob.astype(BF), go_ref[:, cols]))
                gk_tile[b].append(fdot(gs, q_ref[:, cols]))
                part = fdot(gs, k_ref[rows, cols], 0, 0)
                gq = part if gq is None else gq + part
            gq_tile.append(gq)
        left = lane_q < 64
        gq_ref[:, cols] = (jnp.where(left, gq_tile[0], gq_tile[1]) * HD**-0.5).astype(BF)
        for b in range(2):
            rows = slice(b * near, (b + 1) * near)
            gk_ref[rows, cols] = (jnp.where(left, *gk_tile[b]) * HD**-0.5).astype(BF)
            gv_ref[rows, cols] = jnp.where(left, *gv_tile[b]).astype(BF)
    for copy in copies:
        copy.wait()
    far = fdot(gk_ref[near:, :], wbuf[:, UNIT : 2 * UNIT], 1, 1) + fdot(
        gv_ref[near:, :], wbuf[:, 2 * UNIT :], 1, 1
    )
    da_keep[...] = far[:tok]
    da_send[tok:, :] = far[tok:].astype(BF)
    own = (
        fdot(gk_ref[:near, :], wbuf[:, UNIT : 2 * UNIT], 1, 1)
        + fdot(gv_ref[:near, :], wbuf[:, 2 * UNIT :], 1, 1)
        + fdot(gq_ref[...], wbuf[:, :UNIT], 1, 1)
    )
    da_own[...] = own[:tok]
    da_send[:tok, :] = own[tok:].astype(BF)
    rows_ref[...] = jnp.zeros(rows_ref.shape, F32)
    if raw:
        gain_g, bias_g = 0.0, 0.0
        for x, grad in zip(raw, (own[:tok], own[tok:], far[:tok], far[tok:])):
            n = norm_parts(x[...].astype(F32))[0]
            gain_g = gain_g + jnp.sum(grad * n, 0, keepdims=True)
            bias_g = bias_g + jnp.sum(grad, 0, keepdims=True)
        rows_ref[0:1, :] = gain_g
        rows_ref[1:2, :] = bias_g
    sums[...] = jnp.zeros(sums.shape, F32)
    sums[0:1, :] = jnp.sum(gq_ref[...].astype(F32), 0, keepdims=True)
    sums[1:2, :] = jnp.sum(gv_ref[...].astype(F32), 0, keepdims=True)


def attn_bwd(row, saved, raw, go_own, go_oth, idc, units, deps):
    tok = go_own.shape[0]
    width = units.shape[1]
    sds = pltpu.HBM
    shapes = [
        sds((2 * tok, UNIT), BF),
        sds((4 * tok, UNIT), BF),
        sds((4 * tok, UNIT), BF),
        sds((tok, width), F32),
        sds((tok, width), F32),
        sds((2 * tok, width), BF),
        sds((8, UNIT), F32),
        sds((8, width), F32),
    ]
    return pl.pallas_call(
        functools.partial(attn_bwd_kernel, row, len(raw), len(deps)),
        out_shape=shapes,
        in_specs=[VMEM] * (6 + len(raw)) + [ANY] * (3 + len(deps)),
        out_specs=[VMEM] * len(shapes),
        scratch_shapes=[
            pltpu.VMEM((2 * tok, UNIT), BF),
            pltpu.VMEM((width, 3 * UNIT), BF),
            pltpu.SemaphoreType.DMA((5,)),
        ],
        compiler_params=ROOMY,
        cost_estimate=LIGHT,
    )(*pin(*saved, idc, *raw, go_own), go_oth, *pin(units), *deps)


def deal(table, outs, buf, value, j, at):
    buf[at] = value.reshape(32, ROWS, UNIT)
    for dq, out in enumerate(outs):
        for p in range(4):
            for x in range(2):
                out[p, x, j] = buf[at, table[dq * 8 + p * 2 + x]].astype(BF)


def blocks_shape(count):
    return [pltpu.HBM((4, 2, count, ROWS, UNIT), BF)] * 4


def qkv_grad_kernel(with_vec, n_dep, table, core, a_ref, gq, gk, gv, *rest):
    n_vec = 7 if with_vec else 0
    vecs, rest = rest[:n_vec], rest[n_vec + n_dep :]
    outs, buf = rest[:4], rest[4]
    near = gq.shape[0]
    deal(table, outs, buf, fdot(a_ref[:near, :], gq[...], 0, 0), 0, 0)
    deal(table, outs, buf, fdot(a_ref[...], gk[...], 0, 0), 1, 1)
    deal(table, outs, buf, fdot(a_ref[...], gv[...], 0, 0), 2, 0)
    if with_vec:
        vbuf, tbuf, fbuf, wbuf = rest[5:9]
        rows0, rows1, sums0, sums1, fin0, fin1, norm0 = vecs
        vbuf[...] = jnp.zeros(vbuf.shape, F32)
        fbuf[...] = jnp.zeros(fbuf.shape, F32)
        cols = pl.ds(pl.multiple_of(core[0] * UNIT, 128), UNIT)
        vbuf[0:2, :] = norm0[0:2, :]
        vbuf[12:14, :] = rows0[8:10, :]
        for l, (rows, sums, fin) in enumerate(((rows0, sums0, fin0), (rows1, sums1, fin1))):
            vbuf[l * 12 + 2 : l * 12 + 3, cols] = sums[0:1, :]
            vbuf[l * 12 + 3 : l * 12 + 4, cols] = sums[1:2, :]
            vbuf[l * 12 + 4 : l * 12 + 8, :] = rows[4:8, :]
            fbuf[l : l + 1, : fin.shape[1]] = fin[...]
        tbuf[...] = vbuf[...].T.reshape(32, ROWS, 128)
        wbuf[...] = jnp.zeros(wbuf.shape, F32)
        for f in range(32):
            base, off = window(f)
            piece = fbuf[:, base : base + 256]
            if off:
                piece = pltpu.roll(piece, 256 - off, 1)
            wbuf[f, :8, :] = piece[:, :128]
        none = jnp.zeros((ROWS, 128), F32)
        for n, (dq, p, x) in enumerate(SLOTS):
            unit = jnp.concatenate([tbuf[table[n]], wbuf[table[n]], none], 1)
            outs[dq][p, x, 3] = unit.astype(BF)


def qkv_grad(table, core, a_all, gq, gk, gv, vecs, deps):
    count = 4 if vecs else 3
    scratch = [pltpu.VMEM((2, 32, ROWS, UNIT), F32)]
    if vecs:
        scratch += [
            pltpu.VMEM((128, a_all.shape[1]), F32),
            pltpu.VMEM((32, ROWS, 128), F32),
            pltpu.VMEM((8, 4 * a_all.shape[1] + 128), F32),
            pltpu.VMEM((32, ROWS, 128), F32),
        ]
    return pl.pallas_call(
        functools.partial(qkv_grad_kernel, bool(vecs), len(deps)),
        out_shape=blocks_shape(count),
        in_specs=[SMEM] * 2 + [VMEM] * (4 + len(vecs)) + [ANY] * len(deps),
        out_specs=[VMEM] * 4,
        scratch_shapes=scratch,
        compiler_params=ROOMY,
        cost_estimate=LIGHT,
    )(table, core, *pin(a_all, gq, gk, gv, *vecs), *deps)


def mlp_grad_kernel(joint, table, f0, f1, b0, b1, *rest):
    if joint:
        dests, (out, sem, buf, obuf) = rest[4:8], rest[8:]
    else:
        out, buf, obuf = rest
    outs = [out.at[q] for q in range(4)]
    width = f0.shape[1] // 6

    def both(lc, rc):
        return fdot(f0[:, lc], b0[:, rc], 0, 0) + fdot(f1[:, lc], b1[:, rc], 0, 0)

    def cols(begin, size):
        return slice(begin, begin + size)

    for j in range(4):
        deal(table, outs, buf, both(cols(0, width), cols(j * UNIT, UNIT)), j, j % 2)
    ga = cols(2 * width + UNIT, UNIT)
    deal(table, outs, buf, both(cols(5 * width, width), ga), 4, 0)
    for j in range(4):
        part = both(cols((j + 1) * width, width), cols(2 * width, UNIT))
        obuf[j * 8 : (j + 1) * 8] = part.reshape(8, 4, ROWS, UNIT)
    for n, (dq, p, x) in enumerate(SLOTS):
        outs[dq][p, x, pl.ds(5, 4)] = obuf[table[n]].astype(BF)
    if joint:
        spread_units(out, dests, sem, 0)


def mlp_grad(table, packs, joint=()):
    more = len(joint)
    blocks = (4, 4, 2, 9, ROWS, UNIT)
    scratch = [
        pltpu.VMEM((2, 32, ROWS, UNIT), F32),
        pltpu.VMEM((32, 4, ROWS, UNIT), F32),
    ]
    if more:
        scratch = [pltpu.VMEM(blocks, BF), pltpu.SemaphoreType.DMA((4,))] + scratch
    return pl.pallas_call(
        functools.partial(mlp_grad_kernel, more),
        out_shape=blocks_shape(12) if more else pltpu.HBM(blocks, BF),
        in_specs=[SMEM] + [VMEM] * 4 + [ANY] * more,
        out_specs=[ANY] * 4 if more else VMEM,
        input_output_aliases={5 + i: i for i in range(more)},
        scratch_shapes=scratch,
        compiler_params=ROOMY,
        cost_estimate=LIGHT,
    )(table, *pin(packs[0]), packs[1], *pin(packs[2]), packs[3], *pin(*joint))


def spread_units(out, dests, sem, begin):
    count = out.shape[3]
    run_all(
        [
            pltpu.make_async_copy(out.at[q], dest.at[:, :, pl.ds(begin, count)], sem.at[q])
            for q, dest in enumerate(dests)
        ]
    )


def qkv_grad_rest_kernel(n_dep, table, a_ref, gq, gk, gv, *rest):
    rest = rest[n_dep:]
    dests, (out, buf, sem) = rest[:4], rest[4:]
    outs = [out.at[q] for q in range(4)]
    near = gq.shape[0]
    deal(table, outs, buf, fdot(a_ref[:near, :], gq[...], 0, 0), 0, 0)
    deal(table, outs, buf, fdot(a_ref[...], gk[...], 0, 0), 1, 1)
    deal(table, outs, buf, fdot(a_ref[...], gv[...], 0, 0), 2, 0)
    spread_units(out, dests, sem, 9)


def qkv_grad_rest(table, a_all, gq, gk, gv, deps):
    return pl.pallas_call(
        functools.partial(qkv_grad_rest_kernel, len(deps)),
        out_shape=blocks_shape(12),
        in_specs=[SMEM] + [VMEM] * 4 + [ANY] * len(deps),
        out_specs=[ANY] * 4,
        scratch_shapes=[
            pltpu.VMEM((4, 4, 2, 3, ROWS, UNIT), BF),
            pltpu.VMEM((2, 32, ROWS, UNIT), F32),
            pltpu.SemaphoreType.DMA((4,)),
        ],
        compiler_params=ROOMY,
        cost_estimate=LIGHT,
    )(table, *pin(a_all, gq, gk, gv), *deps)


def reduce_along(blocks, sets):
    flat = blocks.reshape(-1, ROWS, UNIT)
    got = lax.psum_scatter(flat, AXES, scatter_dimension=0, axis_index_groups=sets, tiled=True)
    return got.reshape(blocks.shape[1:])


def gather_along(block, sets):
    flat = block.reshape(-1, ROWS, UNIT)
    got = lax.all_gather(flat, AXES, axis=0, axis_index_groups=sets, tiled=True)
    return got.reshape(4, *block.shape)


def finish_kernel(core, own0, oth0, own1, oth1, *rest):
    qkv, proj, fc_in, fc_out, fin = rest[:5]
    vecs, vbuf = rest[5:13], rest[13]
    first = core[0] == 0
    for l, (own, oth) in enumerate(((own0, oth0), (own1, oth1))):

        def put(out, rows, at, unit, own=own, oth=oth):
            lo = jnp.where(first, own[unit], oth[unit]).astype(F32)
            hi = jnp.where(first, oth[unit], own[unit]).astype(F32)
            out[l, rows, at[0] : at[0] + UNIT] = lo
            out[l, rows, at[1] : at[1] + UNIT] = hi

        every = slice(0, ROWS)
        for j in range(4):
            put(fc_in, every, (j * UNIT, (j + 4) * UNIT), j)
            put(fc_out, slice(j * ROWS, (j + 1) * ROWS), (0, UNIT), 5 + j)
        put(proj, every, (0, UNIT), 4)
        for j in range(3):
            at = 12 + j if l == 0 else 9 + j
            put(qkv, every, (2 * j * UNIT, (2 * j + 1) * UNIT), at, own0, oth0)
    both = own0[15].astype(F32) + oth0[15].astype(F32)
    fin[...] = both[0:2, 128:224]
    vbuf[...] = jnp.zeros(vbuf.shape, F32)
    vbuf[:ROWS, :] = both[:, :128]
    turned = vbuf[...].T
    for j, vec in enumerate(vecs):
        for l in range(2):
            vec[l : l + 1, :] = turned[l * 12 + j : l * 12 + j + 1, :ROWS]


def finish(core, parts):
    sds = jax.ShapeDtypeStruct
    width = 2 * UNIT
    return pl.pallas_call(
        finish_kernel,
        out_shape=[
            sds((2, ROWS, 3 * width), F32),
            sds((2, ROWS, width), F32),
            sds((2, ROWS, 4 * width), F32),
            sds((2, 4 * ROWS, width), F32),
            sds((2, 4 * ROWS), F32),
        ]
        + [sds((2, ROWS), F32)] * 8,
        in_specs=[SMEM] + [VMEM] * 4,
        out_specs=[VMEM] * 13,
        scratch_shapes=[pltpu.VMEM((128, 128), F32)],
        compiler_params=ROOMY,
        cost_estimate=LIGHT,
    )(core, *parts)


def body(
    tokens,
    image_ids,
    cotangent,
    attn_norm_gain,
    attn_norm_bias,
    qkv_weight,
    query_bias,
    value_bias,
    proj_weight,
    proj_bias,
    mlp_norm_gain,
    mlp_norm_bias,
    fc_in_weight,
    fc_in_bias,
    fc_out_weight,
    fc_out_bias,
):
    core, xh, xl = (lax.axis_index(n) for n in ("core", "xh", "xl"))
    width = tokens.shape[2]
    tok = tokens.shape[1]

    one = core.astype(jnp.int32).reshape(1)
    xl_one = xl.astype(jnp.int32).reshape(1)
    z, y = lax.axis_index("z"), lax.axis_index("y")
    inner_at = jnp.where(core == 0, y, z).astype(jnp.int32).reshape(1)
    table = slot_table(-1, core)
    table_o = slot_table(-1, 1 - core)
    table_out = slot_table(1, core)
    table_abs = slot_table(-1, core, True)
    table_sum = slot_table(1, core, True)

    def segment(dx, dc):
        return lax.dynamic_slice_in_dim(
            image_ids[0], (((xh + dx) % 2) * 2 + (core + dc) % 2) * tok, tok, 0
        )

    ids = jnp.concatenate([segment(0, 0), segment(0, 1), segment(1, 0), segment(1, 1)])
    idc = ids.astype(F32)[:, None]

    u1, u2, u3 = prep(
        one,
        pin(
            attn_norm_gain,
            attn_norm_bias,
            query_bias,
            value_bias,
            proj_bias,
            mlp_norm_gain,
            mlp_norm_bias,
            fc_out_bias,
            fc_in_bias,
            qkv_weight,
            proj_weight,
            fc_in_weight,
            fc_out_weight,
        ),
    )
    tokens_own = tokens[0]
    p1 = jnp.stack([u1, to_xl(u1)])
    p2 = jnp.stack([u2, to_xl(after(u2, p1))])
    tokens_far = to_xh(after(tokens_own, p1))
    share = [tokens_own, to_core(tokens_own), tokens_far, to_core(tokens_far)]
    s1 = three_inner(p1)
    inner1 = after(inner_of(p1, s1), p2, idc, tokens_far)
    pieces1 = [inner1] + three_outer(inner1)
    p2 = after(p2, *pieces1[1:])
    u3 = after(u3, inner1)
    p3 = jnp.stack([u3, to_xl(u3)])
    p3 = after(p3, *pieces1[1:])
    inner3 = gather_along(p3, INNER)
    s2 = three_inner(p2)
    qkv0, vec_rows, fins = assemble_first(table, pieces1, pin(p2, p3))
    qkv0 = qkv0.reshape(3, width, UNIT)
    fwd0 = attn_fwd(True, 0, one, share, qkv0, vec_rows, idc)
    o_own, o_oth = fwd0[6:]
    o_got = to_core(o_oth)
    inner2 = inner_of(p2, [after(part, o_own) for part in s2])
    pieces2 = [inner2] + [after(piece, o_got) for piece in three_outer(inner2)]
    others2 = [to_core(piece) for piece in pieces2]
    inner3 = after(after(inner3, o_own), *pieces2[1:])
    pieces3 = [inner3] + three_outer(inner3)
    full0 = assemble_both(0, one, [table, table_o], pieces2, others2, [o_got] + pin(inner3))
    m0, pack0, d0, x1, a1 = mlp_fwd(0, False, one, tokens_own, o_own, o_got, vec_rows, fins, full0)
    pack0_o = to_core(pack0)
    a1_far = to_xh(a1)
    share1 = [a1, to_core(a1), a1_far, to_core(a1_far)]
    pieces3 = [inner3] + [after(piece, x1) for piece in pieces3[1:]]
    qkv1, wide1, outs1 = assemble(
        [(0, 3, False), (3, 5, False), (8, 4, True)], table_abs, pieces3, share1[1:]
    )
    full1 = [wide1, outs1, to_core(wide1), to_core(outs1)]
    fwd1 = attn_fwd(False, 12, one, share1, qkv1, vec_rows, idc)
    o_own, o_oth = fwd1[6:]
    o_got = to_core(o_oth)
    others3 = [to_core(part) for part in pieces3]
    m1, pack1, d1, block_output = mlp_fwd(12, True, one, x1, o_own, o_got, vec_rows, fins, full1)
    pack1_o = to_core(pack1)

    gmid1, own1, oth1, rows1, fing1 = mlp_bwd(
        12, True, one, vec_rows, m1, d1, [cotangent[0]], full1, pin(block_output)
    )
    got1 = to_core(oth1)
    block_a = mlp_grad(table_sum, [pack1, pack1_o, own1, got1])
    sum_a = reduce_along(block_a, OUTER)
    gq, gk, gv, da, da_keep, da_send, sums1, _ = attn_bwd(
        12, fwd1[1:6], [], own1, got1, idc, qkv1, pin(block_a)
    )
    da_got = to_core(da_send)
    far_in = (da_keep + da_got[tok:].astype(F32)).astype(BF)
    far = to_xh(far_in)
    block_e = qkv_grad_rest(table_out, fwd1[0], gq, gk, gv, [far_in])

    gmid0, own0, oth0, rows0, fing0 = mlp_bwd(
        0, False, one, vec_rows, m0, d0, [x1, gmid1, da, da_got, far], full0, pin(block_e[0])
    )
    got0 = to_core(oth0)
    sum_a = after(sum_a, gmid0)
    mid_a = sum_a
    sum_a = reduce_along(sum_a, INNER)
    block_b = mlp_grad(table_out, [pack0, pack0_o, own0, got0], block_e)
    sent_b = send_outer(block_b)
    gq, gk, gv, da, da_keep, da_send, sums0, norm0 = attn_bwd(
        0, fwd0[1:6], share, own0, got0, idc, qkv0, pin(block_b[0], mid_a)
    )
    da_got = to_core(da_send)
    far = to_xh((da_keep + da_got[tok:].astype(F32)).astype(BF))

    vecs = [rows0, rows1, sums0, sums1, fing0, fing1, norm0]
    block_c = qkv_grad(table_out, one, fwd0[0], gq, gk, gv, vecs, [])
    sent_c = send_outer(block_c)
    gx = last_norm(0, vec_rows, [tokens_own, gmid0, da, da_got, far])
    mine_a, other_a = sum_inner(xl_one, [[sum_a]], pin(block_c[0]))
    part_a = add_all(mine_a, to_xl(other_a))
    part_a = add_all(part_a, to_xh(part_a))
    part_a_o = to_core(part_a)
    sum_bc = sum_outer(inner_at, [sent_b, sent_c], [far] + pin(other_a))
    sent_bc = [sum_bc[0]] + [to_inner(sum_bc[d], d) for d in (1, 2, 3)]
    mine_bc, other_bc = sum_inner(xl_one, [sent_bc], pin(gx))
    part_bc = add_all(mine_bc, to_xl(other_bc))
    part_bc = add_all(part_bc, to_xh(part_bc))
    done = finish(one, [part_bc, to_core(part_bc), part_a, part_a_o])
    qkv_g, proj_g, fc_in_g, fc_out_g, fin_g = done[:5]
    vec_g = done[5:]
    return (
        block_output[None],
        gx[None],
        vec_g[0],
        vec_g[1],
        qkv_g,
        vec_g[2],
        vec_g[3],
        proj_g,
        vec_g[4],
        vec_g[5],
        vec_g[6],
        fc_in_g,
        fin_g,
        fc_out_g,
        vec_g[7],
    )


def solution(mesh):
    fine = Mesh(mesh.devices.reshape(SIZES), AXES)
    row = P(None, FSDP)
    mat = P(None, FSDP, None)
    tok = P(FSDP, SEQ, None)
    return jax.shard_map(
        body,
        mesh=fine,
        in_specs=(
            tok,
            P(FSDP, None),
            tok,
            row,
            row,
            mat,
            row,
            row,
            mat,
            row,
            row,
            row,
            mat,
            row,
            mat,
            row,
        ),
        out_specs=(tok, tok, row, row, mat, row, row, mat, row, row, row, mat, row, mat, row),
        check_vma=False,
    )
```

```python
import functools

import jax
import jax.numpy as jnp
from jax import lax
from jax.experimental import pallas as pl
from jax.experimental.pallas import tpu as pltpu
from jax.sharding import Mesh
from jax.sharding import PartitionSpec as P

HD = 64
AXES = ("xh", "core", "z", "xl", "y")
SIZES = (2, 2, 4, 2, 4)
FSDP = ("z", "xl", "y")
SEQ = ("xh", "core")
UNIT = 384
ROWS = 24
BF = jnp.bfloat16
F32 = jnp.float32
ANY = pl.BlockSpec(memory_space=pl.ANY)
SMEM = pl.BlockSpec(memory_space=pltpu.SMEM)
VMEM = pl.BlockSpec(memory_space=pltpu.VMEM)
LIGHT = pl.CostEstimate(flops=10**6, bytes_accessed=10**5, transcendentals=0)
ROOMY = pltpu.CompilerParams(vmem_limit_bytes=48 * 2**20)


def ravel(coords):
    index = 0
    for size, coord in zip(SIZES, coords):
        index = index * size + coord % size
    return index


def all_coords():
    xh_n, core_n, z_n, xl_n, y_n = SIZES
    return [
        (xh, core, z, xl, y)
        for xh in range(xh_n)
        for core in range(core_n)
        for z in range(z_n)
        for xl in range(xl_n)
        for y in range(y_n)
    ]


def shift(array, move):
    pairs = [(ravel(c), ravel(move(*c))) for c in all_coords()]
    return lax.ppermute(array, AXES, pairs)


def to_core(array):
    return shift(array, lambda xh, core, z, xl, y: (xh, core + 1, z, xl, y))


def to_xh(array):
    return shift(array, lambda xh, core, z, xl, y: (xh + 1, core, z, xl, y))


def to_xl(array):
    return shift(array, lambda xh, core, z, xl, y: (xh, core, z, xl + 1, y))


def to_next_x(array, d):
    def move(xh, core, z, xl, y):
        x = (2 * xh + xl + d) % 4
        return (x // 2, core, z, x % 2, y)

    return shift(array, move)


def to_inner(array, d):
    return shift(
        array,
        lambda xh, core, z, xl, y: (xh, core, z, xl, y + d) if core == 0 else (xh, core, z + d, xl, y),
    )


def to_outer(array, d):
    return shift(
        array,
        lambda xh, core, z, xl, y: (xh, core, z + d, xl, y) if core == 0 else (xh, core, z, xl, y + d),
    )


def nothing(*refs):
    del refs


def after(array, *deps):
    return pl.pallas_call(
        nothing,
        out_shape=jax.ShapeDtypeStruct(array.shape, array.dtype),
        in_specs=[ANY] * (1 + len(deps)),
        out_specs=ANY,
        input_output_aliases={0: 0},
    )(array, *deps)


def groups(outer):
    sets = []
    for xh in range(2):
        for core in range(2):
            for xl in range(2):
                for other in range(4):
                    along_z = (core == 0) == outer
                    sets.append(
                        [
                            ravel((xh, core, i, xl, other) if along_z else (xh, core, other, xl, i))
                            for i in range(4)
                        ]
                    )
    return sets


OUTER = groups(True)
INNER = groups(False)
PLANE = [
    [ravel((xh, core, z, xl, y)) for z in range(4) for y in range(4)]
    for xh in range(2)
    for core in range(2)
    for xl in range(2)
]


def pin(*arrays):
    return [pltpu.with_memory_space_constraint(array, pltpu.HBM) for array in arrays]


def slot_table(sign, core, absolute=False):
    z, xl, y = (lax.axis_index(n) for n in ("z", "xl", "y"))
    inner = jnp.where(core == 0, y, z)
    outer = jnp.where(core == 0, z, y)
    dq = jnp.arange(4, dtype=jnp.int32)[:, None, None]
    dp = jnp.arange(4, dtype=jnp.int32)[None, :, None]
    dx = jnp.arange(2, dtype=jnp.int32)[None, None, :]
    q = dq + 0 * outer if absolute and sign > 0 else (outer + sign * dq + 4) % 4
    if sign < 0:
        p = dp + 0 * inner if absolute else (inner - dp + 4) % 4
        x = (xl + dx) % 2
    else:
        p = dp
        x = dx
    owner = jnp.where(core == 0, q * 8 + x * 4 + p, p * 8 + x * 4 + q)
    return owner.astype(jnp.int32).reshape(32)


SLOTS = [(dq, dp, dx) for dq in range(4) for dp in range(4) for dx in range(2)]


def run_all(copies):
    for copy in copies:
        copy.start()
    for copy in copies:
        copy.wait()


def pieces_of(srcs):
    if len(srcs) == 1:
        return [srcs[0].at[dq] for dq in range(4)]
    return srcs


def assemble_kernel(specs, n_dep, table, *refs):
    srcs, outs, sem = refs[:4], refs[4 + n_dep : -1], refs[-1]
    copies = []
    for n, (dq, dp, dx) in enumerate(SLOTS):
        f = table[n]
        for m, (begin, count, rows_first) in enumerate(specs):
            src = srcs[dq].at[dp, dx, pl.ds(begin, count)]
            dst = outs[m].at[f] if rows_first else outs[m].at[:, f]
            copies.append(pltpu.make_async_copy(src, dst, sem.at[n, m]))
    run_all(copies)


def assemble(specs, table, pieces, deps):
    shapes = [
        pltpu.HBM((32, count, ROWS, UNIT) if rows_first else (count, 32, ROWS, UNIT), BF)
        for _, count, rows_first in specs
    ]
    outs = pl.pallas_call(
        functools.partial(assemble_kernel, specs, len(deps)),
        out_shape=shapes,
        in_specs=[SMEM] + [ANY] * (4 + len(deps)),
        out_specs=[VMEM] * len(shapes),
        scratch_shapes=[pltpu.SemaphoreType.DMA((32, len(shapes)))],
        compiler_params=ROOMY,
        cost_estimate=LIGHT,
    )(table, *pieces, *deps)
    return [
        out.reshape(32 * count * ROWS, UNIT) if rows_first else out.reshape(count, 32 * ROWS, UNIT)
        for out, (_, count, rows_first) in zip(outs, specs)
    ]


def window(f):
    return (f * 96 // 128) * 128, f * 96 % 128


def assemble_first_kernel(n_dep, table, *refs):
    srcs, (out, rows_ref, fins_ref, vun, fbuf, sem) = refs[:4], refs[4 + n_dep :]
    copies = []
    for n, (dq, dp, dx) in enumerate(SLOTS):
        src = srcs[dq].at[dp, dx]
        f = table[n]
        copies.append(pltpu.make_async_copy(src.at[3], vun.at[f], sem.at[n, 0]))
        copies.append(pltpu.make_async_copy(src.at[pl.ds(0, 3)], out.at[:, f], sem.at[n, 1]))
    run_all(copies)
    vectors = vun[...].astype(F32)
    rows_ref[...] = vectors[:, :, :128].reshape(32 * ROWS, 128).T[:32]
    fbuf[...] = jnp.zeros(fbuf.shape, F32)
    for f in range(32):
        base, off = window(f)
        piece = jnp.concatenate([vectors[f, :8, 128:256], jnp.zeros((8, 128), F32)], 1)
        if off:
            piece = pltpu.roll(piece, off, 1)
        fbuf[:, base : base + 256] += piece
    fins_ref[...] = fbuf[:, : fins_ref.shape[1]]


def assemble_first(table, pieces, deps):
    return pl.pallas_call(
        functools.partial(assemble_first_kernel, len(deps)),
        out_shape=[
            pltpu.HBM((3, 32, ROWS, UNIT), BF),
            pltpu.HBM((32, 32 * ROWS), F32),
            pltpu.HBM((8, 128 * ROWS), F32),
        ],
        in_specs=[SMEM] + [ANY] * (4 + len(deps)),
        out_specs=[VMEM] * 3,
        scratch_shapes=[
            pltpu.VMEM((32, ROWS, UNIT), BF),
            pltpu.VMEM((8, 128 * ROWS + 128), F32),
            pltpu.SemaphoreType.DMA((32, 2)),
        ],
        compiler_params=ROOMY,
        cost_estimate=LIGHT,
    )(table, *pieces, *deps)


def assemble_both_kernel(begin, core, table, table_o, *refs):
    srcs, (wide, outs, sem) = refs[:8], refs[-3:]
    copies = []
    for side, at, tab in ((0, core[0], table), (1, 1 - core[0], table_o)):
        for n, (dq, dp, dx) in enumerate(SLOTS):
            src = srcs[4 * side + dq].at[dp, dx]
            f = tab[n]
            copies.append(
                pltpu.make_async_copy(src.at[pl.ds(begin, 5)], wide.at[at, :, f], sem.at[n, side, 0])
            )
            copies.append(
                pltpu.make_async_copy(
                    src.at[pl.ds(begin + 5, 4)], outs.at[at, f], sem.at[n, side, 1]
                )
            )
    run_all(copies)


def assemble_both(begin, core, tables, pieces, others, deps):
    wide, outs = pl.pallas_call(
        functools.partial(assemble_both_kernel, begin),
        out_shape=[
            pltpu.HBM((2, 5, 32, ROWS, UNIT), BF),
            pltpu.HBM((2, 32, 4, ROWS, UNIT), BF),
        ],
        in_specs=[SMEM] * (1 + len(tables)) + [ANY] * (2 * len(pieces) + len(deps)),
        out_specs=[VMEM] * 2,
        scratch_shapes=[pltpu.SemaphoreType.DMA((32, 2, 5))],
        compiler_params=ROOMY,
        cost_estimate=LIGHT,
    )(core, *tables, *pieces, *others, *deps)
    return wide.reshape(2, 5, 32 * ROWS, UNIT), outs.reshape(2, 128 * ROWS, UNIT)


def prep_kernel(core, *refs):
    vecs, (fin, qkv, proj, fc_in, fc_out, u1, u2, u3, vbuf, ubuf) = refs[:8], refs[8:]
    at = pl.multiple_of(core[0] * UNIT, 128)
    wide = pl.multiple_of(core[0] * 4 * UNIT, 128)
    for l in range(2):
        units = [qkv[l, :, pl.ds(at + 2 * j * UNIT, UNIT)] for j in range(3)]
        units.append(proj[l, :, pl.ds(at, UNIT)])
        units += [fc_in[l, :, pl.ds(wide + j * UNIT, UNIT)] for j in range(4)]
        rows = fc_out[l, :, pl.ds(at, UNIT)].astype(F32)
        units += [rows[j * ROWS : (j + 1) * ROWS].astype(BF) for j in range(4)]
        for j, unit in enumerate(units):
            if l == 0:
                if j < 3:
                    u1[j] = unit
                else:
                    u2[j - 3] = unit
            else:
                u3[j] = unit
    vbuf[...] = jnp.zeros(vbuf.shape, F32)
    for j, vec in enumerate(vecs):
        value = vec[...].astype(F32)
        for l in range(2):
            vbuf[l * 12 + j : l * 12 + j + 1, :ROWS] = value[l : l + 1]
    ubuf[...] = jnp.zeros(ubuf.shape, F32)
    ubuf[:, :128] = vbuf[...].T[:ROWS]
    ubuf[0:2, 128:224] = fin[...].astype(F32)
    u1[3] = ubuf[...].astype(BF)


def prep(core, arrays):
    return pl.pallas_call(
        prep_kernel,
        out_shape=[pltpu.HBM((count, ROWS, UNIT), BF) for count in (4, 9, 12)],
        in_specs=[SMEM] + [VMEM] * 13,
        out_specs=[VMEM] * 3,
        scratch_shapes=[pltpu.VMEM((128, 128), F32), pltpu.VMEM((ROWS, UNIT), F32)],
        compiler_params=ROOMY,
        cost_estimate=LIGHT,
    )(core, *arrays)


def inner_of(pair, got, units=slice(None)):
    return jnp.stack([part[:, units] for part in [pair] + got])


def three_inner(pair):
    return [to_inner(pair, d) for d in (1, 2, 3)]


def three_outer(block):
    return [to_outer(block, d) for d in (1, 2, 3)]


def send_outer(blocks):
    return [blocks[0]] + [to_outer(blocks[d], d) for d in (1, 2, 3)]


def take_sets(sizes, refs):
    sets = []
    for size in sizes:
        sets.append(refs[:size])
        refs = refs[size:]
    return sets


def sum_outer_kernel(n_set, n_dep, place_at, *refs):
    sets, outs = take_sets(n_set, refs), refs[sum(n_set) + n_dep :]
    for d, out in enumerate(outs):
        at = lax.rem(place_at[0] + d, 4)
        begin = 0
        for parts in sets:
            count = parts[0].shape[2]
            for x in range(2):
                total = parts[0][at, x].astype(F32)
                for part in parts[1:]:
                    total = total + part[at, x].astype(F32)
                out[x, begin : begin + count] = total.astype(BF)
            begin += count


def sum_outer(place_at, sets, deps=()):
    flat = [part for parts in sets for part in pin(parts[0]) + list(parts[1:])]
    count = sum(parts[0].shape[2] for parts in sets)
    return pl.pallas_call(
        functools.partial(sum_outer_kernel, [len(s) for s in sets], len(deps)),
        out_shape=[pltpu.HBM((2, count, ROWS, UNIT), BF)] * 4,
        in_specs=[SMEM] + [VMEM] * len(flat) + [ANY] * len(deps),
        out_specs=[VMEM] * 4,
        compiler_params=ROOMY,
        cost_estimate=LIGHT,
    )(place_at, *flat, *deps)


def sum_inner_kernel(n_set, n_dep, xl, *refs):
    sets, outs = take_sets(n_set, refs), refs[sum(n_set) + n_dep :]
    for j, out in enumerate(outs):
        at = xl[0] if j == 0 else 1 - xl[0]
        begin = 0
        for parts in sets:
            count = parts[0].shape[1]
            total = parts[0][at].astype(F32)
            for part in parts[1:]:
                total = total + part[at].astype(F32)
            out[begin : begin + count] = total.astype(BF)
            begin += count


def sum_inner(xl, sets, deps=()):
    flat = [part for parts in sets for part in pin(parts[0]) + list(parts[1:])]
    count = sum(parts[0].shape[1] for parts in sets)
    return pl.pallas_call(
        functools.partial(sum_inner_kernel, [len(s) for s in sets], len(deps)),
        out_shape=[pltpu.HBM((count, ROWS, UNIT), BF)] * 2,
        in_specs=[SMEM] + [VMEM] * len(flat) + [ANY] * len(deps),
        out_specs=[VMEM] * 2,
        compiler_params=ROOMY,
        cost_estimate=LIGHT,
    )(xl, *flat, *deps)


def add_all(*parts):
    total = parts[0].astype(F32)
    for part in parts[1:]:
        total = total + part.astype(F32)
    return total.astype(BF)


def norm_parts(values):
    centred = values - jnp.mean(values, -1, keepdims=True)
    scale = lax.rsqrt(jnp.mean(centred * centred, -1, keepdims=True) + 1e-06)
    return centred * scale, scale


def layer_norm(values, gain, bias):
    return norm_parts(values)[0] * gain + bias


def norm_back(values, gain, grad):
    n, scale = norm_parts(values)
    dg = grad * gain
    out = scale * (
        dg - jnp.mean(dg, -1, keepdims=True) - n * jnp.mean(dg * n, -1, keepdims=True)
    )
    return out, jnp.sum(grad * n, 0, keepdims=True), jnp.sum(grad, 0, keepdims=True)


def fdot(a, b, ca=1, cb=0):
    return lax.dot_general(a, b, (((ca,), (cb,)), ((), ())), preferred_element_type=F32)


def lanes(rows):
    return lax.broadcasted_iota(jnp.int32, (rows, 128), 1)


def place(lane, base, columns):
    out = jnp.zeros(lane.shape, F32)
    for j, column in enumerate(columns):
        out = jnp.where(lane == base + j, column, out)
    return out


def load_qkv(units, wbuf, sem):
    return [
        pltpu.make_async_copy(units.at[j], wbuf.at[:, pl.ds(j * UNIT, UNIT)], sem.at[j])
        for j in range(3)
    ]


def lane_mask(hh):
    lane = lax.broadcasted_iota(jnp.int32, (1, 128), 1)
    return jnp.where((lane < 64) == (hh == 0), 1.0, 0.0).astype(BF)


def three(column):
    hi = column.astype(BF).astype(F32)
    mid = (column - hi).astype(BF).astype(F32)
    return [hi, mid, column - hi - mid]


def attn_fwd_kernel(raw, row, n_dep, core, x0, x1, x2, x3, units, vec, idc, *rest):
    rest = rest[n_dep:]
    a_ref, q_ref, k_ref, v_ref, lse_ref, o32_ref, own_ref, oth_ref, wbuf, sem = rest
    copies = load_qkv(units, wbuf, sem)
    for copy in copies:
        copy.start()
    tok = x0.shape[0]
    for j, x in enumerate((x0, x1, x2, x3)):
        if raw:
            a = layer_norm(x[...].astype(F32), vec[row : row + 1, :], vec[row + 1 : row + 2, :])
            a_ref[j * tok : (j + 1) * tok, :] = a.astype(BF)
        else:
            a_ref[j * tok : (j + 1) * tok, :] = x[...]
    start = pl.multiple_of(core[0] * UNIT, 128)
    qb = vec[row + 2 : row + 3, pl.ds(start, UNIT)]
    vb = vec[row + 3 : row + 4, pl.ds(start, UNIT)]
    for copy in copies:
        copy.wait()
    k_ref[...] = fdot(a_ref[...], wbuf[:, UNIT : 2 * UNIT]).astype(BF)
    v_ref[...] = (fdot(a_ref[...], wbuf[:, 2 * UNIT :]) + vb).astype(BF)
    q_ref[...] = (fdot(a_ref[: 2 * tok, :], wbuf[:, :UNIT]) + qb).astype(BF)
    ids = idc[...]
    lane_k = lanes(4 * tok)
    lane_q = lanes(tok)
    masks = [lane_mask(hh) for hh in range(2)]
    feats = [
        place(lane_k, 64 * (1 - hh), [-1e30 * (1 - ids), -1e30 * ids]).astype(BF) for hh in range(2)
    ]
    own = ids[: 2 * tok, :]
    lane_2 = lanes(2 * tok)
    feats_q = [place(lane_2, 64 * (1 - hh), [own, 1 - own]).astype(BF) for hh in range(2)]
    lse_all = [jnp.zeros((tok, 128), F32) for _ in range(2)]
    items = [(t, hh, b) for t in range(3) for hh in range(2) for b in range(2)]

    def scores(item):
        t, hh, b = item
        cols = slice(t * 128, (t + 1) * 128)
        rows = slice(b * tok, (b + 1) * tok)
        kk = k_ref[:, cols] * masks[hh] + feats[hh]
        qq = q_ref[rows, cols] * (masks[hh] * BF(HD**-0.5)) + feats_q[hh][rows, :]
        return fdot(qq, kk, 1, 1)

    ahead = scores(items[0])
    tiles = {}
    for n, (t, hh, b) in enumerate(items):
        cols = slice(t * 128, (t + 1) * 128)
        s = ahead
        if n + 1 < len(items):
            ahead = scores(items[n + 1])
        base = 64 * (1 - hh)
        peak = jnp.max(s, -1, keepdims=True)
        e = jnp.exp(s - peak).astype(BF)
        o = fdot(e, v_ref[:, cols] * masks[hh] + masks[1 - hh])
        total = o[:, base : base + 1]
        lse = peak + jnp.log(total)
        lse_all[b] = jnp.where(lane_q == 2 * t + hh, lse, lse_all[b])
        tiles[hh, b] = o / total
        if hh == 1:
            out = oth_ref if b else own_ref
            o = jnp.where(lane_q < 64, tiles[0, b], tiles[1, b])
            o32_ref[b * tok : (b + 1) * tok, cols] = o
            out[:, cols] = o.astype(BF)
    for b in range(2):
        lse_ref[b * tok : (b + 1) * tok, :] = lse_all[b]


def attn_fwd(raw, row, core, parts, units, vec, idc, deps=()):
    tok = parts[0].shape[0]
    width = parts[0].shape[1]
    sds = pltpu.HBM
    shapes = [
        sds((4 * tok, width), BF),
        sds((2 * tok, UNIT), BF),
        sds((4 * tok, UNIT), BF),
        sds((4 * tok, UNIT), BF),
        sds((2 * tok, 128), F32),
        sds((2 * tok, UNIT), F32),
        sds((tok, UNIT), BF),
        sds((tok, UNIT), BF),
    ]
    scratch = [pltpu.VMEM((width, 3 * UNIT), BF), pltpu.SemaphoreType.DMA((3,))]
    return pl.pallas_call(
        functools.partial(attn_fwd_kernel, raw, row, len(deps)),
        out_shape=shapes,
        in_specs=[SMEM] + [VMEM] * 4 + [ANY] + [VMEM] * 2 + [ANY] * len(deps),
        out_specs=[VMEM] * len(shapes),
        scratch_shapes=scratch,
        compiler_params=ROOMY,
        cost_estimate=LIGHT,
    )(core, *pin(parts[0]), *parts[1:], *pin(units, vec), idc, *deps)


def load_mlp(core, parts, pbuf, ibuf, obuf, sem):
    proj, inner, last = [], [], []
    for side in range(2):
        if len(parts) == 2:
            wide, outs, place_at = parts[0].at[side], parts[1].at[side], side
        else:
            wide, outs = parts[2 * side : 2 * side + 2]
            place_at = core[0] if side == 0 else 1 - core[0]

        def cols(at):
            return pl.ds(at if isinstance(at, int) else pl.multiple_of(at, 128), UNIT)

        proj.append(
            pltpu.make_async_copy(wide.at[0], pbuf.at[:, cols(place_at * UNIT)], sem.at[side, 0])
        )
        for j in range(4):
            at = cols((place_at * 4 + j) * UNIT)
            inner.append(
                pltpu.make_async_copy(wide.at[1 + j], ibuf.at[:, at], sem.at[side, 1 + j])
            )
        last.append(pltpu.make_async_copy(outs, obuf.at[:, cols(place_at * UNIT)], sem.at[side, 5]))
    return proj, inner, last


def wait_all(copies):
    for copy in copies:
        copy.wait()


def mlp_fwd_kernel(row, last, n_part, core, x, o_own, o_oth, vec, fin, *rest):
    parts, outs = rest[:n_part], rest[n_part:-5]
    pbuf, ibuf, obuf, full, sem = rest[-5:]
    m_ref, pack, d_ref, y_ref = outs[:4]
    proj, inner, outer = load_mlp(core, parts, pbuf, ibuf, obuf, sem)
    for copy in proj + inner + outer:
        copy.start()
    width = x.shape[1]
    here = pl.multiple_of(core[0] * UNIT, 128)
    there = pl.multiple_of((1 - core[0]) * UNIT, 128)
    full[:, pl.ds(here, UNIT)] = o_own[...]
    full[:, pl.ds(there, UNIT)] = o_oth[...]
    pack[:, 5 * width :] = full[...]
    wait_all(proj)
    m = x[...].astype(F32) + (fdot(full[...], pbuf[...]) + vec[row + 4 : row + 5, :])
    m_ref[...] = m
    c = layer_norm(m, vec[row + 5 : row + 6, :], vec[row + 6 : row + 7, :]).astype(BF)
    pack[:, :width] = c
    wait_all(inner)
    total = None
    for j in range(4):
        cols = slice(j * width, (j + 1) * width)
        u = fdot(c, ibuf[:, cols]) + fin[row // 12 : row // 12 + 1, cols]
        cdf = 0.5 + 0.5 * lax.erf(u * 0.5**0.5)
        z = (u * cdf).astype(BF)
        pack[:, (j + 1) * width : (j + 2) * width] = z
        d_ref[:, cols] = (cdf + u * (jnp.exp(-0.5 * u * u) * (0.5 / jnp.pi) ** 0.5)).astype(d_ref.dtype)
        if j == 0:
            wait_all(outer)
        part = fdot(z, obuf[cols, :])
        total = part if total is None else total + part
    y = m + (total + vec[row + 7 : row + 8, :])
    y_ref[...] = y.astype(y_ref.dtype)
    if not last:
        a = layer_norm(y, vec[row + 12 : row + 13, :], vec[row + 13 : row + 14, :])
        outs[4][...] = a.astype(BF)


def mlp_scratch(width):
    return [
        pltpu.VMEM((width, width), BF),
        pltpu.VMEM((width, 4 * width), BF),
        pltpu.VMEM((4 * width, width), BF),
        pltpu.VMEM((8, 128), F32),
        pltpu.SemaphoreType.DMA((2, 6)),
    ]


def mlp_fwd(row, last, core, x, o_own, o_oth, vec, fin, weights):
    tok, width = x.shape
    sds = pltpu.HBM
    shapes = [
        sds((tok, width), F32),
        sds((tok, 6 * width), BF),
        sds((tok, 4 * width), F32),
        sds((tok, width), BF if last else F32),
    ]
    if not last:
        shapes.append(sds((tok, width), BF))
    scratch = mlp_scratch(width)
    scratch[3] = pltpu.VMEM((tok, width), BF)
    return pl.pallas_call(
        functools.partial(mlp_fwd_kernel, row, last, len(weights)),
        out_shape=shapes,
        in_specs=[SMEM] + [VMEM] * 5 + [ANY] * len(weights),
        out_specs=[VMEM] * len(shapes),
        scratch_shapes=scratch,
        compiler_params=ROOMY,
        cost_estimate=LIGHT,
    )(core, *pin(x, o_own), o_oth, *pin(vec, fin, *weights[:2]), *weights[2:])


def norm_back_kernel(row, vec, x, gmid, da, near, far):
    grad = da[...] + near[: da.shape[0], :].astype(F32) + far[...].astype(F32)
    dx, gain_g, bias_g = norm_back(x[...].astype(F32), vec[row : row + 1, :], grad)
    return gmid[...] + dx, gain_g, bias_g


def mlp_bwd_kernel(row, first, n_part, n_dep, core, vec, m_ref, d_ref, *rest):
    n_in = 1 if first else 5
    ins, parts, rest = rest[:n_in], rest[n_in : n_in + n_part], rest[n_in + n_part + n_dep :]
    pbuf, ibuf, obuf, full, sem = rest[-5:]
    gmid_ref, own, oth, rows_ref, fin_ref = rest[:-5]
    proj, inner, outer = load_mlp(core, parts, pbuf, ibuf, obuf, sem)
    for copy in outer + inner + proj:
        copy.start()
    width = m_ref.shape[1]
    half = width // 2

    def split(value, at):
        full[:, :width] = value
        here = pl.multiple_of(core[0] * half, 128)
        there = pl.multiple_of((1 - core[0]) * half, 128)
        own[:, at : at + half] = full[:, pl.ds(here, half)]
        oth[:, at : at + half] = full[:, pl.ds(there, half)]

    rows_ref[...] = jnp.zeros(rows_ref.shape, F32)
    if first:
        gx = ins[0][...].astype(F32)
    else:
        gx, gain_g, bias_g = norm_back_kernel(row + 12, vec, *ins)
        rows_ref[8:9, :] = gain_g
        rows_ref[9:10, :] = bias_g
    gm = gx.astype(BF)
    rows_ref[7:8, :] = jnp.sum(gm.astype(F32), 0, keepdims=True)
    split(gm, 2 * width)
    wait_all(outer)
    total = None
    for j in range(4):
        cols = slice(j * width, (j + 1) * width)
        dz = fdot(gm, obuf[cols, :], 1, 1)
        gu = (d_ref[:, cols].astype(F32) * dz).astype(BF)
        full[:, cols] = gu
        fin_ref[:, cols] = jnp.sum(gu.astype(F32), 0, keepdims=True)
        if j == 0:
            wait_all(inner)
        part = fdot(gu, ibuf[:, cols], 1, 1)
        total = part if total is None else total + part
    own[:, : 2 * width] = full[:, pl.ds(pl.multiple_of(core[0] * 2 * width, 128), 2 * width)]
    oth[:, : 2 * width] = full[:, pl.ds(pl.multiple_of((1 - core[0]) * 2 * width, 128), 2 * width)]
    dm, gain_g, bias_g = norm_back(m_ref[...], vec[row + 5 : row + 6, :], total)
    rows_ref[5:6, :] = gain_g
    rows_ref[6:7, :] = bias_g
    gmid = gx + dm
    gmid_ref[...] = gmid
    ga = gmid.astype(BF)
    rows_ref[4:5, :] = jnp.sum(ga.astype(F32), 0, keepdims=True)
    split(ga, 2 * width + half)
    wait_all(proj)
    split(fdot(ga, pbuf[...], 1, 1).astype(BF), 3 * width)


def mlp_bwd(row, first, core, vec, m, d, ins, weights, deps):
    tok, width = m.shape
    sds = pltpu.HBM
    shapes = (
        [sds((tok, width), F32)]
        + [sds((tok, 7 * width // 2), BF)] * 2
        + [sds((16, width), F32), sds((1, 4 * width), F32)]
    )
    scratch = mlp_scratch(width)
    scratch[3] = pltpu.VMEM((tok, 4 * width), BF)
    return pl.pallas_call(
        functools.partial(mlp_bwd_kernel, row, first, len(weights), len(deps)),
        out_shape=shapes,
        in_specs=[SMEM] + [VMEM] * (3 + len(ins)) + [ANY] * (len(weights) + len(deps)),
        out_specs=[VMEM] * len(shapes),
        scratch_shapes=scratch,
        compiler_params=ROOMY,
        cost_estimate=LIGHT,
    )(core, *pin(vec, m, d, *ins[:3]), *ins[3:], *pin(*weights[:2]), *weights[2:], *deps)


def last_norm_kernel(row, vec, x, gmid, da, near, far, gx_ref):
    gx_ref[...] = norm_back_kernel(row, vec, x, gmid, da, near, far)[0]


def last_norm(row, vec, ins):
    return pl.pallas_call(
        functools.partial(last_norm_kernel, row),
        out_shape=pltpu.HBM(ins[1].shape, F32),
        in_specs=[VMEM] * 6,
        out_specs=VMEM,
        compiler_params=ROOMY,
        cost_estimate=LIGHT,
    )(*pin(vec, *ins[:3]), *ins[3:])


def attn_bwd_kernel(row, n_raw, n_dep, q_ref, k_ref, v_ref, lse_ref, o32_ref, idc, *rest):
    raw, rest = rest[:n_raw], rest[n_raw:]
    (go_own, go_oth, units), rest = rest[:3], rest[3 + n_dep :]
    (
        gq_ref,
        gk_ref,
        gv_ref,
        da_own,
        da_keep,
        da_send,
        sums,
        rows_ref,
        go_ref,
        wbuf,
        sem,
    ) = rest
    tok = go_own.shape[0]
    width = units.shape[1]
    at = pl.ds(3 * width, UNIT)
    first = [
        pltpu.make_async_copy(go_own.at[:, at], go_ref.at[pl.ds(0, tok)], sem.at[3]),
        pltpu.make_async_copy(go_oth.at[:, at], go_ref.at[pl.ds(tok, tok)], sem.at[4]),
    ]
    copies = load_qkv(units, wbuf, sem)
    for copy in first + copies:
        copy.start()
    wait_all(first)
    ids = idc[...]
    near = 2 * tok
    lane_q = lanes(near)
    masks = [lane_mask(hh) for hh in range(2)]
    feats_q = [place(lane_q, 64 * (1 - hh), [ids[:near, :], 1 - ids[:near, :]]) for hh in range(2)]
    feats_k = [
        [
            place(
                lane_q,
                64 * (1 - hh),
                [
                    -1e30 * (1 - ids[b * near : (b + 1) * near, :]),
                    -1e30 * ids[b * near : (b + 1) * near, :],
                    1.0,
                    1.0,
                    1.0,
                ],
            ).astype(BF)
            for b in range(2)
        ]
        for hh in range(2)
    ]
    feats_v = [place(lane_q[:8], 64 * (1 - hh), [1.0] * 3)[0:1].astype(BF) for hh in range(2)]
    for t in range(3):
        cols = slice(t * 128, (t + 1) * 128)
        k_turned = [
            k_ref[b * near : (b + 1) * near, cols].astype(F32).T.astype(BF) for b in range(2)
        ]
        gq_tile = []
        gk_tile = [[], []]
        gv_tile = [[], []]
        for hh in range(2):
            base = 64 * (1 - hh)
            h = 2 * t + hh
            sel = (lane_q < 64) == (hh == 0)
            go32 = go_ref[:, cols].astype(F32)
            inner = jnp.sum(jnp.where(sel, go32 * o32_ref[:, cols], 0.0), -1, keepdims=True)
            lse = lse_ref[:, h : h + 1]
            scaled = q_ref[:, cols] * (masks[hh] * BF(HD**-0.5))
            lse3 = place(lane_q, base + 2, three(-lse)) + feats_q[hh]
            qq = scaled + lse3.astype(BF)
            gg = go_ref[:, cols] * masks[hh] + place(lane_q, base, three(-inner)).astype(BF)
            gq = None
            for b in range(2):
                rows = slice(b * near, (b + 1) * near)
                kk = k_ref[rows, cols] * masks[hh] + feats_k[hh][b]
                vv = v_ref[rows, cols] * masks[hh] + feats_v[hh]
                prob = jnp.exp(fdot(kk, qq, 1, 1))
                gs = (prob * fdot(vv, gg, 1, 1)).astype(BF)
                gv_tile[b].append(fdot(prob.astype(BF), go_ref[:, cols]))
                gk_tile[b].append(fdot(gs, q_ref[:, cols]))
                part = fdot(k_turned[b], gs)
                gq = part if gq is None else gq + part
            gq_tile.append(gq)
        left = lane_q < 64
        turned = jnp.concatenate([gq_tile[0][:64], gq_tile[1][64:]], 0)
        gq_ref[:, cols] = (turned.T * HD**-0.5).astype(BF)
        for b in range(2):
            rows = slice(b * near, (b + 1) * near)
            gk_ref[rows, cols] = (jnp.where(left, *gk_tile[b]) * HD**-0.5).astype(BF)
            gv_ref[rows, cols] = jnp.where(left, *gv_tile[b]).astype(BF)
    for copy in copies:
        copy.wait()
    far = fdot(gk_ref[near:, :], wbuf[:, UNIT : 2 * UNIT], 1, 1) + fdot(
        gv_ref[near:, :], wbuf[:, 2 * UNIT :], 1, 1
    )
    da_keep[...] = far[:tok]
    da_send[tok:, :] = far[tok:].astype(BF)
    own = (
        fdot(gk_ref[:near, :], wbuf[:, UNIT : 2 * UNIT], 1, 1)
        + fdot(gv_ref[:near, :], wbuf[:, 2 * UNIT :], 1, 1)
        + fdot(gq_ref[...], wbuf[:, :UNIT], 1, 1)
    )
    da_own[...] = own[:tok]
    da_send[:tok, :] = own[tok:].astype(BF)
    rows_ref[...] = jnp.zeros(rows_ref.shape, F32)
    if raw:
        gain_g, bias_g = 0.0, 0.0
        for x, grad in zip(raw, (own[:tok], own[tok:], far[:tok], far[tok:])):
            n = norm_parts(x[...].astype(F32))[0]
            gain_g = gain_g + jnp.sum(grad * n, 0, keepdims=True)
            bias_g = bias_g + jnp.sum(grad, 0, keepdims=True)
        rows_ref[0:1, :] = gain_g
        rows_ref[1:2, :] = bias_g
    sums[...] = jnp.zeros(sums.shape, F32)
    sums[0:1, :] = jnp.sum(gq_ref[...].astype(F32), 0, keepdims=True)
    sums[1:2, :] = jnp.sum(gv_ref[...].astype(F32), 0, keepdims=True)


def attn_bwd(row, saved, raw, go_own, go_oth, idc, units, deps):
    tok = go_own.shape[0]
    width = units.shape[1]
    sds = pltpu.HBM
    shapes = [
        sds((2 * tok, UNIT), BF),
        sds((4 * tok, UNIT), BF),
        sds((4 * tok, UNIT), BF),
        sds((tok, width), F32),
        sds((tok, width), F32),
        sds((2 * tok, width), BF),
        sds((8, UNIT), F32),
        sds((8, width), F32),
    ]
    return pl.pallas_call(
        functools.partial(attn_bwd_kernel, row, len(raw), len(deps)),
        out_shape=shapes,
        in_specs=[VMEM] * (6 + len(raw)) + [ANY] * (3 + len(deps)),
        out_specs=[VMEM] * len(shapes),
        scratch_shapes=[
            pltpu.VMEM((2 * tok, UNIT), BF),
            pltpu.VMEM((width, 3 * UNIT), BF),
            pltpu.SemaphoreType.DMA((5,)),
        ],
        compiler_params=ROOMY,
        cost_estimate=LIGHT,
    )(*pin(*saved, idc, *raw, go_own), go_oth, *pin(units), *deps)


def deal(table, outs, buf, value, j, at):
    buf[at] = value.reshape(32, ROWS, UNIT)
    for dq, out in enumerate(outs):
        for p in range(4):
            for x in range(2):
                out[p, x, j] = buf[at, table[dq * 8 + p * 2 + x]].astype(BF)


def blocks_shape(count):
    return [pltpu.HBM((4, 2, count, ROWS, UNIT), BF)] * 4


def qkv_grad_kernel(with_vec, n_dep, table, core, a_ref, gq, gk, gv, *rest):
    n_vec = 7 if with_vec else 0
    vecs, rest = rest[:n_vec], rest[n_vec + n_dep :]
    outs, buf = rest[:4], rest[4]
    near = gq.shape[0]
    deal(table, outs, buf, fdot(a_ref[:near, :], gq[...], 0, 0), 0, 0)
    deal(table, outs, buf, fdot(a_ref[...], gk[...], 0, 0), 1, 1)
    deal(table, outs, buf, fdot(a_ref[...], gv[...], 0, 0), 2, 0)
    if with_vec:
        vbuf, tbuf, fbuf, wbuf = rest[5:9]
        rows0, rows1, sums0, sums1, fin0, fin1, norm0 = vecs
        vbuf[...] = jnp.zeros(vbuf.shape, F32)
        fbuf[...] = jnp.zeros(fbuf.shape, F32)
        cols = pl.ds(pl.multiple_of(core[0] * UNIT, 128), UNIT)
        vbuf[0:2, :] = norm0[0:2, :]
        vbuf[12:14, :] = rows0[8:10, :]
        for l, (rows, sums, fin) in enumerate(((rows0, sums0, fin0), (rows1, sums1, fin1))):
            vbuf[l * 12 + 2 : l * 12 + 3, cols] = sums[0:1, :]
            vbuf[l * 12 + 3 : l * 12 + 4, cols] = sums[1:2, :]
            vbuf[l * 12 + 4 : l * 12 + 8, :] = rows[4:8, :]
            fbuf[l : l + 1, : fin.shape[1]] = fin[...]
        tbuf[...] = vbuf[...].T.reshape(32, ROWS, 128)
        wbuf[...] = jnp.zeros(wbuf.shape, F32)
        for f in range(32):
            base, off = window(f)
            piece = fbuf[:, base : base + 256]
            if off:
                piece = pltpu.roll(piece, 256 - off, 1)
            wbuf[f, :8, :] = piece[:, :128]
        none = jnp.zeros((ROWS, 128), F32)
        for n, (dq, p, x) in enumerate(SLOTS):
            unit = jnp.concatenate([tbuf[table[n]], wbuf[table[n]], none], 1)
            outs[dq][p, x, 3] = unit.astype(BF)


def qkv_grad(table, core, a_all, gq, gk, gv, vecs, deps):
    count = 4 if vecs else 3
    scratch = [pltpu.VMEM((2, 32, ROWS, UNIT), F32)]
    if vecs:
        scratch += [
            pltpu.VMEM((128, a_all.shape[1]), F32),
            pltpu.VMEM((32, ROWS, 128), F32),
            pltpu.VMEM((8, 4 * a_all.shape[1] + 128), F32),
            pltpu.VMEM((32, ROWS, 128), F32),
        ]
    return pl.pallas_call(
        functools.partial(qkv_grad_kernel, bool(vecs), len(deps)),
        out_shape=blocks_shape(count),
        in_specs=[SMEM] * 2 + [VMEM] * (4 + len(vecs)) + [ANY] * len(deps),
        out_specs=[VMEM] * 4,
        scratch_shapes=scratch,
        compiler_params=ROOMY,
        cost_estimate=LIGHT,
    )(table, core, *pin(a_all, gq, gk, gv, *vecs), *deps)


def mlp_grad_kernel(joint, table, f0, f1, b0, b1, *rest):
    if joint:
        dests, (out, sem, buf, obuf) = rest[4:8], rest[8:]
    else:
        out, buf, obuf = rest
    outs = [out.at[q] for q in range(4)]
    width = f0.shape[1] // 6

    def both(lc, rc):
        return fdot(f0[:, lc], b0[:, rc], 0, 0) + fdot(f1[:, lc], b1[:, rc], 0, 0)

    def cols(begin, size):
        return slice(begin, begin + size)

    for j in range(4):
        deal(table, outs, buf, both(cols(0, width), cols(j * UNIT, UNIT)), j, j % 2)
    ga = cols(2 * width + UNIT, UNIT)
    deal(table, outs, buf, both(cols(5 * width, width), ga), 4, 0)
    for j in range(4):
        part = both(cols((j + 1) * width, width), cols(2 * width, UNIT))
        obuf[j * 8 : (j + 1) * 8] = part.reshape(8, 4, ROWS, UNIT)
    for n, (dq, p, x) in enumerate(SLOTS):
        outs[dq][p, x, pl.ds(5, 4)] = obuf[table[n]].astype(BF)
    if joint:
        spread_units(out, dests, sem, 0)


def mlp_grad(table, packs, joint=()):
    more = len(joint)
    blocks = (4, 4, 2, 9, ROWS, UNIT)
    scratch = [
        pltpu.VMEM((2, 32, ROWS, UNIT), F32),
        pltpu.VMEM((32, 4, ROWS, UNIT), F32),
    ]
    if more:
        scratch = [pltpu.VMEM(blocks, BF), pltpu.SemaphoreType.DMA((4,))] + scratch
    return pl.pallas_call(
        functools.partial(mlp_grad_kernel, more),
        out_shape=blocks_shape(12) if more else pltpu.HBM(blocks, BF),
        in_specs=[SMEM] + [VMEM] * 4 + [ANY] * more,
        out_specs=[ANY] * 4 if more else VMEM,
        input_output_aliases={5 + i: i for i in range(more)},
        scratch_shapes=scratch,
        compiler_params=ROOMY,
        cost_estimate=LIGHT,
    )(table, *pin(packs[0]), packs[1], *pin(packs[2]), packs[3], *pin(*joint))


def spread_units(out, dests, sem, begin):
    count = out.shape[3]
    run_all(
        [
            pltpu.make_async_copy(out.at[q], dest.at[:, :, pl.ds(begin, count)], sem.at[q])
            for q, dest in enumerate(dests)
        ]
    )


def qkv_grad_rest_kernel(n_dep, table, a_ref, gq, gk, gv, *rest):
    rest = rest[n_dep:]
    dests, (out, buf, sem) = rest[:4], rest[4:]
    outs = [out.at[q] for q in range(4)]
    near = gq.shape[0]
    deal(table, outs, buf, fdot(a_ref[:near, :], gq[...], 0, 0), 0, 0)
    deal(table, outs, buf, fdot(a_ref[...], gk[...], 0, 0), 1, 1)
    deal(table, outs, buf, fdot(a_ref[...], gv[...], 0, 0), 2, 0)
    spread_units(out, dests, sem, 9)


def qkv_grad_rest(table, a_all, gq, gk, gv, deps):
    return pl.pallas_call(
        functools.partial(qkv_grad_rest_kernel, len(deps)),
        out_shape=blocks_shape(12),
        in_specs=[SMEM] + [VMEM] * 4 + [ANY] * len(deps),
        out_specs=[ANY] * 4,
        scratch_shapes=[
            pltpu.VMEM((4, 4, 2, 3, ROWS, UNIT), BF),
            pltpu.VMEM((2, 32, ROWS, UNIT), F32),
            pltpu.SemaphoreType.DMA((4,)),
        ],
        compiler_params=ROOMY,
        cost_estimate=LIGHT,
    )(table, *pin(a_all, gq, gk, gv), *deps)


def reduce_along(blocks, sets):
    flat = blocks.reshape(-1, ROWS, UNIT)
    got = lax.psum_scatter(flat, AXES, scatter_dimension=0, axis_index_groups=sets, tiled=True)
    return got.reshape(blocks.shape[1:])


def gather_along(block, sets):
    flat = block.reshape(-1, ROWS, UNIT)
    got = lax.all_gather(flat, AXES, axis=0, axis_index_groups=sets, tiled=True)
    return got.reshape(4, *block.shape)


def finish_kernel(core, own0, oth0, own1, oth1, *rest):
    qkv, proj, fc_in, fc_out, fin = rest[:5]
    vecs, vbuf = rest[5:13], rest[13]
    first = core[0] == 0
    for l, (own, oth) in enumerate(((own0, oth0), (own1, oth1))):

        def put(out, rows, at, unit, own=own, oth=oth):
            lo = jnp.where(first, own[unit], oth[unit]).astype(F32)
            hi = jnp.where(first, oth[unit], own[unit]).astype(F32)
            out[l, rows, at[0] : at[0] + UNIT] = lo
            out[l, rows, at[1] : at[1] + UNIT] = hi

        every = slice(0, ROWS)
        for j in range(4):
            put(fc_in, every, (j * UNIT, (j + 4) * UNIT), j)
            put(fc_out, slice(j * ROWS, (j + 1) * ROWS), (0, UNIT), 5 + j)
        put(proj, every, (0, UNIT), 4)
        for j in range(3):
            at = 12 + j if l == 0 else 9 + j
            put(qkv, every, (2 * j * UNIT, (2 * j + 1) * UNIT), at, own0, oth0)
    both = own0[15].astype(F32) + oth0[15].astype(F32)
    fin[...] = both[0:2, 128:224]
    vbuf[...] = jnp.zeros(vbuf.shape, F32)
    vbuf[:ROWS, :] = both[:, :128]
    turned = vbuf[...].T
    for j, vec in enumerate(vecs):
        for l in range(2):
            vec[l : l + 1, :] = turned[l * 12 + j : l * 12 + j + 1, :ROWS]


def finish(core, parts):
    sds = jax.ShapeDtypeStruct
    width = 2 * UNIT
    return pl.pallas_call(
        finish_kernel,
        out_shape=[
            sds((2, ROWS, 3 * width), F32),
            sds((2, ROWS, width), F32),
            sds((2, ROWS, 4 * width), F32),
            sds((2, 4 * ROWS, width), F32),
            sds((2, 4 * ROWS), F32),
        ]
        + [sds((2, ROWS), F32)] * 8,
        in_specs=[SMEM] + [VMEM] * 4,
        out_specs=[VMEM] * 13,
        scratch_shapes=[pltpu.VMEM((128, 128), F32)],
        compiler_params=ROOMY,
        cost_estimate=LIGHT,
    )(core, *parts)


def body(
    tokens,
    image_ids,
    cotangent,
    attn_norm_gain,
    attn_norm_bias,
    qkv_weight,
    query_bias,
    value_bias,
    proj_weight,
    proj_bias,
    mlp_norm_gain,
    mlp_norm_bias,
    fc_in_weight,
    fc_in_bias,
    fc_out_weight,
    fc_out_bias,
):
    core, xh, xl = (lax.axis_index(n) for n in ("core", "xh", "xl"))
    width = tokens.shape[2]
    tok = tokens.shape[1]

    one = core.astype(jnp.int32).reshape(1)
    xl_one = xl.astype(jnp.int32).reshape(1)
    z, y = lax.axis_index("z"), lax.axis_index("y")
    inner_at = jnp.where(core == 0, y, z).astype(jnp.int32).reshape(1)
    table = slot_table(-1, core)
    table_o = slot_table(-1, 1 - core)
    table_out = slot_table(1, core)
    table_abs = slot_table(-1, core, True)
    table_sum = slot_table(1, core, True)

    def segment(dx, dc):
        return lax.dynamic_slice_in_dim(
            image_ids[0], (((xh + dx) % 2) * 2 + (core + dc) % 2) * tok, tok, 0
        )

    ids = jnp.concatenate([segment(0, 0), segment(0, 1), segment(1, 0), segment(1, 1)])
    idc = ids.astype(F32)[:, None]

    u1, u2, u3 = prep(
        one,
        pin(
            attn_norm_gain,
            attn_norm_bias,
            query_bias,
            value_bias,
            proj_bias,
            mlp_norm_gain,
            mlp_norm_bias,
            fc_out_bias,
            fc_in_bias,
            qkv_weight,
            proj_weight,
            fc_in_weight,
            fc_out_weight,
        ),
    )
    tokens_own = tokens[0]
    p1 = jnp.stack([u1, to_xl(u1)])
    p2 = jnp.stack([u2, to_xl(after(u2, p1))])
    tokens_far = to_xh(after(tokens_own, p1))
    share = [tokens_own, to_core(tokens_own), tokens_far, to_core(tokens_far)]
    s1 = three_inner(p1)
    inner1 = after(inner_of(p1, s1), p2, idc, tokens_far)
    pieces1 = [inner1] + three_outer(inner1)
    p2 = after(p2, *pieces1[1:])
    u3 = after(u3, inner1)
    p3 = jnp.stack([u3, to_xl(u3)])
    p3 = after(p3, *pieces1[1:])
    inner3 = gather_along(p3, INNER)
    s2 = three_inner(p2)
    qkv0, vec_rows, fins = assemble_first(table, pieces1, pin(p2, p3))
    qkv0 = qkv0.reshape(3, width, UNIT)
    fwd0 = attn_fwd(True, 0, one, share, qkv0, vec_rows, idc)
    o_own, o_oth = fwd0[6:]
    o_got = to_core(o_oth)
    inner2 = inner_of(p2, [after(part, o_own) for part in s2])
    pieces2 = [inner2] + [after(piece, o_got) for piece in three_outer(inner2)]
    others2 = [to_core(piece) for piece in pieces2]
    inner3 = after(after(inner3, o_own), *pieces2[1:])
    pieces3 = [inner3] + three_outer(inner3)
    full0 = assemble_both(0, one, [table, table_o], pieces2, others2, [o_got] + pin(inner3))
    m0, pack0, d0, x1, a1 = mlp_fwd(0, False, one, tokens_own, o_own, o_got, vec_rows, fins, full0)
    pack0_o = to_core(pack0)
    a1_far = to_xh(a1)
    share1 = [a1, to_core(a1), a1_far, to_core(a1_far)]
    pieces3 = [inner3] + [after(piece, x1) for piece in pieces3[1:]]
    qkv1, wide1, outs1 = assemble(
        [(0, 3, False), (3, 5, False), (8, 4, True)], table_abs, pieces3, share1[1:]
    )
    full1 = [wide1, outs1, to_core(wide1), to_core(outs1)]
    fwd1 = attn_fwd(False, 12, one, share1, qkv1, vec_rows, idc)
    o_own, o_oth = fwd1[6:]
    o_got = to_core(o_oth)
    others3 = [to_core(part) for part in pieces3]
    m1, pack1, d1, block_output = mlp_fwd(12, True, one, x1, o_own, o_got, vec_rows, fins, full1)
    pack1_o = to_core(pack1)

    gmid1, own1, oth1, rows1, fing1 = mlp_bwd(
        12, True, one, vec_rows, m1, d1, [cotangent[0]], full1, pin(block_output)
    )
    got1 = to_core(oth1)
    block_a = mlp_grad(table_sum, [pack1, pack1_o, own1, got1])
    sum_a = reduce_along(block_a, OUTER)
    gq, gk, gv, da, da_keep, da_send, sums1, _ = attn_bwd(
        12, fwd1[1:6], [], own1, got1, idc, qkv1, pin(block_a)
    )
    da_got = to_core(da_send)
    far_in = (da_keep + da_got[tok:].astype(F32)).astype(BF)
    far = to_xh(far_in)
    block_e = qkv_grad_rest(table_out, fwd1[0], gq, gk, gv, [far_in])

    gmid0, own0, oth0, rows0, fing0 = mlp_bwd(
        0, False, one, vec_rows, m0, d0, [x1, gmid1, da, da_got, far], full0, pin(block_e[0])
    )
    got0 = to_core(oth0)
    sum_a = after(sum_a, gmid0)
    mid_a = sum_a
    sum_a = reduce_along(sum_a, INNER)
    block_b = mlp_grad(table_out, [pack0, pack0_o, own0, got0], block_e)
    sent_b = send_outer(block_b)
    gq, gk, gv, da, da_keep, da_send, sums0, norm0 = attn_bwd(
        0, fwd0[1:6], share, own0, got0, idc, qkv0, pin(block_b[0], mid_a)
    )
    da_got = to_core(da_send)
    far = to_xh((da_keep + da_got[tok:].astype(F32)).astype(BF))

    vecs = [rows0, rows1, sums0, sums1, fing0, fing1, norm0]
    block_c = qkv_grad(table_out, one, fwd0[0], gq, gk, gv, vecs, [])
    sent_c = send_outer(block_c)
    gx = last_norm(0, vec_rows, [tokens_own, gmid0, da, da_got, far])
    mine_a, other_a = sum_inner(xl_one, [[sum_a]], pin(block_c[0]))
    part_a = add_all(mine_a, to_xl(other_a))
    part_a = add_all(part_a, to_xh(part_a))
    part_a_o = to_core(part_a)
    sum_bc = sum_outer(inner_at, [sent_b, sent_c], [far] + pin(other_a))
    sent_bc = [sum_bc[0]] + [to_inner(sum_bc[d], d) for d in (1, 2, 3)]
    mine_bc, other_bc = sum_inner(xl_one, [sent_bc], pin(gx))
    part_bc = add_all(mine_bc, to_xl(other_bc))
    part_bc = add_all(part_bc, to_xh(part_bc))
    done = finish(one, [part_bc, to_core(part_bc), part_a, part_a_o])
    qkv_g, proj_g, fc_in_g, fc_out_g, fin_g = done[:5]
    vec_g = done[5:]
    return (
        block_output[None],
        gx[None],
        vec_g[0],
        vec_g[1],
        qkv_g,
        vec_g[2],
        vec_g[3],
        proj_g,
        vec_g[4],
        vec_g[5],
        vec_g[6],
        fc_in_g,
        fin_g,
        fc_out_g,
        vec_g[7],
    )


def solution(mesh):
    fine = Mesh(mesh.devices.reshape(SIZES), AXES)
    row = P(None, FSDP)
    mat = P(None, FSDP, None)
    tok = P(FSDP, SEQ, None)
    return jax.shard_map(
        body,
        mesh=fine,
        in_specs=(
            tok,
            P(FSDP, None),
            tok,
            row,
            row,
            mat,
            row,
            row,
            mat,
            row,
            row,
            row,
            mat,
            row,
            mat,
            row,
        ),
        out_specs=(tok, tok, row, row, mat, row, row, mat, row, row, row, mat, row, mat, row),
        check_vma=False,
    )
```

```python
import functools

import jax
import jax.numpy as jnp
from jax import lax
from jax.experimental import pallas as pl
from jax.experimental.pallas import tpu as pltpu
from jax.sharding import Mesh
from jax.sharding import PartitionSpec as P

HD = 64
AXES = ("xh", "core", "z", "xl", "y")
SIZES = (2, 2, 4, 2, 4)
FSDP = ("z", "xl", "y")
SEQ = ("xh", "core")
UNIT = 384
ROWS = 24
BF = jnp.bfloat16
F32 = jnp.float32
ANY = pl.BlockSpec(memory_space=pl.ANY)
SMEM = pl.BlockSpec(memory_space=pltpu.SMEM)
VMEM = pl.BlockSpec(memory_space=pltpu.VMEM)
LIGHT = pl.CostEstimate(flops=10**6, bytes_accessed=10**5, transcendentals=0)
ROOMY = pltpu.CompilerParams(vmem_limit_bytes=48 * 2**20)


def ravel(coords):
    index = 0
    for size, coord in zip(SIZES, coords):
        index = index * size + coord % size
    return index


def all_coords():
    xh_n, core_n, z_n, xl_n, y_n = SIZES
    return [
        (xh, core, z, xl, y)
        for xh in range(xh_n)
        for core in range(core_n)
        for z in range(z_n)
        for xl in range(xl_n)
        for y in range(y_n)
    ]


def shift(array, move):
    pairs = [(ravel(c), ravel(move(*c))) for c in all_coords()]
    return lax.ppermute(array, AXES, pairs)


def to_core(array):
    return shift(array, lambda xh, core, z, xl, y: (xh, core + 1, z, xl, y))


def to_xh(array):
    return shift(array, lambda xh, core, z, xl, y: (xh + 1, core, z, xl, y))


def to_xl(array):
    return shift(array, lambda xh, core, z, xl, y: (xh, core, z, xl + 1, y))


def to_next_x(array, d):
    def move(xh, core, z, xl, y):
        x = (2 * xh + xl + d) % 4
        return (x // 2, core, z, x % 2, y)

    return shift(array, move)


def to_inner(array, d):
    return shift(
        array,
        lambda xh, core, z, xl, y: (xh, core, z, xl, y + d) if core == 0 else (xh, core, z + d, xl, y),
    )


def to_outer(array, d):
    return shift(
        array,
        lambda xh, core, z, xl, y: (xh, core, z + d, xl, y) if core == 0 else (xh, core, z, xl, y + d),
    )


def nothing(*refs):
    del refs


def after(array, *deps):
    return pl.pallas_call(
        nothing,
        out_shape=jax.ShapeDtypeStruct(array.shape, array.dtype),
        in_specs=[ANY] * (1 + len(deps)),
        out_specs=ANY,
        input_output_aliases={0: 0},
    )(array, *deps)


def groups(outer):
    sets = []
    for xh in range(2):
        for core in range(2):
            for xl in range(2):
                for other in range(4):
                    along_z = (core == 0) == outer
                    sets.append(
                        [
                            ravel((xh, core, i, xl, other) if along_z else (xh, core, other, xl, i))
                            for i in range(4)
                        ]
                    )
    return sets


OUTER = groups(True)
INNER = groups(False)
PLANE = [
    [ravel((xh, core, z, xl, y)) for z in range(4) for y in range(4)]
    for xh in range(2)
    for core in range(2)
    for xl in range(2)
]


def pin(*arrays):
    return [pltpu.with_memory_space_constraint(array, pltpu.HBM) for array in arrays]


def slot_table(sign, core, absolute=False):
    z, xl, y = (lax.axis_index(n) for n in ("z", "xl", "y"))
    inner = jnp.where(core == 0, y, z)
    outer = jnp.where(core == 0, z, y)
    dq = jnp.arange(4, dtype=jnp.int32)[:, None, None]
    dp = jnp.arange(4, dtype=jnp.int32)[None, :, None]
    dx = jnp.arange(2, dtype=jnp.int32)[None, None, :]
    q = dq + 0 * outer if absolute and sign > 0 else (outer + sign * dq + 4) % 4
    if sign < 0:
        p = dp + 0 * inner if absolute else (inner - dp + 4) % 4
        x = (xl + dx) % 2
    else:
        p = dp
        x = dx
    owner = jnp.where(core == 0, q * 8 + x * 4 + p, p * 8 + x * 4 + q)
    return owner.astype(jnp.int32).reshape(32)


SLOTS = [(dq, dp, dx) for dq in range(4) for dp in range(4) for dx in range(2)]


def run_all(copies):
    for copy in copies:
        copy.start()
    for copy in copies:
        copy.wait()


def pieces_of(srcs):
    if len(srcs) == 1:
        return [srcs[0].at[dq] for dq in range(4)]
    return srcs


def assemble_kernel(specs, n_dep, table, *refs):
    srcs, outs, sem = refs[:4], refs[4 + n_dep : -1], refs[-1]
    copies = []
    for n, (dq, dp, dx) in enumerate(SLOTS):
        f = table[n]
        for m, (begin, count, rows_first) in enumerate(specs):
            src = srcs[dq].at[dp, dx, pl.ds(begin, count)]
            dst = outs[m].at[f] if rows_first else outs[m].at[:, f]
            copies.append(pltpu.make_async_copy(src, dst, sem.at[n, m]))
    run_all(copies)


def assemble(specs, table, pieces, deps):
    shapes = [
        pltpu.HBM((32, count, ROWS, UNIT) if rows_first else (count, 32, ROWS, UNIT), BF)
        for _, count, rows_first in specs
    ]
    outs = pl.pallas_call(
        functools.partial(assemble_kernel, specs, len(deps)),
        out_shape=shapes,
        in_specs=[SMEM] + [ANY] * (4 + len(deps)),
        out_specs=[VMEM] * len(shapes),
        scratch_shapes=[pltpu.SemaphoreType.DMA((32, len(shapes)))],
        compiler_params=ROOMY,
        cost_estimate=LIGHT,
    )(table, *pieces, *deps)
    return [
        out.reshape(32 * count * ROWS, UNIT) if rows_first else out.reshape(count, 32 * ROWS, UNIT)
        for out, (_, count, rows_first) in zip(outs, specs)
    ]


def window(f):
    return (f * 96 // 128) * 128, f * 96 % 128


def assemble_first_kernel(n_dep, table, *refs):
    srcs, (out, rows_ref, fins_ref, vun, fbuf, sem) = refs[:4], refs[4 + n_dep :]
    copies = []
    for n, (dq, dp, dx) in enumerate(SLOTS):
        src = srcs[dq].at[dp, dx]
        f = table[n]
        copies.append(pltpu.make_async_copy(src.at[3], vun.at[f], sem.at[n, 0]))
        copies.append(pltpu.make_async_copy(src.at[pl.ds(0, 3)], out.at[:, f], sem.at[n, 1]))
    run_all(copies)
    vectors = vun[...].astype(F32)
    rows_ref[...] = vectors[:, :, :128].reshape(32 * ROWS, 128).T[:32]
    fbuf[...] = jnp.zeros(fbuf.shape, F32)
    for f in range(32):
        base, off = window(f)
        piece = jnp.concatenate([vectors[f, :8, 128:256], jnp.zeros((8, 128), F32)], 1)
        if off:
            piece = pltpu.roll(piece, off, 1)
        fbuf[:, base : base + 256] += piece
    fins_ref[...] = fbuf[:, : fins_ref.shape[1]]


def assemble_first(table, pieces, deps):
    return pl.pallas_call(
        functools.partial(assemble_first_kernel, len(deps)),
        out_shape=[
            pltpu.HBM((3, 32, ROWS, UNIT), BF),
            pltpu.HBM((32, 32 * ROWS), F32),
            pltpu.HBM((8, 128 * ROWS), F32),
        ],
        in_specs=[SMEM] + [ANY] * (4 + len(deps)),
        out_specs=[VMEM] * 3,
        scratch_shapes=[
            pltpu.VMEM((32, ROWS, UNIT), BF),
            pltpu.VMEM((8, 128 * ROWS + 128), F32),
            pltpu.SemaphoreType.DMA((32, 2)),
        ],
        compiler_params=ROOMY,
        cost_estimate=LIGHT,
    )(table, *pieces, *deps)


def assemble_both_kernel(begin, core, table, table_o, *refs):
    srcs, (wide, outs, sem) = refs[:8], refs[-3:]
    copies = []
    for side, at, tab in ((0, core[0], table), (1, 1 - core[0], table_o)):
        for n, (dq, dp, dx) in enumerate(SLOTS):
            src = srcs[4 * side + dq].at[dp, dx]
            f = tab[n]
            copies.append(
                pltpu.make_async_copy(src.at[pl.ds(begin, 5)], wide.at[at, :, f], sem.at[n, side, 0])
            )
            copies.append(
                pltpu.make_async_copy(
                    src.at[pl.ds(begin + 5, 4)], outs.at[at, f], sem.at[n, side, 1]
                )
            )
    run_all(copies)


def assemble_both(begin, core, tables, pieces, others, deps):
    wide, outs = pl.pallas_call(
        functools.partial(assemble_both_kernel, begin),
        out_shape=[
            pltpu.HBM((2, 5, 32, ROWS, UNIT), BF),
            pltpu.HBM((2, 32, 4, ROWS, UNIT), BF),
        ],
        in_specs=[SMEM] * (1 + len(tables)) + [ANY] * (2 * len(pieces) + len(deps)),
        out_specs=[VMEM] * 2,
        scratch_shapes=[pltpu.SemaphoreType.DMA((32, 2, 5))],
        compiler_params=ROOMY,
        cost_estimate=LIGHT,
    )(core, *tables, *pieces, *others, *deps)
    return wide.reshape(2, 5, 32 * ROWS, UNIT), outs.reshape(2, 128 * ROWS, UNIT)


def prep_kernel(core, *refs):
    vecs, (fin, qkv, proj, fc_in, fc_out, u1, u2, u3, vbuf, ubuf) = refs[:8], refs[8:]
    at = pl.multiple_of(core[0] * UNIT, 128)
    wide = pl.multiple_of(core[0] * 4 * UNIT, 128)
    for l in range(2):
        units = [qkv[l, :, pl.ds(at + 2 * j * UNIT, UNIT)] for j in range(3)]
        units.append(proj[l, :, pl.ds(at, UNIT)])
        units += [fc_in[l, :, pl.ds(wide + j * UNIT, UNIT)] for j in range(4)]
        rows = fc_out[l, :, pl.ds(at, UNIT)].astype(F32)
        units += [rows[j * ROWS : (j + 1) * ROWS].astype(BF) for j in range(4)]
        for j, unit in enumerate(units):
            if l == 0:
                if j < 3:
                    u1[j] = unit
                else:
                    u2[j - 3] = unit
            else:
                u3[j] = unit
    vbuf[...] = jnp.zeros(vbuf.shape, F32)
    for j, vec in enumerate(vecs):
        value = vec[...].astype(F32)
        for l in range(2):
            vbuf[l * 12 + j : l * 12 + j + 1, :ROWS] = value[l : l + 1]
    ubuf[...] = jnp.zeros(ubuf.shape, F32)
    ubuf[:, :128] = vbuf[...].T[:ROWS]
    ubuf[0:2, 128:224] = fin[...].astype(F32)
    u1[3] = ubuf[...].astype(BF)


def prep(core, arrays):
    return pl.pallas_call(
        prep_kernel,
        out_shape=[pltpu.HBM((count, ROWS, UNIT), BF) for count in (4, 9, 12)],
        in_specs=[SMEM] + [VMEM] * 13,
        out_specs=[VMEM] * 3,
        scratch_shapes=[pltpu.VMEM((128, 128), F32), pltpu.VMEM((ROWS, UNIT), F32)],
        compiler_params=ROOMY,
        cost_estimate=LIGHT,
    )(core, *arrays)


def inner_of(pair, got, units=slice(None)):
    return jnp.stack([part[:, units] for part in [pair] + got])


def three_inner(pair):
    return [to_inner(pair, d) for d in (1, 2, 3)]


def three_outer(block):
    return [to_outer(block, d) for d in (1, 2, 3)]


def send_outer(blocks):
    return [blocks[0]] + [to_outer(blocks[d], d) for d in (1, 2, 3)]


def take_sets(sizes, refs):
    sets = []
    for size in sizes:
        sets.append(refs[:size])
        refs = refs[size:]
    return sets


def sum_outer_kernel(n_set, n_dep, place_at, *refs):
    sets, outs = take_sets(n_set, refs), refs[sum(n_set) + n_dep :]
    for d, out in enumerate(outs):
        at = lax.rem(place_at[0] + d, 4)
        begin = 0
        for parts in sets:
            count = parts[0].shape[2]
            for x in range(2):
                total = parts[0][at, x].astype(F32)
                for part in parts[1:]:
                    total = total + part[at, x].astype(F32)
                out[x, begin : begin + count] = total.astype(BF)
            begin += count


def sum_outer(place_at, sets, deps=()):
    flat = [part for parts in sets for part in pin(parts[0]) + list(parts[1:])]
    count = sum(parts[0].shape[2] for parts in sets)
    return pl.pallas_call(
        functools.partial(sum_outer_kernel, [len(s) for s in sets], len(deps)),
        out_shape=[pltpu.HBM((2, count, ROWS, UNIT), BF)] * 4,
        in_specs=[SMEM] + [VMEM] * len(flat) + [ANY] * len(deps),
        out_specs=[VMEM] * 4,
        compiler_params=ROOMY,
        cost_estimate=LIGHT,
    )(place_at, *flat, *deps)


def sum_inner_kernel(n_set, n_dep, xl, *refs):
    sets, outs = take_sets(n_set, refs), refs[sum(n_set) + n_dep :]
    for j, out in enumerate(outs):
        at = xl[0] if j == 0 else 1 - xl[0]
        begin = 0
        for parts in sets:
            count = parts[0].shape[1]
            total = parts[0][at].astype(F32)
            for part in parts[1:]:
                total = total + part[at].astype(F32)
            out[begin : begin + count] = total.astype(BF)
            begin += count


def sum_inner(xl, sets, deps=()):
    flat = [part for parts in sets for part in pin(parts[0]) + list(parts[1:])]
    count = sum(parts[0].shape[1] for parts in sets)
    return pl.pallas_call(
        functools.partial(sum_inner_kernel, [len(s) for s in sets], len(deps)),
        out_shape=[pltpu.HBM((count, ROWS, UNIT), BF)] * 2,
        in_specs=[SMEM] + [VMEM] * len(flat) + [ANY] * len(deps),
        out_specs=[VMEM] * 2,
        compiler_params=ROOMY,
        cost_estimate=LIGHT,
    )(xl, *flat, *deps)


def add_all(*parts):
    total = parts[0].astype(F32)
    for part in parts[1:]:
        total = total + part.astype(F32)
    return total.astype(BF)


def norm_parts(values):
    centred = values - jnp.mean(values, -1, keepdims=True)
    scale = lax.rsqrt(jnp.mean(centred * centred, -1, keepdims=True) + 1e-06)
    return centred * scale, scale


def layer_norm(values, gain, bias):
    return norm_parts(values)[0] * gain + bias


def norm_back(values, gain, grad):
    n, scale = norm_parts(values)
    dg = grad * gain
    out = scale * (
        dg - jnp.mean(dg, -1, keepdims=True) - n * jnp.mean(dg * n, -1, keepdims=True)
    )
    return out, jnp.sum(grad * n, 0, keepdims=True), jnp.sum(grad, 0, keepdims=True)


def fdot(a, b, ca=1, cb=0):
    return lax.dot_general(a, b, (((ca,), (cb,)), ((), ())), preferred_element_type=F32)


def lanes(rows):
    return lax.broadcasted_iota(jnp.int32, (rows, 128), 1)


def place(lane, base, columns):
    out = jnp.zeros(lane.shape, F32)
    for j, column in enumerate(columns):
        out = jnp.where(lane == base + j, column, out)
    return out


def load_qkv(units, wbuf, sem):
    return [
        pltpu.make_async_copy(units.at[j], wbuf.at[:, pl.ds(j * UNIT, UNIT)], sem.at[j])
        for j in range(3)
    ]


def lane_mask(hh):
    lane = lax.broadcasted_iota(jnp.int32, (1, 128), 1)
    return jnp.where((lane < 64) == (hh == 0), 1.0, 0.0).astype(BF)


def three(column):
    hi = column.astype(BF).astype(F32)
    mid = (column - hi).astype(BF).astype(F32)
    return [hi, mid, column - hi - mid]


def attn_fwd_kernel(raw, row, n_dep, core, x0, x1, x2, x3, units, vec, idc, *rest):
    rest = rest[n_dep:]
    a_ref, q_ref, k_ref, v_ref, lse_ref, o32_ref, own_ref, oth_ref, wbuf, sem = rest
    copies = load_qkv(units, wbuf, sem)
    for copy in copies:
        copy.start()
    tok = x0.shape[0]
    for j, x in enumerate((x0, x1, x2, x3)):
        if raw:
            a = layer_norm(x[...].astype(F32), vec[row : row + 1, :], vec[row + 1 : row + 2, :])
            a_ref[j * tok : (j + 1) * tok, :] = a.astype(BF)
        else:
            a_ref[j * tok : (j + 1) * tok, :] = x[...]
    start = pl.multiple_of(core[0] * UNIT, 128)
    qb = vec[row + 2 : row + 3, pl.ds(start, UNIT)]
    vb = vec[row + 3 : row + 4, pl.ds(start, UNIT)]
    for copy in copies:
        copy.wait()
    k_ref[...] = fdot(a_ref[...], wbuf[:, UNIT : 2 * UNIT]).astype(BF)
    v_ref[...] = (fdot(a_ref[...], wbuf[:, 2 * UNIT :]) + vb).astype(BF)
    q_ref[...] = (fdot(a_ref[: 2 * tok, :], wbuf[:, :UNIT]) + qb).astype(BF)
    ids = idc[...]
    lane_k = lanes(4 * tok)
    lane_q = lanes(tok)
    masks = [lane_mask(hh) for hh in range(2)]
    feats = [
        place(lane_k, 64 * (1 - hh), [-1e30 * (1 - ids), -1e30 * ids]).astype(BF) for hh in range(2)
    ]
    own = ids[: 2 * tok, :]
    lane_2 = lanes(2 * tok)
    feats_q = [place(lane_2, 64 * (1 - hh), [own, 1 - own]).astype(BF) for hh in range(2)]
    lse_all = [jnp.zeros((tok, 128), F32) for _ in range(2)]
    items = [(t, hh, b) for t in range(3) for hh in range(2) for b in range(2)]

    def scores(item):
        t, hh, b = item
        cols = slice(t * 128, (t + 1) * 128)
        rows = slice(b * tok, (b + 1) * tok)
        kk = k_ref[:, cols] * masks[hh] + feats[hh]
        qq = q_ref[rows, cols] * (masks[hh] * BF(HD**-0.5)) + feats_q[hh][rows, :]
        return fdot(qq, kk, 1, 1)

    ahead = scores(items[0])
    tiles = {}
    for n, (t, hh, b) in enumerate(items):
        cols = slice(t * 128, (t + 1) * 128)
        s = ahead
        if n + 1 < len(items):
            ahead = scores(items[n + 1])
        base = 64 * (1 - hh)
        peak = jnp.max(s, -1, keepdims=True)
        e = jnp.exp(s - peak).astype(BF)
        o = fdot(e, v_ref[:, cols] * masks[hh] + masks[1 - hh])
        total = o[:, base : base + 1]
        lse = peak + jnp.log(total)
        lse_all[b] = jnp.where(lane_q == 2 * t + hh, lse, lse_all[b])
        tiles[hh, b] = o / total
        if hh == 1:
            out = oth_ref if b else own_ref
            o = jnp.where(lane_q < 64, tiles[0, b], tiles[1, b])
            o32_ref[b * tok : (b + 1) * tok, cols] = o
            out[:, cols] = o.astype(BF)
    for b in range(2):
        lse_ref[b * tok : (b + 1) * tok, :] = lse_all[b]


def attn_fwd(raw, row, core, parts, units, vec, idc, deps=()):
    tok = parts[0].shape[0]
    width = parts[0].shape[1]
    sds = pltpu.HBM
    shapes = [
        sds((4 * tok, width), BF),
        sds((2 * tok, UNIT), BF),
        sds((4 * tok, UNIT), BF),
        sds((4 * tok, UNIT), BF),
        sds((2 * tok, 128), F32),
        sds((2 * tok, UNIT), F32),
        sds((tok, UNIT), BF),
        sds((tok, UNIT), BF),
    ]
    scratch = [pltpu.VMEM((width, 3 * UNIT), BF), pltpu.SemaphoreType.DMA((3,))]
    return pl.pallas_call(
        functools.partial(attn_fwd_kernel, raw, row, len(deps)),
        out_shape=shapes,
        in_specs=[SMEM] + [VMEM] * 4 + [ANY] + [VMEM] * 2 + [ANY] * len(deps),
        out_specs=[VMEM] * len(shapes),
        scratch_shapes=scratch,
        compiler_params=ROOMY,
        cost_estimate=LIGHT,
    )(core, *pin(parts[0]), *parts[1:], *pin(units, vec), idc, *deps)


def load_mlp(core, parts, pbuf, ibuf, obuf, sem):
    proj, inner, last = [], [], []
    for side in range(2):
        if len(parts) == 2:
            wide, outs, place_at = parts[0].at[side], parts[1].at[side], side
        else:
            wide, outs = parts[2 * side : 2 * side + 2]
            place_at = core[0] if side == 0 else 1 - core[0]

        def cols(at):
            return pl.ds(at if isinstance(at, int) else pl.multiple_of(at, 128), UNIT)

        proj.append(
            pltpu.make_async_copy(wide.at[0], pbuf.at[:, cols(place_at * UNIT)], sem.at[side, 0])
        )
        for j in range(4):
            at = cols((place_at * 4 + j) * UNIT)
            inner.append(
                pltpu.make_async_copy(wide.at[1 + j], ibuf.at[:, at], sem.at[side, 1 + j])
            )
        last.append(pltpu.make_async_copy(outs, obuf.at[:, cols(place_at * UNIT)], sem.at[side, 5]))
    return proj, inner, last


def wait_all(copies):
    for copy in copies:
        copy.wait()


def mlp_fwd_kernel(row, last, n_part, core, x, o_own, o_oth, vec, fin, *rest):
    parts, outs = rest[:n_part], rest[n_part:-5]
    pbuf, ibuf, obuf, full, sem = rest[-5:]
    m_ref, pack, d_ref, y_ref = outs[:4]
    proj, inner, outer = load_mlp(core, parts, pbuf, ibuf, obuf, sem)
    for copy in proj + inner + outer:
        copy.start()
    width = x.shape[1]
    here = pl.multiple_of(core[0] * UNIT, 128)
    there = pl.multiple_of((1 - core[0]) * UNIT, 128)
    full[:, pl.ds(here, UNIT)] = o_own[...]
    full[:, pl.ds(there, UNIT)] = o_oth[...]
    pack[:, 5 * width :] = full[...]
    wait_all(proj)
    m = x[...].astype(F32) + (fdot(full[...], pbuf[...]) + vec[row + 4 : row + 5, :])
    m_ref[...] = m
    c = layer_norm(m, vec[row + 5 : row + 6, :], vec[row + 6 : row + 7, :]).astype(BF)
    pack[:, :width] = c
    wait_all(inner)
    total = None
    for j in range(4):
        cols = slice(j * width, (j + 1) * width)
        u = fdot(c, ibuf[:, cols]) + fin[row // 12 : row // 12 + 1, cols]
        cdf = 0.5 + 0.5 * lax.erf(u * 0.5**0.5)
        z = (u * cdf).astype(BF)
        pack[:, (j + 1) * width : (j + 2) * width] = z
        d_ref[:, cols] = (cdf + u * (jnp.exp(-0.5 * u * u) * (0.5 / jnp.pi) ** 0.5)).astype(d_ref.dtype)
        if j == 0:
            wait_all(outer)
        part = fdot(z, obuf[cols, :])
        total = part if total is None else total + part
    y = m + (total + vec[row + 7 : row + 8, :])
    y_ref[...] = y.astype(y_ref.dtype)
    if not last:
        a = layer_norm(y, vec[row + 12 : row + 13, :], vec[row + 13 : row + 14, :])
        outs[4][...] = a.astype(BF)


def mlp_scratch(width):
    return [
        pltpu.VMEM((width, width), BF),
        pltpu.VMEM((width, 4 * width), BF),
        pltpu.VMEM((4 * width, width), BF),
        pltpu.VMEM((8, 128), F32),
        pltpu.SemaphoreType.DMA((2, 6)),
    ]


def mlp_fwd(row, last, core, x, o_own, o_oth, vec, fin, weights):
    tok, width = x.shape
    sds = pltpu.HBM
    shapes = [
        sds((tok, width), F32),
        sds((tok, 6 * width), BF),
        sds((tok, 4 * width), F32),
        sds((tok, width), BF if last else F32),
    ]
    if not last:
        shapes.append(sds((tok, width), BF))
    scratch = mlp_scratch(width)
    scratch[3] = pltpu.VMEM((tok, width), BF)
    return pl.pallas_call(
        functools.partial(mlp_fwd_kernel, row, last, len(weights)),
        out_shape=shapes,
        in_specs=[SMEM] + [VMEM] * 5 + [ANY] * len(weights),
        out_specs=[VMEM] * len(shapes),
        scratch_shapes=scratch,
        compiler_params=ROOMY,
        cost_estimate=LIGHT,
    )(core, *pin(x, o_own), o_oth, *pin(vec, fin, *weights[:2]), *weights[2:])


def norm_back_kernel(row, vec, x, gmid, da, near, far):
    grad = da[...] + near[: da.shape[0], :].astype(F32) + far[...].astype(F32)
    dx, gain_g, bias_g = norm_back(x[...].astype(F32), vec[row : row + 1, :], grad)
    return gmid[...] + dx, gain_g, bias_g


def mlp_bwd_kernel(row, first, n_part, n_dep, core, vec, m_ref, d_ref, *rest):
    n_in = 1 if first else 5
    ins, parts, rest = rest[:n_in], rest[n_in : n_in + n_part], rest[n_in + n_part + n_dep :]
    pbuf, ibuf, obuf, full, sem = rest[-5:]
    gmid_ref, own, oth, rows_ref, fin_ref = rest[:-5]
    proj, inner, outer = load_mlp(core, parts, pbuf, ibuf, obuf, sem)
    for copy in outer + inner + proj:
        copy.start()
    width = m_ref.shape[1]
    half = width // 2

    def split(value, at):
        full[:, :width] = value
        here = pl.multiple_of(core[0] * half, 128)
        there = pl.multiple_of((1 - core[0]) * half, 128)
        own[:, at : at + half] = full[:, pl.ds(here, half)]
        oth[:, at : at + half] = full[:, pl.ds(there, half)]

    rows_ref[...] = jnp.zeros(rows_ref.shape, F32)
    if first:
        gx = ins[0][...].astype(F32)
    else:
        gx, gain_g, bias_g = norm_back_kernel(row + 12, vec, *ins)
        rows_ref[8:9, :] = gain_g
        rows_ref[9:10, :] = bias_g
    gm = gx.astype(BF)
    rows_ref[7:8, :] = jnp.sum(gm.astype(F32), 0, keepdims=True)
    split(gm, 2 * width)
    wait_all(outer)
    total = None
    for j in range(4):
        cols = slice(j * width, (j + 1) * width)
        dz = fdot(gm, obuf[cols, :], 1, 1)
        gu = (d_ref[:, cols].astype(F32) * dz).astype(BF)
        full[:, cols] = gu
        fin_ref[:, cols] = jnp.sum(gu.astype(F32), 0, keepdims=True)
        if j == 0:
            wait_all(inner)
        part = fdot(gu, ibuf[:, cols], 1, 1)
        total = part if total is None else total + part
    own[:, : 2 * width] = full[:, pl.ds(pl.multiple_of(core[0] * 2 * width, 128), 2 * width)]
    oth[:, : 2 * width] = full[:, pl.ds(pl.multiple_of((1 - core[0]) * 2 * width, 128), 2 * width)]
    dm, gain_g, bias_g = norm_back(m_ref[...], vec[row + 5 : row + 6, :], total)
    rows_ref[5:6, :] = gain_g
    rows_ref[6:7, :] = bias_g
    gmid = gx + dm
    gmid_ref[...] = gmid
    ga = gmid.astype(BF)
    rows_ref[4:5, :] = jnp.sum(ga.astype(F32), 0, keepdims=True)
    split(ga, 2 * width + half)
    wait_all(proj)
    split(fdot(ga, pbuf[...], 1, 1).astype(BF), 3 * width)


def mlp_bwd(row, first, core, vec, m, d, ins, weights, deps):
    tok, width = m.shape
    sds = pltpu.HBM
    shapes = (
        [sds((tok, width), F32)]
        + [sds((tok, 7 * width // 2), BF)] * 2
        + [sds((16, width), F32), sds((1, 4 * width), F32)]
    )
    scratch = mlp_scratch(width)
    scratch[3] = pltpu.VMEM((tok, 4 * width), BF)
    return pl.pallas_call(
        functools.partial(mlp_bwd_kernel, row, first, len(weights), len(deps)),
        out_shape=shapes,
        in_specs=[SMEM] + [VMEM] * (3 + len(ins)) + [ANY] * (len(weights) + len(deps)),
        out_specs=[VMEM] * len(shapes),
        scratch_shapes=scratch,
        compiler_params=ROOMY,
        cost_estimate=LIGHT,
    )(core, *pin(vec, m, d, *ins[:3]), *ins[3:], *pin(*weights[:2]), *weights[2:], *deps)


def last_norm_kernel(row, vec, x, gmid, da, near, far, gx_ref):
    gx_ref[...] = norm_back_kernel(row, vec, x, gmid, da, near, far)[0]


def last_norm(row, vec, ins):
    return pl.pallas_call(
        functools.partial(last_norm_kernel, row),
        out_shape=pltpu.HBM(ins[1].shape, F32),
        in_specs=[VMEM] * 6,
        out_specs=VMEM,
        compiler_params=ROOMY,
        cost_estimate=LIGHT,
    )(*pin(vec, *ins[:3]), *ins[3:])


def attn_bwd_kernel(row, n_raw, n_dep, q_ref, k_ref, v_ref, lse_ref, o32_ref, idc, *rest):
    raw, rest = rest[:n_raw], rest[n_raw:]
    (go_own, go_oth, units), rest = rest[:3], rest[3 + n_dep :]
    (
        gq_ref,
        gk_ref,
        gv_ref,
        da_own,
        da_keep,
        da_send,
        sums,
        rows_ref,
        go_ref,
        wbuf,
        sem,
    ) = rest
    tok = go_own.shape[0]
    width = units.shape[1]
    at = pl.ds(3 * width, UNIT)
    first = [
        pltpu.make_async_copy(go_own.at[:, at], go_ref.at[pl.ds(0, tok)], sem.at[3]),
        pltpu.make_async_copy(go_oth.at[:, at], go_ref.at[pl.ds(tok, tok)], sem.at[4]),
    ]
    copies = load_qkv(units, wbuf, sem)
    for copy in first + copies:
        copy.start()
    wait_all(first)
    ids = idc[...]
    near = 2 * tok
    lane_q = lanes(near)
    masks = [lane_mask(hh) for hh in range(2)]
    feats_q = [place(lane_q, 64 * (1 - hh), [ids[:near, :], 1 - ids[:near, :]]) for hh in range(2)]
    feats_k = [
        [
            place(
                lane_q,
                64 * (1 - hh),
                [
                    -1e30 * (1 - ids[b * near : (b + 1) * near, :]),
                    -1e30 * ids[b * near : (b + 1) * near, :],
                    1.0,
                    1.0,
                    1.0,
                ],
            ).astype(BF)
            for b in range(2)
        ]
        for hh in range(2)
    ]
    feats_v = [place(lane_q[:8], 64 * (1 - hh), [1.0] * 3)[0:1].astype(BF) for hh in range(2)]
    for t in range(3):
        cols = slice(t * 128, (t + 1) * 128)
        k_turned = [
            k_ref[b * near : (b + 1) * near, cols].astype(F32).T.astype(BF) for b in range(2)
        ]
        gq_tile = []
        gk_tile = [[], []]
        gv_tile = [[], []]
        for hh in range(2):
            base = 64 * (1 - hh)
            h = 2 * t + hh
            sel = (lane_q < 64) == (hh == 0)
            go32 = go_ref[:, cols].astype(F32)
            inner = jnp.sum(jnp.where(sel, go32 * o32_ref[:, cols], 0.0), -1, keepdims=True)
            lse = lse_ref[:, h : h + 1]
            scaled = q_ref[:, cols] * (masks[hh] * BF(HD**-0.5))
            lse3 = place(lane_q, base + 2, three(-lse)) + feats_q[hh]
            qq = scaled + lse3.astype(BF)
            gg = go_ref[:, cols] * masks[hh] + place(lane_q, base, three(-inner)).astype(BF)
            gq = None
            for b in range(2):
                rows = slice(b * near, (b + 1) * near)
                kk = k_ref[rows, cols] * masks[hh] + feats_k[hh][b]
                vv = v_ref[rows, cols] * masks[hh] + feats_v[hh]
                prob = jnp.exp(fdot(kk, qq, 1, 1))
                gs = (prob * fdot(vv, gg, 1, 1)).astype(BF)
                gv_tile[b].append(fdot(prob.astype(BF), go_ref[:, cols]))
                gk_tile[b].append(fdot(gs, q_ref[:, cols]))
                part = fdot(k_turned[b], gs)
                gq = part if gq is None else gq + part
            gq_tile.append(gq)
        left = lane_q < 64
        turned = jnp.concatenate([gq_tile[0][:64], gq_tile[1][64:]], 0)
        gq_ref[:, cols] = (turned.T * HD**-0.5).astype(BF)
        for b in range(2):
            rows = slice(b * near, (b + 1) * near)
            gk_ref[rows, cols] = (jnp.where(left, *gk_tile[b]) * HD**-0.5).astype(BF)
            gv_ref[rows, cols] = jnp.where(left, *gv_tile[b]).astype(BF)
    for copy in copies:
        copy.wait()
    far = fdot(gk_ref[near:, :], wbuf[:, UNIT : 2 * UNIT], 1, 1) + fdot(
        gv_ref[near:, :], wbuf[:, 2 * UNIT :], 1, 1
    )
    da_keep[...] = far[:tok]
    da_send[tok:, :] = far[tok:].astype(BF)
    own = (
        fdot(gk_ref[:near, :], wbuf[:, UNIT : 2 * UNIT], 1, 1)
        + fdot(gv_ref[:near, :], wbuf[:, 2 * UNIT :], 1, 1)
        + fdot(gq_ref[...], wbuf[:, :UNIT], 1, 1)
    )
    da_own[...] = own[:tok]
    da_send[:tok, :] = own[tok:].astype(BF)
    rows_ref[...] = jnp.zeros(rows_ref.shape, F32)
    if raw:
        gain_g, bias_g = 0.0, 0.0
        for x, grad in zip(raw, (own[:tok], own[tok:], far[:tok], far[tok:])):
            n = norm_parts(x[...].astype(F32))[0]
            gain_g = gain_g + jnp.sum(grad * n, 0, keepdims=True)
            bias_g = bias_g + jnp.sum(grad, 0, keepdims=True)
        rows_ref[0:1, :] = gain_g
        rows_ref[1:2, :] = bias_g
    sums[...] = jnp.zeros(sums.shape, F32)
    sums[0:1, :] = jnp.sum(gq_ref[...].astype(F32), 0, keepdims=True)
    sums[1:2, :] = jnp.sum(gv_ref[...].astype(F32), 0, keepdims=True)


def attn_bwd(row, saved, raw, go_own, go_oth, idc, units, deps):
    tok = go_own.shape[0]
    width = units.shape[1]
    sds = pltpu.HBM
    shapes = [
        sds((2 * tok, UNIT), BF),
        sds((4 * tok, UNIT), BF),
        sds((4 * tok, UNIT), BF),
        sds((tok, width), F32),
        sds((tok, width), F32),
        sds((2 * tok, width), BF),
        sds((8, UNIT), F32),
        sds((8, width), F32),
    ]
    return pl.pallas_call(
        functools.partial(attn_bwd_kernel, row, len(raw), len(deps)),
        out_shape=shapes,
        in_specs=[VMEM] * (6 + len(raw)) + [ANY] * (3 + len(deps)),
        out_specs=[VMEM] * len(shapes),
        scratch_shapes=[
            pltpu.VMEM((2 * tok, UNIT), BF),
            pltpu.VMEM((width, 3 * UNIT), BF),
            pltpu.SemaphoreType.DMA((5,)),
        ],
        compiler_params=ROOMY,
        cost_estimate=LIGHT,
    )(*pin(*saved, idc, *raw, go_own), go_oth, *pin(units), *deps)


def deal(table, outs, buf, value, j, at):
    buf[at] = value.reshape(32, ROWS, UNIT)
    for dq, out in enumerate(outs):
        for p in range(4):
            for x in range(2):
                out[p, x, j] = buf[at, table[dq * 8 + p * 2 + x]].astype(BF)


def blocks_shape(count):
    return [pltpu.HBM((4, 2, count, ROWS, UNIT), BF)] * 4


def qkv_grad_kernel(with_vec, n_dep, table, core, a_ref, gq, gk, gv, *rest):
    n_vec = 7 if with_vec else 0
    vecs, rest = rest[:n_vec], rest[n_vec + n_dep :]
    outs, buf = rest[:4], rest[4]
    near = gq.shape[0]
    deal(table, outs, buf, fdot(a_ref[:near, :], gq[...], 0, 0), 0, 0)
    deal(table, outs, buf, fdot(a_ref[...], gk[...], 0, 0), 1, 1)
    deal(table, outs, buf, fdot(a_ref[...], gv[...], 0, 0), 2, 0)
    if with_vec:
        vbuf, tbuf, fbuf, wbuf = rest[5:9]
        rows0, rows1, sums0, sums1, fin0, fin1, norm0 = vecs
        vbuf[...] = jnp.zeros(vbuf.shape, F32)
        fbuf[...] = jnp.zeros(fbuf.shape, F32)
        cols = pl.ds(pl.multiple_of(core[0] * UNIT, 128), UNIT)
        vbuf[0:2, :] = norm0[0:2, :]
        vbuf[12:14, :] = rows0[8:10, :]
        for l, (rows, sums, fin) in enumerate(((rows0, sums0, fin0), (rows1, sums1, fin1))):
            vbuf[l * 12 + 2 : l * 12 + 3, cols] = sums[0:1, :]
            vbuf[l * 12 + 3 : l * 12 + 4, cols] = sums[1:2, :]
            vbuf[l * 12 + 4 : l * 12 + 8, :] = rows[4:8, :]
            fbuf[l : l + 1, : fin.shape[1]] = fin[...]
        tbuf[...] = vbuf[...].T.reshape(32, ROWS, 128)
        wbuf[...] = jnp.zeros(wbuf.shape, F32)
        for f in range(32):
            base, off = window(f)
            piece = fbuf[:, base : base + 256]
            if off:
                piece = pltpu.roll(piece, 256 - off, 1)
            wbuf[f, :8, :] = piece[:, :128]
        none = jnp.zeros((ROWS, 128), F32)
        for n, (dq, p, x) in enumerate(SLOTS):
            unit = jnp.concatenate([tbuf[table[n]], wbuf[table[n]], none], 1)
            outs[dq][p, x, 3] = unit.astype(BF)


def qkv_grad(table, core, a_all, gq, gk, gv, vecs, deps):
    count = 4 if vecs else 3
    scratch = [pltpu.VMEM((2, 32, ROWS, UNIT), F32)]
    if vecs:
        scratch += [
            pltpu.VMEM((128, a_all.shape[1]), F32),
            pltpu.VMEM((32, ROWS, 128), F32),
            pltpu.VMEM((8, 4 * a_all.shape[1] + 128), F32),
            pltpu.VMEM((32, ROWS, 128), F32),
        ]
    return pl.pallas_call(
        functools.partial(qkv_grad_kernel, bool(vecs), len(deps)),
        out_shape=blocks_shape(count),
        in_specs=[SMEM] * 2 + [VMEM] * (4 + len(vecs)) + [ANY] * len(deps),
        out_specs=[VMEM] * 4,
        scratch_shapes=scratch,
        compiler_params=ROOMY,
        cost_estimate=LIGHT,
    )(table, core, *pin(a_all, gq, gk, gv, *vecs), *deps)


def mlp_grad_kernel(joint, table, f0, f1, b0, b1, *rest):
    if joint:
        dests, (out, sem, buf, obuf) = rest[4:8], rest[8:]
    else:
        out, buf, obuf = rest
    outs = [out.at[q] for q in range(4)]
    width = f0.shape[1] // 6

    def both(lc, rc):
        return fdot(f0[:, lc], b0[:, rc], 0, 0) + fdot(f1[:, lc], b1[:, rc], 0, 0)

    def cols(begin, size):
        return slice(begin, begin + size)

    for j in range(4):
        deal(table, outs, buf, both(cols(0, width), cols(j * UNIT, UNIT)), j, j % 2)
    ga = cols(2 * width + UNIT, UNIT)
    deal(table, outs, buf, both(cols(5 * width, width), ga), 4, 0)
    for j in range(4):
        part = both(cols((j + 1) * width, width), cols(2 * width, UNIT))
        obuf[j * 8 : (j + 1) * 8] = part.reshape(8, 4, ROWS, UNIT)
    for n, (dq, p, x) in enumerate(SLOTS):
        outs[dq][p, x, pl.ds(5, 4)] = obuf[table[n]].astype(BF)
    if joint:
        spread_units(out, dests, sem, 0)


def mlp_grad(table, packs, joint=()):
    more = len(joint)
    blocks = (4, 4, 2, 9, ROWS, UNIT)
    scratch = [
        pltpu.VMEM((2, 32, ROWS, UNIT), F32),
        pltpu.VMEM((32, 4, ROWS, UNIT), F32),
    ]
    if more:
        scratch = [pltpu.VMEM(blocks, BF), pltpu.SemaphoreType.DMA((4,))] + scratch
    return pl.pallas_call(
        functools.partial(mlp_grad_kernel, more),
        out_shape=blocks_shape(12) if more else pltpu.HBM(blocks, BF),
        in_specs=[SMEM] + [VMEM] * 4 + [ANY] * more,
        out_specs=[ANY] * 4 if more else VMEM,
        input_output_aliases={5 + i: i for i in range(more)},
        scratch_shapes=scratch,
        compiler_params=ROOMY,
        cost_estimate=LIGHT,
    )(table, *pin(packs[0]), packs[1], *pin(packs[2]), packs[3], *pin(*joint))


def spread_units(out, dests, sem, begin):
    count = out.shape[3]
    run_all(
        [
            pltpu.make_async_copy(out.at[q], dest.at[:, :, pl.ds(begin, count)], sem.at[q])
            for q, dest in enumerate(dests)
        ]
    )


def qkv_grad_rest_kernel(n_dep, table, a_ref, gq, gk, gv, *rest):
    rest = rest[n_dep:]
    dests, (out, buf, sem) = rest[:4], rest[4:]
    outs = [out.at[q] for q in range(4)]
    near = gq.shape[0]
    deal(table, outs, buf, fdot(a_ref[:near, :], gq[...], 0, 0), 0, 0)
    deal(table, outs, buf, fdot(a_ref[...], gk[...], 0, 0), 1, 1)
    deal(table, outs, buf, fdot(a_ref[...], gv[...], 0, 0), 2, 0)
    spread_units(out, dests, sem, 9)


def qkv_grad_rest(table, a_all, gq, gk, gv, deps):
    return pl.pallas_call(
        functools.partial(qkv_grad_rest_kernel, len(deps)),
        out_shape=blocks_shape(12),
        in_specs=[SMEM] + [VMEM] * 4 + [ANY] * len(deps),
        out_specs=[ANY] * 4,
        scratch_shapes=[
            pltpu.VMEM((4, 4, 2, 3, ROWS, UNIT), BF),
            pltpu.VMEM((2, 32, ROWS, UNIT), F32),
            pltpu.SemaphoreType.DMA((4,)),
        ],
        compiler_params=ROOMY,
        cost_estimate=LIGHT,
    )(table, *pin(a_all, gq, gk, gv), *deps)


def reduce_along(blocks, sets):
    flat = blocks.reshape(-1, ROWS, UNIT)
    got = lax.psum_scatter(flat, AXES, scatter_dimension=0, axis_index_groups=sets, tiled=True)
    return got.reshape(blocks.shape[1:])


def gather_along(block, sets):
    flat = block.reshape(-1, ROWS, UNIT)
    got = lax.all_gather(flat, AXES, axis=0, axis_index_groups=sets, tiled=True)
    return got.reshape(4, *block.shape)


def finish_kernel(core, own0, oth0, own1, oth1, *rest):
    qkv, proj, fc_in, fc_out, fin = rest[:5]
    vecs, vbuf = rest[5:13], rest[13]
    first = core[0] == 0
    for l, (own, oth) in enumerate(((own0, oth0), (own1, oth1))):

        def put(out, rows, at, unit, own=own, oth=oth):
            lo = jnp.where(first, own[unit], oth[unit]).astype(F32)
            hi = jnp.where(first, oth[unit], own[unit]).astype(F32)
            out[l, rows, at[0] : at[0] + UNIT] = lo
            out[l, rows, at[1] : at[1] + UNIT] = hi

        every = slice(0, ROWS)
        for j in range(4):
            put(fc_in, every, (j * UNIT, (j + 4) * UNIT), j)
            put(fc_out, slice(j * ROWS, (j + 1) * ROWS), (0, UNIT), 5 + j)
        put(proj, every, (0, UNIT), 4)
        for j in range(3):
            at = 12 + j if l == 0 else 9 + j
            put(qkv, every, (2 * j * UNIT, (2 * j + 1) * UNIT), at, own0, oth0)
    both = own0[15].astype(F32) + oth0[15].astype(F32)
    fin[...] = both[0:2, 128:224]
    vbuf[...] = jnp.zeros(vbuf.shape, F32)
    vbuf[:ROWS, :] = both[:, :128]
    turned = vbuf[...].T
    for j, vec in enumerate(vecs):
        for l in range(2):
            vec[l : l + 1, :] = turned[l * 12 + j : l * 12 + j + 1, :ROWS]


def finish(core, parts):
    sds = jax.ShapeDtypeStruct
    width = 2 * UNIT
    return pl.pallas_call(
        finish_kernel,
        out_shape=[
            sds((2, ROWS, 3 * width), F32),
            sds((2, ROWS, width), F32),
            sds((2, ROWS, 4 * width), F32),
            sds((2, 4 * ROWS, width), F32),
            sds((2, 4 * ROWS), F32),
        ]
        + [sds((2, ROWS), F32)] * 8,
        in_specs=[SMEM] + [VMEM] * 4,
        out_specs=[VMEM] * 13,
        scratch_shapes=[pltpu.VMEM((128, 128), F32)],
        compiler_params=ROOMY,
        cost_estimate=LIGHT,
    )(core, *parts)


def body(
    tokens,
    image_ids,
    cotangent,
    attn_norm_gain,
    attn_norm_bias,
    qkv_weight,
    query_bias,
    value_bias,
    proj_weight,
    proj_bias,
    mlp_norm_gain,
    mlp_norm_bias,
    fc_in_weight,
    fc_in_bias,
    fc_out_weight,
    fc_out_bias,
):
    core, xh, xl = (lax.axis_index(n) for n in ("core", "xh", "xl"))
    width = tokens.shape[2]
    tok = tokens.shape[1]

    one = core.astype(jnp.int32).reshape(1)
    xl_one = xl.astype(jnp.int32).reshape(1)
    z, y = lax.axis_index("z"), lax.axis_index("y")
    inner_at = jnp.where(core == 0, y, z).astype(jnp.int32).reshape(1)
    table = slot_table(-1, core)
    table_o = slot_table(-1, 1 - core)
    table_out = slot_table(1, core)
    table_abs = slot_table(-1, core, True)
    table_sum = slot_table(1, core, True)

    def segment(dx, dc):
        return lax.dynamic_slice_in_dim(
            image_ids[0], (((xh + dx) % 2) * 2 + (core + dc) % 2) * tok, tok, 0
        )

    ids = jnp.concatenate([segment(0, 0), segment(0, 1), segment(1, 0), segment(1, 1)])
    idc = ids.astype(F32)[:, None]

    u1, u2, u3 = prep(
        one,
        pin(
            attn_norm_gain,
            attn_norm_bias,
            query_bias,
            value_bias,
            proj_bias,
            mlp_norm_gain,
            mlp_norm_bias,
            fc_out_bias,
            fc_in_bias,
            qkv_weight,
            proj_weight,
            fc_in_weight,
            fc_out_weight,
        ),
    )
    tokens_own = tokens[0]
    p1 = jnp.stack([u1, to_xl(u1)])
    p2 = jnp.stack([u2, to_xl(after(u2, p1))])
    tokens_far = to_xh(after(tokens_own, p2))
    share = [tokens_own, to_core(tokens_own), tokens_far, to_core(tokens_far)]
    s1 = three_inner(p1)
    inner1 = after(inner_of(p1, s1), p2, idc)
    pieces1 = [inner1] + three_outer(inner1)
    p2 = after(p2, *pieces1[1:])
    u3 = after(u3, inner1)
    p3 = jnp.stack([u3, to_xl(u3)])
    p3 = after(p3, *pieces1[1:])
    inner3 = gather_along(p3, INNER)
    s2 = three_inner(p2)
    qkv0, vec_rows, fins = assemble_first(table, pieces1, pin(p2, p3) + [tokens_far])
    qkv0 = qkv0.reshape(3, width, UNIT)
    fwd0 = attn_fwd(True, 0, one, share, qkv0, vec_rows, idc)
    o_own, o_oth = fwd0[6:]
    o_got = to_core(o_oth)
    inner2 = inner_of(p2, [after(part, o_own) for part in s2])
    pieces2 = [inner2] + [after(piece, o_got) for piece in three_outer(inner2)]
    others2 = [to_core(piece) for piece in pieces2]
    inner3 = after(after(inner3, o_own), *pieces2[1:])
    pieces3 = [inner3] + three_outer(inner3)
    full0 = assemble_both(0, one, [table, table_o], pieces2, others2, [o_got] + pin(inner3))
    m0, pack0, d0, x1, a1 = mlp_fwd(0, False, one, tokens_own, o_own, o_got, vec_rows, fins, full0)
    pack0_o = to_core(pack0)
    a1_far = to_xh(a1)
    share1 = [a1, to_core(a1), a1_far, to_core(a1_far)]
    pieces3 = [inner3] + [after(piece, x1) for piece in pieces3[1:]]
    qkv1, wide1, outs1 = assemble(
        [(0, 3, False), (3, 5, False), (8, 4, True)], table_abs, pieces3, share1[1:]
    )
    full1 = [wide1, outs1, to_core(wide1), to_core(outs1)]
    fwd1 = attn_fwd(False, 12, one, share1, qkv1, vec_rows, idc)
    o_own, o_oth = fwd1[6:]
    o_got = to_core(o_oth)
    others3 = [to_core(part) for part in pieces3]
    m1, pack1, d1, block_output = mlp_fwd(12, True, one, x1, o_own, o_got, vec_rows, fins, full1)
    pack1_o = to_core(pack1)

    gmid1, own1, oth1, rows1, fing1 = mlp_bwd(
        12, True, one, vec_rows, m1, d1, [cotangent[0]], full1, pin(block_output)
    )
    got1 = to_core(oth1)
    block_a = mlp_grad(table_sum, [pack1, pack1_o, own1, got1])
    sum_a = reduce_along(block_a, OUTER)
    gq, gk, gv, da, da_keep, da_send, sums1, _ = attn_bwd(
        12, fwd1[1:6], [], own1, got1, idc, qkv1, pin(block_a)
    )
    da_got = to_core(da_send)
    far_in = (da_keep + da_got[tok:].astype(F32)).astype(BF)
    far = to_xh(far_in)
    block_e = qkv_grad_rest(table_out, fwd1[0], gq, gk, gv, [far_in])

    gmid0, own0, oth0, rows0, fing0 = mlp_bwd(
        0, False, one, vec_rows, m0, d0, [x1, gmid1, da, da_got, far], full0, pin(block_e[0])
    )
    got0 = to_core(oth0)
    sum_a = after(sum_a, gmid0)
    mid_a = sum_a
    sum_a = reduce_along(sum_a, INNER)
    block_b = mlp_grad(table_out, [pack0, pack0_o, own0, got0], block_e)
    sent_b = send_outer(block_b)
    gq, gk, gv, da, da_keep, da_send, sums0, norm0 = attn_bwd(
        0, fwd0[1:6], share, own0, got0, idc, qkv0, pin(block_b[0], mid_a)
    )
    da_got = to_core(da_send)
    far = to_xh((da_keep + da_got[tok:].astype(F32)).astype(BF))

    vecs = [rows0, rows1, sums0, sums1, fing0, fing1, norm0]
    block_c = qkv_grad(table_out, one, fwd0[0], gq, gk, gv, vecs, [])
    sent_c = send_outer(block_c)
    gx = last_norm(0, vec_rows, [tokens_own, gmid0, da, da_got, far])
    mine_a, other_a = sum_inner(xl_one, [[sum_a]], pin(block_c[0]))
    part_a = add_all(mine_a, to_xl(other_a))
    part_a = add_all(part_a, to_xh(part_a))
    part_a_o = to_core(part_a)
    sum_bc = sum_outer(inner_at, [sent_b, sent_c], [far] + pin(other_a))
    sent_bc = [sum_bc[0]] + [to_inner(sum_bc[d], d) for d in (1, 2, 3)]
    mine_bc, other_bc = sum_inner(xl_one, [sent_bc], pin(gx))
    part_bc = add_all(mine_bc, to_xl(other_bc))
    part_bc = add_all(part_bc, to_xh(part_bc))
    done = finish(one, [part_bc, to_core(part_bc), part_a, part_a_o])
    qkv_g, proj_g, fc_in_g, fc_out_g, fin_g = done[:5]
    vec_g = done[5:]
    return (
        block_output[None],
        gx[None],
        vec_g[0],
        vec_g[1],
        qkv_g,
        vec_g[2],
        vec_g[3],
        proj_g,
        vec_g[4],
        vec_g[5],
        vec_g[6],
        fc_in_g,
        fin_g,
        fc_out_g,
        vec_g[7],
    )


def solution(mesh):
    fine = Mesh(mesh.devices.reshape(SIZES), AXES)
    row = P(None, FSDP)
    mat = P(None, FSDP, None)
    tok = P(FSDP, SEQ, None)
    return jax.shard_map(
        body,
        mesh=fine,
        in_specs=(
            tok,
            P(FSDP, None),
            tok,
            row,
            row,
            mat,
            row,
            row,
            mat,
            row,
            row,
            row,
            mat,
            row,
            mat,
            row,
        ),
        out_specs=(tok, tok, row, row, mat, row, row, mat, row, row, row, mat, row, mat, row),
        check_vma=False,
    )
```
